128 devices in a mesh: dp: 32 (over y, z, core), mp: 4 (over x).
Axes of the slice: x: 4, y: 4, z: 4, core: 2. Of those that a mesh axis runs over, the one named last changes fastest.
Arguments:
- latents: bfloat16 [32768, 1536], P('dp', 'mp'), may hold values from -6 to 6
- targets: bfloat16 [32768, 1536], P('dp', 'mp'), may hold values from -6 to 6
- tok_count: int32 [32], P('dp'), may hold values from 64 to 256, as said below
- caption_states: bfloat16 [32, 128, 4096], P('dp', None, 'mp'), may hold values from -6 to 6
- cap_len: int32 [32], P('dp'), may hold values from 16 to 128, as said below
- owner: int32 [32], replicated, may hold values from 0 to 31, each once
- ctx_w: bfloat16 [4096, 1536], P('mp'), may hold values from -0.09375 to 0.09375
- mod_w: bfloat16 [1536, 3, 1536], P(None, None, 'mp'), may hold values from -0.15625 to 0.15625
- in_w: bfloat16 [1536, 6144], P(None, 'mp'), may hold values from -0.15625 to 0.15625
- out_w: bfloat16 [1536, 6144], P(None, 'mp'), may hold values from -0.078125 to 0.078125
- noise_in: float32 [1536, 6144], P('dp', 'mp'), may hold values from -6 to 6
- noise_out: float32 [1536, 6144], P('dp', 'mp'), may hold values from -6 to 6
Outputs:
- grad_in: float32 [1536, 6144], P('dp', 'mp')
- grad_out: float32 [1536, 6144], P('dp', 'mp')
The draws below stay inside these ranges and needn't reach their ends.
Inputs may be any that keep to these rules, and one draw needn't show every extreme that they name: `tok_count`: one example has all 256 tokens live. `cap_len`: one caption fills all 128 slots. `owner`: every learner slot appears exactly once.
All inputs are finite; a program needn't handle non-finite values.
Results may differ from the reference program's by a relative error of at most 0.0043.
Values may be sent and summed in bfloat16 or wider, within the bound.
No kernel may reach another device: no remote copies, remote signals or barrier semaphores. Data moves between devices by JAX's collectives and lax.ppermute only.
A program may use at most 128 MiB of HBM per device.

```python
import math
import jax
import jax.numpy as jnp
from jax import lax

D = 1536
FF = 6144
DT = 4096
DRAWS = 4
TOK = 256
CAP = 128
EXAMPLES = 32
ROWS = 32768


def draw_tok_count(key, part):
    key = jax.random.fold_in(key, 11)
    values = jax.random.randint(key, (EXAMPLES,), TOK // 4, TOK + 1)
    return values.at[0].set(TOK).astype(jnp.int32)


def draw_cap_len(key, part):
    key = jax.random.fold_in(key, 23)
    values = jax.random.randint(key, (EXAMPLES,), CAP // 8, CAP + 1)
    return values.at[0].set(CAP).astype(jnp.int32)


def levels(key, extent, shards, low, high):
    def one(position, shards_of):
        heights = jax.random.uniform(jax.random.fold_in(jax.random.fold_in(key, 6), position), (shards_of,), jnp.float32, low / len(shards), high / len(shards))
        return jnp.repeat(jnp.exp(heights), extent[position] // shards_of).reshape((-1,) + (1,) * (len(extent) - position - 1))

    level = one(*shards[0])
    for cut in shards[1:]:
        level = level * one(*cut)
    return level


def centred(rng, dims, scale, bound, pieces=(), dtype=jnp.bfloat16):
    values = scale * jax.random.normal(rng, dims, jnp.float32)
    if pieces:
        values = values * levels(rng, dims, pieces, -0.22, 0.18)
    return jnp.clip(values, -bound, bound).astype(dtype)


def setup_inputs(seed: int = 0) -> dict:
    seeds = jax.random.split(jax.random.key(seed), 13)
    return {
        "latents": centred(seeds[0], (ROWS, D), 1.0, 6.0, ((0, 32), (1, 4))),
        "targets": centred(seeds[1], (ROWS, D), 1.0, 6.0, ((0, 32), (1, 4))),
        "tok_count": draw_tok_count(jax.random.fold_in(seeds[12], 71), 0),
        "caption_states": centred(seeds[3], (EXAMPLES, CAP, DT), 1.0, 6.0, ((0, 32), (2, 4))),
        "cap_len": draw_cap_len(jax.random.fold_in(seeds[12], 71), 0),
        "owner": jax.random.permutation(seeds[5], EXAMPLES).astype(jnp.int32),
        "ctx_w": centred(seeds[6], (DT, D), DT ** -0.5, 0.09375, ((0, 4),)),
        "mod_w": centred(seeds[7], (D, 3, D), D ** -0.5, 0.15625, ((2, 4),)),
        "in_w": centred(seeds[8], (D, FF), D ** -0.5, 0.15625, ((1, 4),)),
        "out_w": centred(seeds[9], (D, FF), FF ** -0.5, 0.078125, ((1, 4),)),
        "noise_in": centred(seeds[10], (D, FF), 1.0, 6.0, ((0, 32), (1, 4)), jnp.float32),
        "noise_out": centred(seeds[11], (D, FF), 1.0, 6.0, ((0, 32), (1, 4)), jnp.float32),
    }


def gelu_tanh(values):
    return jax.nn.gelu(values, approximate=True)

def reference(latents, targets, tok_count, caption_states, cap_len, owner, ctx_w, mod_w, in_w, out_w, noise_in, noise_out):
    keep_mask = (jnp.arange(CAP)[None, :] < cap_len[:, None]).astype(jnp.float32)
    summed = jnp.einsum('ec,ecf->ef', keep_mask, caption_states.astype(jnp.float32))
    pooled = (summed / cap_len[:, None].astype(jnp.float32)).astype(jnp.bfloat16)
    context = jnp.dot(pooled, ctx_w, preferred_element_type=jnp.float32)
    conditioning = context * lax.rsqrt(lax.optimization_barrier(jnp.mean(context * context, 1, keepdims=True)) + 1e-06)
    activated = jax.nn.silu(conditioning).astype(jnp.bfloat16)
    picker = (owner[None, :] == jnp.arange(EXAMPLES)[:, None]).astype(jnp.bfloat16)
    chosen = jnp.dot(picker, activated, preferred_element_type=jnp.float32)
    modulation = jnp.einsum('ed,dkf->ekf', chosen, mod_w.astype(jnp.float32))
    example_rows = DRAWS * TOK
    lat_all = latents.reshape(EXAMPLES, example_rows, D)
    tgt_all = targets.reshape(EXAMPLES, example_rows, D)
    root = math.sqrt(2.0 * D * FF)

    def one_example(carry, item):
        lat, tgt, modes, count = item
        values = lat.astype(jnp.float32)
        center = lax.optimization_barrier(jnp.mean(values, 1, keepdims=True))
        spread = lax.optimization_barrier(jnp.mean(values * values, 1, keepdims=True)) - center * center
        normed = (values - center) * lax.rsqrt(spread + 1e-06)
        modded = (normed * (1.0 + modes[1][None, :]) + modes[0][None, :]).astype(jnp.bfloat16)
        pre = jnp.dot(modded, in_w, preferred_element_type=jnp.float32)
        hidden_full, gelu_back = jax.vjp(gelu_tanh, pre)
        hidden = hidden_full.astype(jnp.bfloat16)
        branch = lax.dot_general(hidden, out_w, (((1,), (1,)), ((), ())), preferred_element_type=jnp.float32)
        output = values + modes[2][None, :] * branch
        live = (jnp.arange(example_rows) % TOK < count).astype(jnp.float32)[:, None]
        delta = (output - tgt.astype(jnp.float32)) * live * (2.0 / (D * DRAWS * count.astype(jnp.float32)))
        back = (modes[2][None, :] * delta).astype(jnp.bfloat16)
        hidden_grad = jnp.dot(back, out_w, preferred_element_type=jnp.float32)
        pre_grad = gelu_back(hidden_grad)[0].astype(jnp.bfloat16)
        grad_first = lax.dot_general(modded, pre_grad, (((0,), (0,)), ((), ())), preferred_element_type=jnp.float32)
        grad_second = lax.dot_general(back, hidden, (((0,), (0,)), ((), ())), preferred_element_type=jnp.float32)
        norm_value = jnp.sqrt(jnp.sum(grad_first * grad_first) + jnp.sum(grad_second * grad_second))
        unit = root / (norm_value + 0.01)
        return ((carry[0] + unit * grad_first, carry[1] + unit * grad_second), None)
    start = (jnp.zeros((D, FF), jnp.float32), jnp.zeros((D, FF), jnp.float32))
    totals, _ = lax.scan(one_example, start, (lat_all, tgt_all, modulation, tok_count))
    return ((totals[0] + noise_in) / EXAMPLES, (totals[1] + noise_out) / EXAMPLES)
```

```python
import math

import jax
import jax.numpy as jnp
from jax import lax
from jax.experimental import pallas as pl
from jax.experimental.pallas import tpu as pltpu
from jax.sharding import PartitionSpec as P

D = 1536
FF = 6144
DRAWS = 4
BF = jnp.bfloat16
F32 = jnp.float32
RING = 4
PART = D // RING
WIDE = 512
VMEM_LIMIT = 32 * 1024 * 1024
C1 = math.sqrt(2.0 / math.pi)
C2 = 0.044715


def dot(left, right):
    return jnp.dot(left, right, preferred_element_type=F32)


def sign(core, way):
    return way if core == 0 else -way


def by_x(value, way):
    pairs = []
    for dp in range(32):
        for x in range(RING):
            pairs.append((dp * RING + x, dp * RING + (x + sign(dp % 2, way)) % RING))
    return lax.ppermute(value, ("dp", "mp"), pairs)


def by_dp(value, target):
    pairs = []
    for y in range(RING):
        for z in range(RING):
            for c in range(2):
                ty, tz, tc = target(y, z, c)
                pairs.append(((y * RING + z) * 2 + c, ((ty % RING) * RING + tz % RING) * 2 + tc))
    return lax.ppermute(value, "dp", pairs)


def by_turns(value, way, first):
    return by_dp(
        value,
        lambda y, z, c: (y + way, z, c) if (c == 0) == first else (y, z + way, c),
    )


def by_core(value):
    return by_dp(value, lambda y, z, c: (y, z, 1 - c))


def swap_x(value, kind):
    other = [x ^ 1 for x in range(RING)] if kind == 0 else [3 - x for x in range(RING)]
    return lax.ppermute(value, "mp", list(enumerate(other)))


def params():
    return pltpu.CompilerParams(vmem_limit_bytes=VMEM_LIMIT)


def shaped(shape, dtype=BF):
    return jax.ShapeDtypeStruct(shape, dtype)


def cost(flops, size, special=0):
    return pl.CostEstimate(flops=flops, bytes_accessed=size, transcendentals=special)


def in_hbm(value):
    return pltpu.with_memory_space_constraint(value, pltpu.HBM)


def whole(shape):
    return pl.BlockSpec(shape, lambda s, *_: (0, 0))


def columns(rows, width):
    return pl.BlockSpec((rows, width), lambda s, *_: (0, s))


def call(kernel, grid, in_specs, out_specs, out_shape, scratch, estimate, name, aliases={}):
    return pl.pallas_call(
        kernel,
        grid_spec=pltpu.PrefetchScalarGridSpec(
            num_scalar_prefetch=1,
            grid=(grid,),
            in_specs=in_specs,
            out_specs=out_specs,
            scratch_shapes=scratch,
        ),
        out_shape=out_shape,
        input_output_aliases=aliases,
        compiler_params=params(),
        cost_estimate=estimate,
        name=name,
    )


def forward_kernel(at, x0, x1, x2, x3, m0, m1, m2, in_w, modded_o, hidden, pre, mods, modded):
    step = pl.program_id(0)

    @pl.when(step == 0)
    def _():
        for place, ref, row in ((0, m0, 0), (1, m1, 0), (2, m2, 0), (3, m2, 3)):
            mods[:, pl.ds(pl.multiple_of(at[place], 128), PART)] = ref[row : row + 2]
        total = 0.0
        squares = 0.0
        for ref in (x0, x1, x2, x3):
            value = ref[...].astype(F32)
            total = total + jnp.sum(value, 1, keepdims=True)
            squares = squares + jnp.sum(value * value, 1, keepdims=True)
        center = total / D
        scale = lax.rsqrt(squares / D - center * center + 1e-06)
        for k, ref in enumerate((x0, x1, x2, x3)):
            cols = pl.ds(pl.multiple_of(at[8 + k] * PART, 128), PART)
            normed = (ref[...].astype(F32) - center) * scale
            modded[:, cols] = (normed * (1.0 + mods[1:2, cols]) + mods[0:1, cols]).astype(BF)

    modded_o[...] = modded[:, pl.ds(pl.multiple_of(step * WIDE, 128), WIDE)]
    value = dot(modded[...], in_w[...])
    pre[...] = value
    bent = jnp.tanh(value * (C1 + (C1 * C2) * (value * value)))
    hidden[...] = ((0.5 * value) * (1.0 + bent)).astype(BF)


def forward(chunk, at, blocks, mods, in_w):
    rows, ff = blocks[0].shape[0] // 2, in_w.shape[1]
    piece = pl.BlockSpec((rows, PART), lambda s, *_: (chunk, 0))
    return call(
        forward_kernel,
        ff // WIDE,
        [piece] * 4
        + [whole((3, PART)), whole((3, PART)), whole((6, PART)), columns(D, WIDE)],
        [columns(rows, WIDE)] * 3,
        [shaped((rows, D)), shaped((rows, ff)), shaped((rows, ff), F32)],
        [pltpu.VMEM((2, D), F32), pltpu.VMEM((rows, D), BF)],
        cost(2 * rows * D * ff, 12 * 10**6, rows * ff),
        "forward",
    )(at, *[in_hbm(b) for b in blocks], *mods, in_hbm(in_w))


def split_rows(at, turned, keep, send):
    mine = at[4]
    for z in range(RING):
        keep[z * 48 : (z + 1) * 48] = turned[pl.ds(pl.multiple_of(z * 96 + mine, 16), 48)]
        send[z * 48 : (z + 1) * 48] = turned[pl.ds(pl.multiple_of(z * 96 + 48 - mine, 16), 48)]


def turn_kernel(at, top, low, keep, send, turned):
    turned[:, : top.shape[0]] = top[...].T
    turned[:, top.shape[0] :] = low[...].T
    split_rows(at, turned, keep, send)


def turn(at, top, low):
    rows = top.shape[0]
    out = pl.BlockSpec((PART // 2, 2 * rows), lambda s, *_: (s, 0))
    return call(
        turn_kernel,
        RING,
        [columns(rows, PART)] * 2,
        [out, out],
        [shaped((D // 2, 2 * rows))] * 2,
        [pltpu.VMEM((PART, 2 * rows), BF)],
        cost(2 * rows * D, 8 * rows * D),
        "turn",
    )(at, top, low)


def backward_kernel(at, b0, b1, b2, b3, out_w, slope, grad, back):
    @pl.when(pl.program_id(0) == 0)
    def _():
        for k, ref in enumerate((b0, b1, b2, b3)):
            back[:, pl.ds(pl.multiple_of(at[8 + k] * PART, 128), PART)] = ref[...]

    grad[...] = (dot(back[...], out_w[...]) * slope[...].astype(F32)).astype(BF)


def backward(at, blocks, out_w, slope):
    rows, ff = slope.shape
    return call(
        backward_kernel,
        ff // WIDE,
        [whole((rows, PART))] * 4 + [columns(D, WIDE), columns(rows, WIDE)],
        columns(rows, WIDE),
        shaped((rows, ff)),
        [pltpu.VMEM((rows, D), BF)],
        cost(2 * rows * D * ff, 14 * 10**6),
        "backward",
    )(at, *blocks, out_w, slope)


def rows_kernel(count, at, *refs):
    tops, lows = refs[:count], refs[count : 2 * count]
    right0, right1 = refs[2 * count : 2 * count + 2]
    keep, send, square, turned = refs[-4:]
    rows = right0.shape[0]
    for k in range(count):

        @pl.when(pl.program_id(0) == k)
        def _():
            turned[:, :rows] = tops[k][...].T
            turned[:, rows:] = lows[k][...].T

    mine = at[4]
    for n in range(right0.shape[1] // 512):
        cols = slice(n * 512, (n + 1) * 512)
        value = dot(turned[:, :rows], right0[:, cols]) + dot(turned[:, rows:], right1[:, cols])
        piece = jnp.sum(value * value, 0, keepdims=True)

        @pl.when(pl.program_id(0) == 0)
        def _():
            square[:, cols] = piece

        @pl.when(pl.program_id(0) > 0)
        def _():
            square[:, cols] += piece

        for z in range(RING):
            low = value[z * 96 : z * 96 + 48].astype(BF)
            high = value[z * 96 + 48 : (z + 1) * 96].astype(BF)
            at_rows = slice(z * 48, (z + 1) * 48)
            keep[at_rows, cols] = jnp.where(mine == 0, low, high)
            send[at_rows, cols] = jnp.where(mine == 0, high, low)


def rows_grad(at, places, tops, lows, rights, before):
    rows, ff = rights[0].shape
    count = len(tops)
    first = places[0]
    step = places[1] - first if count > 1 else 0
    out = pl.BlockSpec((PART // 2, ff), lambda s, a: (a[8 + first + s * step], 0))
    return call(
        lambda *refs: rows_kernel(count, *refs),
        count,
        [whole((rows, PART))] * (2 * count)
        + [whole((rows, ff))] * 2
        + [pl.BlockSpec(memory_space=pl.ANY)] * len(before),
        [out, out, whole((1, ff))],
        [shaped((D // 2, ff))] * 2 + [shaped((1, ff), F32)],
        [pltpu.VMEM((PART, 2 * rows), BF)],
        cost(4 * rows * PART * ff * count, 5 * 10**6 * count),
        "rows_grad",
        {2 * count + 3 + n: n for n in range(len(before))},
    )(at, *tops, *lows, *rights, *before)


def weight_kernel(at, keep_l, send_l, right0, right1, q0, q1, q2, keep, send, square, sums):
    rows = right0.shape[0]
    keep_v = dot(keep_l[:, :rows], right0[...]) + dot(keep_l[:, rows:], right1[...])
    send_v = dot(send_l[:, :rows], right0[...]) + dot(send_l[:, rows:], right1[...])
    keep[...] = keep_v.astype(BF)
    send[...] = send_v.astype(BF)
    piece = jnp.sum(keep_v * keep_v, 0, keepdims=True) + jnp.sum(send_v * send_v, 0, keepdims=True)
    step = pl.program_id(0)

    @pl.when(step == 0)
    def _():
        sums[...] = piece

    @pl.when(step > 0)
    def _():
        sums[...] += piece

    @pl.when(step == pl.num_programs(0) - 1)
    def _():
        rest = q0[...] + q1[...] + q2[...]
        total = jnp.sum(sums[...], 1, keepdims=True) + jnp.sum(rest, 1, keepdims=True)
        square[...] = jnp.broadcast_to(total, square.shape)


def weight_grad(at, keep_l, send_l, rights, squares):
    rows, ff = rights[0].shape
    width = 512
    return call(
        weight_kernel,
        ff // width,
        [whole((D // 2, 2 * rows))] * 2 + [columns(rows, width)] * 2 + [whole((1, ff))] * 3,
        [columns(D // 2, width)] * 2 + [whole((1, 128))],
        [shaped((D // 2, ff))] * 2 + [shaped((1, 128), F32)],
        [pltpu.VMEM((1, width), F32)],
        cost(4 * rows * D * ff, 11 * 10**6),
        "weight_grad",
    )(at, keep_l, send_l, *rights, *squares)


def scaled(kept, got, u0, u1):
    return kept[...].astype(F32) * u0[0:1, 0:1] + got[...].astype(F32) * u1[0:1, 0:1]


def far_kernel(at, u0, u1, k1, k2, g1, g2, far1, far2):
    far1[0] = scaled(k1, g1, u0, u1).astype(BF)
    far2[0] = scaled(k2, g2, u0, u1).astype(BF)


def near_kernel(at, u0, u1, k1, k2, k3, k4, g1, g2, g3, g4, own, ahead2, behind1):
    own[0, 0] = scaled(k1, g1, u0, u1)
    own[0, 1] = scaled(k2, g2, u0, u1)
    behind1[0] = scaled(k3, g3, u0, u1).astype(BF)
    ahead2[0] = scaled(k4, g4, u0, u1).astype(BF)


def relay_kernel(at, u0, u1, k1, k2, g1, g2, up, down, ahead1, behind2):
    ahead1[0] = (scaled(k1, g1, u0, u1) + up[0].astype(F32)).astype(BF)
    behind2[0] = (scaled(k2, g2, u0, u1) + down[0].astype(F32)).astype(BF)


def close_kernel(at, own, up1, down1, up2, down2, out):
    out[0, 0] = (own[0, 0] + up1[0].astype(F32) + down1[0].astype(F32)).astype(BF)
    out[0, 1] = (own[0, 1] + up2[0].astype(F32) + down2[0].astype(F32)).astype(BF)


def ring_stage(at, u0, u1, first, second, move):
    ff = first[0].shape[1]
    block = lambda k: pl.BlockSpec((48, ff), lambda s, a: (a[12 + k] + s * a[5], 0))
    one = pl.BlockSpec((1, 48, ff), lambda s, *_: (s, 0, 0))
    both = pl.BlockSpec((1, 2, 48, ff), lambda s, *_: (s, 0, 0, 0))
    single = shaped((RING, 48, ff))
    unit = [whole((1, 128))] * 2
    size = RING * 48 * ff
    far1, far2 = call(
        far_kernel,
        RING,
        unit + [block(2)] * 4,
        [one, one],
        [single] * 2,
        [],
        cost(6 * size, 12 * size),
        "far",
    )(at, u0, u1, first[0], second[0], first[1], second[1])
    far1, far2 = move(far1, 1), move(far2, -1)
    order = [block(0), block(0), block(3), block(1)]
    own, ahead2, behind1 = call(
        near_kernel,
        RING,
        unit + order * 2,
        [both, one, one],
        [shaped((RING, 2, 48, ff), F32), single, single],
        [],
        cost(12 * size, 28 * size),
        "near",
    )(
        at, u0, u1, first[0], second[0], first[0], second[0],
        first[1], second[1], first[1], second[1],
    )
    up2, down1 = move(ahead2, 1), move(behind1, -1)
    ahead1, behind2 = call(
        relay_kernel,
        RING,
        unit + [block(1), block(3)] * 2 + [one, one],
        [one, one],
        [single] * 2,
        [],
        cost(8 * size, 16 * size),
        "relay",
    )(at, u0, u1, first[0], second[0], first[1], second[1], far1, far2)
    up1, down2 = move(ahead1, 1), move(behind2, -1)
    return call(
        close_kernel,
        RING,
        [both] + [one] * 4,
        both,
        shaped((RING, 2, 48, ff)),
        [],
        cost(4 * size, 20 * size),
        "close",
    )(at, own, up1, down1, up2, down2)


def local(
    latents,
    targets,
    tok_count,
    caption_states,
    cap_len,
    owner,
    ctx_w,
    mod_w,
    in_w,
    out_w,
    noise_in,
    noise_out,
):
    rows = latents.shape[0]
    token_span = rows // DRAWS
    me_x = lax.axis_index("mp")
    me_dp = lax.axis_index("dp")
    me_y, me_z, me_c = me_dp // 8, (me_dp // 2) % 4, me_dp % 2
    way = 1 - 2 * me_c

    ahead = [(me_x + k * way) % RING for k in range(RING)]
    swapped = [me_x, me_x ^ 1, 3 - me_x, (3 - me_x) ^ 1]
    me_one = jnp.where(me_c == 0, me_y, me_z)
    stride = jnp.where(me_c == 0, 4, 1)
    at = jnp.stack(
        [b * PART for b in swapped]
        + [me_c * 48, jnp.where(me_c == 0, 1, 4), me_c * 0, me_c * 0]
        + ahead
        + [((me_one + k) % RING) * stride for k in range(RING)]
    ).astype(jnp.int32)
    outs = [lax.dynamic_slice_in_dim(out_w, b * PART, PART, 0) for b in ahead]

    positions = jnp.arange(caption_states.shape[1])
    keep_mask = (positions[None, :] < cap_len[:, None]).astype(BF)
    summed = jnp.einsum("ec,ecf->ef", keep_mask, caption_states, preferred_element_type=F32)
    pooled = (summed / cap_len[:, None].astype(F32)).astype(BF).astype(F32)
    everywhere = jnp.broadcast_to(pooled.reshape(1, 8, -1), (32, 8, pooled.shape[1] // 8))
    received = lax.all_to_all(everywhere, "dp", 0, 0, tiled=True)

    behind, next_ahead = by_x(latents, 1), by_x(latents, -1)
    half = rows // 2
    received, behind, next_ahead, at, outs = lax.optimization_barrier(
        (received, behind, next_ahead, at, outs)
    )
    far = by_x(behind, 1)
    wanted = (owner == me_dp)[:, None, None]
    mine = jnp.sum(jnp.where(wanted, received, 0.0), 0).reshape(1, -1).astype(BF)

    context = dot(mine, ctx_w)
    context = context + swap_x(context, 0)
    swapped_context, far = lax.optimization_barrier((swap_x(context, 1), far))
    context = context + swapped_context
    conditioning = context * lax.rsqrt(jnp.mean(context * context, 1, keepdims=True) + 1e-06)
    chosen = jax.nn.silu(conditioning).astype(BF)
    modulation = jnp.einsum("ed,dkf->ekf", chosen, mod_w, preferred_element_type=F32)[0]
    gate = modulation[2:3]
    own_mods = modulation
    pair_mods = swap_x(own_mods, 0)
    far_mods = swap_x(jnp.concatenate([own_mods, pair_mods], 0), 1)
    mods = (own_mods, pair_mods, far_mods)

    count = tok_count[0]
    factor = 2.0 / (D * DRAWS * count.astype(F32))

    def slope_of(pre):
        square = pre * pre
        bent = jnp.tanh(pre * (C1 + (C1 * C2) * square))
        half = 0.5 * (1.0 + bent)
        return half + (0.5 * pre) * (1.0 - bent * bent) * (C1 + (3.0 * C1 * C2) * square)

    def project(hidden, j):
        return lax.dot_general(
            hidden, outs[j], (((1,), (1,)), ((), ())), preferred_element_type=F32
        )

    def leave(k, own, up, down):
        at_rows = slice(k * half, (k + 1) * half)
        output = latents[at_rows].astype(F32) + gate * (
            own + up.astype(F32) + down.astype(F32)
        )
        live = (jnp.arange(k * half, (k + 1) * half) % token_span < count).astype(F32)[:, None]
        delta = (output - targets[at_rows].astype(F32)) * live * factor
        return (gate * delta).astype(BF)

    latent_blocks = (latents, next_ahead, far, behind)
    modded0, hidden0, pre0 = forward(0, at, latent_blocks, mods, in_w)
    far0, down0 = project(hidden0, 2).astype(BF), project(hidden0, 3).astype(BF)
    far0 = by_x(far0, 1)
    at_next, down0 = lax.optimization_barrier((at, down0))
    down0 = by_x(down0, -1)
    up0, own0 = lax.optimization_barrier((project(hidden0, 1), project(hidden0, 0)))
    modded1, hidden1, pre1 = forward(1, at_next, latent_blocks, mods, in_w)
    hidden1, far0, down0 = lax.optimization_barrier((hidden1, far0, down0))
    up0 = by_x((up0 + far0.astype(F32)).astype(BF), 1)
    far1, up1 = project(hidden1, 2).astype(BF), project(hidden1, 1).astype(BF)
    far1, up1, hidden1, at_late, pre0, pre1 = lax.optimization_barrier(
        (far1, up1, hidden1, at, pre0, pre1)
    )
    far1, up1 = by_x(far1, -1), by_x(up1, 1)
    down1, own1 = lax.optimization_barrier((project(hidden1, 3), project(hidden1, 0)))
    back0 = leave(0, own0, up0, down0)
    behind0, ahead0 = by_x(back0, 1), by_x(back0, -1)
    down1 = by_x((down1 + far1.astype(F32)).astype(BF), -1)
    slope0, slope1 = slope_of(pre0).astype(BF), slope_of(pre1).astype(BF)
    mod_keep, mod_send = turn(at_late, modded0, modded1)
    down1, slope0, slope1, mod_keep, mod_send, behind0, ahead0 = lax.optimization_barrier(
        (down1, slope0, slope1, mod_keep, mod_send, behind0, ahead0)
    )
    back1 = leave(1, own1, up1, down1)
    far0 = by_x(behind0, 1)
    behind1, ahead1 = by_x(back1, 1), by_x(back1, -1)
    far1 = by_x(ahead1, -1)

    rights = (hidden0, hidden1)
    *second, square_a = rows_grad(at, (0,), (back0,), (back1,), rights, ())
    grad0 = backward(at, (back0, ahead0, far0, behind0), out_w, slope0)
    *second, square_b = rows_grad(
        at, (1, 3), (ahead0, behind0), (ahead1, behind1), rights, tuple(second)
    )
    grad1 = backward(at, (back1, ahead1, far1, behind1), out_w, slope1)
    *second, square_c = rows_grad(at, (2,), (far0,), (far1,), rights, tuple(second))
    keep2, send2 = second
    got2 = by_core(send2)
    keep1, send1, square = weight_grad(
        at, mod_keep, mod_send, (grad0, grad1), (square_a, square_b, square_c)
    )
    got1 = by_core(send1)
    square = square + swap_x(square, 0)
    square = square + swap_x(square, 1)
    root = math.sqrt(2.0 * D * FF)
    unit = root / (jnp.sqrt(square) + 0.01)

    value = ring_stage(
        at, unit, by_core(unit), (keep1, got1), (keep2, got2), lambda v, w: by_turns(v, w, True)
    )
    groups = [[(y * RING + z) * 2 for z in range(RING)] for y in range(RING)]
    groups += [[(y * RING + z) * 2 + 1 for y in range(RING)] for z in range(RING)]
    got = lax.all_to_all(value, "dp", 0, 0, axis_index_groups=groups, tiled=True)
    value = jnp.sum(got.astype(F32), 0)
    return (value[0] + noise_in) / 32.0, (value[1] + noise_out) / 32.0


def solution(mesh):
    placed = (
        P("dp", "mp"),
        P("dp", "mp"),
        P("dp"),
        P("dp", None, "mp"),
        P("dp"),
        P(),
        P("mp", None),
        P(None, None, "mp"),
        P(None, "mp"),
        P(None, "mp"),
        P("dp", "mp"),
        P("dp", "mp"),
    )
    return jax.shard_map(
        local, mesh=mesh, in_specs=placed, out_specs=(P("dp", "mp"), P("dp", "mp")), check_vma=False
    )
```

```python
import math

import jax
import jax.numpy as jnp
from jax import lax
from jax.experimental import pallas as pl
from jax.experimental.pallas import tpu as pltpu
from jax.sharding import PartitionSpec as P

D = 1536
FF = 6144
DRAWS = 4
BF = jnp.bfloat16
F32 = jnp.float32
RING = 4
PART = D // RING
WIDE = 512
VMEM_LIMIT = 32 * 1024 * 1024
C1 = math.sqrt(2.0 / math.pi)
C2 = 0.044715


def dot(left, right):
    return jnp.dot(left, right, preferred_element_type=F32)


def sign(core, way):
    return way if core == 0 else -way


def by_x(value, way):
    pairs = []
    for dp in range(32):
        for x in range(RING):
            pairs.append((dp * RING + x, dp * RING + (x + sign(dp % 2, way)) % RING))
    return lax.ppermute(value, ("dp", "mp"), pairs)


def by_dp(value, target):
    pairs = []
    for y in range(RING):
        for z in range(RING):
            for c in range(2):
                ty, tz, tc = target(y, z, c)
                pairs.append(((y * RING + z) * 2 + c, ((ty % RING) * RING + tz % RING) * 2 + tc))
    return lax.ppermute(value, "dp", pairs)


def by_turns(value, way, first):
    return by_dp(
        value,
        lambda y, z, c: (y + way, z, c) if (c == 0) == first else (y, z + way, c),
    )


def by_core(value):
    return by_dp(value, lambda y, z, c: (y, z, 1 - c))


def swap_x(value, kind):
    other = [x ^ 1 for x in range(RING)] if kind == 0 else [3 - x for x in range(RING)]
    return lax.ppermute(value, "mp", list(enumerate(other)))


def params():
    return pltpu.CompilerParams(vmem_limit_bytes=VMEM_LIMIT)


def shaped(shape, dtype=BF):
    return jax.ShapeDtypeStruct(shape, dtype)


def cost(flops, size, special=0):
    return pl.CostEstimate(flops=flops, bytes_accessed=size, transcendentals=special)


def in_hbm(value):
    return pltpu.with_memory_space_constraint(value, pltpu.HBM)


def whole(shape):
    return pl.BlockSpec(shape, lambda s, *_: (0, 0))


def columns(rows, width):
    return pl.BlockSpec((rows, width), lambda s, *_: (0, s))


def call(kernel, grid, in_specs, out_specs, out_shape, scratch, estimate, name, aliases={}):
    return pl.pallas_call(
        kernel,
        grid_spec=pltpu.PrefetchScalarGridSpec(
            num_scalar_prefetch=1,
            grid=(grid,),
            in_specs=in_specs,
            out_specs=out_specs,
            scratch_shapes=scratch,
        ),
        out_shape=out_shape,
        input_output_aliases=aliases,
        compiler_params=params(),
        cost_estimate=estimate,
        name=name,
    )


def forward_kernel(at, x0, x1, x2, x3, m0, m1, m2, in_w, modded_o, hidden, pre, mods, modded):
    step = pl.program_id(0)

    @pl.when(step == 0)
    def _():
        for place, ref, row in ((0, m0, 0), (1, m1, 0), (2, m2, 0), (3, m2, 3)):
            mods[:, pl.ds(pl.multiple_of(at[place], 128), PART)] = ref[row : row + 2]
        total = 0.0
        squares = 0.0
        for ref in (x0, x1, x2, x3):
            value = ref[...].astype(F32)
            total = total + jnp.sum(value, 1, keepdims=True)
            squares = squares + jnp.sum(value * value, 1, keepdims=True)
        center = total / D
        scale = lax.rsqrt(squares / D - center * center + 1e-06)
        for k, ref in enumerate((x0, x1, x2, x3)):
            cols = pl.ds(pl.multiple_of(at[8 + k] * PART, 128), PART)
            normed = (ref[...].astype(F32) - center) * scale
            modded[:, cols] = (normed * (1.0 + mods[1:2, cols]) + mods[0:1, cols]).astype(BF)

    modded_o[...] = modded[:, pl.ds(pl.multiple_of(step * WIDE, 128), WIDE)]
    value = dot(modded[...], in_w[...])
    pre[...] = value
    bent = jnp.tanh(value * (C1 + (C1 * C2) * (value * value)))
    hidden[...] = ((0.5 * value) * (1.0 + bent)).astype(BF)


def forward(chunk, at, blocks, mods, in_w):
    rows, ff = blocks[0].shape[0] // 2, in_w.shape[1]
    piece = pl.BlockSpec((rows, PART), lambda s, *_: (chunk, 0))
    return call(
        forward_kernel,
        ff // WIDE,
        [piece] * 4
        + [whole((3, PART)), whole((3, PART)), whole((6, PART)), columns(D, WIDE)],
        [columns(rows, WIDE)] * 3,
        [shaped((rows, D)), shaped((rows, ff)), shaped((rows, ff), F32)],
        [pltpu.VMEM((2, D), F32), pltpu.VMEM((rows, D), BF)],
        cost(2 * rows * D * ff, 12 * 10**6, rows * ff),
        "forward",
    )(at, *[in_hbm(b) for b in blocks], *mods, in_hbm(in_w))


def split_rows(at, turned, keep, send):
    mine = at[4]
    for z in range(RING):
        keep[z * 48 : (z + 1) * 48] = turned[pl.ds(pl.multiple_of(z * 96 + mine, 16), 48)]
        send[z * 48 : (z + 1) * 48] = turned[pl.ds(pl.multiple_of(z * 96 + 48 - mine, 16), 48)]


def turn_kernel(at, top, low, keep, send, turned):
    turned[:, : top.shape[0]] = top[...].T
    turned[:, top.shape[0] :] = low[...].T
    split_rows(at, turned, keep, send)


def turn(at, top, low):
    rows = top.shape[0]
    out = pl.BlockSpec((PART // 2, 2 * rows), lambda s, *_: (s, 0))
    return call(
        turn_kernel,
        RING,
        [columns(rows, PART)] * 2,
        [out, out],
        [shaped((D // 2, 2 * rows))] * 2,
        [pltpu.VMEM((PART, 2 * rows), BF)],
        cost(2 * rows * D, 8 * rows * D),
        "turn",
    )(at, top, low)


def early_kernel(at, b0, b1, b2, w0, w1, w2, out, back, weights):
    @pl.when(pl.program_id(0) == 0)
    def _():
        for k, ref in enumerate((b0, b1, b2)):
            back[:, k * PART : (k + 1) * PART] = ref[...]

    for k, ref in enumerate((w0, w1, w2)):
        weights[k * PART : (k + 1) * PART] = ref[...]
    out[...] = dot(back[...], weights[...])


def backward_early(at, blocks, weights):
    rows, ff = blocks[0].shape[0], weights[0].shape[1]
    return call(
        early_kernel,
        ff // WIDE,
        [whole((rows, PART))] * 3 + [columns(PART, WIDE)] * 3,
        columns(rows, WIDE),
        shaped((rows, ff), F32),
        [pltpu.VMEM((rows, 3 * PART), BF), pltpu.VMEM((3 * PART, WIDE), BF)],
        cost(6 * rows * PART * ff, 9 * 10**6),
        "backward_early",
    )(at, *blocks, *weights)


def late_kernel(at, block, weights, partial, slope, grad):
    value = partial[...] + dot(block[...], weights[...])
    grad[...] = (value * slope[...].astype(F32)).astype(BF)


def backward_late(at, block, weights, partial, slope):
    rows, ff = slope.shape
    return call(
        late_kernel,
        ff // WIDE,
        [whole((rows, PART)), columns(PART, WIDE), columns(rows, WIDE), columns(rows, WIDE)],
        columns(rows, WIDE),
        shaped((rows, ff)),
        [],
        cost(2 * rows * PART * ff, 8 * 10**6),
        "backward_late",
    )(at, block, weights, partial, slope)


def rows_kernel(count, at, *refs):
    tops, lows = refs[:count], refs[count : 2 * count]
    right0, right1 = refs[2 * count : 2 * count + 2]
    keep, send, square, turned = refs[-4:]
    rows = right0.shape[0]
    for k in range(count):

        @pl.when(pl.program_id(0) == k)
        def _():
            turned[:, :rows] = tops[k][...].T
            turned[:, rows:] = lows[k][...].T

    mine = at[4]
    for n in range(right0.shape[1] // 512):
        cols = slice(n * 512, (n + 1) * 512)
        value = dot(turned[:, :rows], right0[:, cols]) + dot(turned[:, rows:], right1[:, cols])
        piece = jnp.sum(value * value, 0, keepdims=True)

        @pl.when(pl.program_id(0) == 0)
        def _():
            square[:, cols] = piece

        @pl.when(pl.program_id(0) > 0)
        def _():
            square[:, cols] += piece

        for z in range(RING):
            low = value[z * 96 : z * 96 + 48].astype(BF)
            high = value[z * 96 + 48 : (z + 1) * 96].astype(BF)
            at_rows = slice(z * 48, (z + 1) * 48)
            keep[at_rows, cols] = jnp.where(mine == 0, low, high)
            send[at_rows, cols] = jnp.where(mine == 0, high, low)


def rows_grad(at, places, tops, lows, rights, before):
    rows, ff = rights[0].shape
    count = len(tops)
    first = places[0]
    step = places[1] - first if count > 1 else 0
    out = pl.BlockSpec((PART // 2, ff), lambda s, a: (a[8 + first + s * step], 0))
    return call(
        lambda *refs: rows_kernel(count, *refs),
        count,
        [whole((rows, PART))] * (2 * count)
        + [whole((rows, ff))] * 2
        + [pl.BlockSpec(memory_space=pl.ANY)] * len(before),
        [out, out, whole((1, ff))],
        [shaped((D // 2, ff))] * 2 + [shaped((1, ff), F32)],
        [pltpu.VMEM((PART, 2 * rows), BF)],
        cost(4 * rows * PART * ff * count, 5 * 10**6 * count),
        "rows_grad",
        {2 * count + 3 + n: n for n in range(len(before))},
    )(at, *tops, *lows, *rights, *before)


def weight_kernel(at, keep_l, send_l, right0, right1, q0, q1, q2, keep, send, square, sums):
    rows = right0.shape[0]
    keep_v = dot(keep_l[:, :rows], right0[...]) + dot(keep_l[:, rows:], right1[...])
    send_v = dot(send_l[:, :rows], right0[...]) + dot(send_l[:, rows:], right1[...])
    keep[...] = keep_v.astype(BF)
    send[...] = send_v.astype(BF)
    piece = jnp.sum(keep_v * keep_v, 0, keepdims=True) + jnp.sum(send_v * send_v, 0, keepdims=True)
    step = pl.program_id(0)

    @pl.when(step == 0)
    def _():
        sums[...] = piece

    @pl.when(step > 0)
    def _():
        sums[...] += piece

    @pl.when(step == pl.num_programs(0) - 1)
    def _():
        rest = q0[...] + q1[...] + q2[...]
        total = jnp.sum(sums[...], 1, keepdims=True) + jnp.sum(rest, 1, keepdims=True)
        square[...] = jnp.broadcast_to(total, square.shape)


def weight_grad(at, keep_l, send_l, rights, squares):
    rows, ff = rights[0].shape
    width = 512
    return call(
        weight_kernel,
        ff // width,
        [whole((D // 2, 2 * rows))] * 2 + [columns(rows, width)] * 2 + [whole((1, ff))] * 3,
        [columns(D // 2, width)] * 2 + [whole((1, 128))],
        [shaped((D // 2, ff))] * 2 + [shaped((1, 128), F32)],
        [pltpu.VMEM((1, width), F32)],
        cost(4 * rows * D * ff, 11 * 10**6),
        "weight_grad",
    )(at, keep_l, send_l, *rights, *squares)


def scaled(kept, got, u0, u1):
    return kept[...].astype(F32) * u0[0:1, 0:1] + got[...].astype(F32) * u1[0:1, 0:1]


def far_kernel(at, u0, u1, k1, k2, g1, g2, far1, far2):
    far1[0] = scaled(k1, g1, u0, u1).astype(BF)
    far2[0] = scaled(k2, g2, u0, u1).astype(BF)


def near_kernel(at, u0, u1, k1, k2, k3, k4, g1, g2, g3, g4, own, ahead2, behind1):
    own[0, 0] = scaled(k1, g1, u0, u1)
    own[0, 1] = scaled(k2, g2, u0, u1)
    behind1[0] = scaled(k3, g3, u0, u1).astype(BF)
    ahead2[0] = scaled(k4, g4, u0, u1).astype(BF)


def relay_kernel(at, u0, u1, k1, k2, g1, g2, up, down, ahead1, behind2):
    ahead1[0] = (scaled(k1, g1, u0, u1) + up[0].astype(F32)).astype(BF)
    behind2[0] = (scaled(k2, g2, u0, u1) + down[0].astype(F32)).astype(BF)


def close_kernel(at, own, up1, down1, up2, down2, own_o, ahead, far, behind):
    first = own[0, 0] + up1[0].astype(F32) + down1[0].astype(F32)
    second = own[0, 1] + up2[0].astype(F32) + down2[0].astype(F32)
    step = pl.program_id(0)
    for k, out in enumerate((far, ahead, behind, own_o)):

        @pl.when(step == k)
        def _():
            out[0] = first.astype(out.dtype)
            out[1] = second.astype(out.dtype)


def ring_stage(at, u0, u1, first, second, move):
    ff = first[0].shape[1]
    block = lambda k: pl.BlockSpec((48, ff), lambda s, a: (a[12 + k] + s * a[5], 0))
    one = pl.BlockSpec((1, 48, ff), lambda s, *_: (s, 0, 0))
    both = pl.BlockSpec((1, 2, 48, ff), lambda s, *_: (s, 0, 0, 0))
    single = shaped((RING, 48, ff))
    unit = [whole((1, 128))] * 2
    size = RING * 48 * ff
    far1, far2 = call(
        far_kernel,
        RING,
        unit + [block(2)] * 4,
        [one, one],
        [single] * 2,
        [],
        cost(6 * size, 12 * size),
        "far",
    )(at, u0, u1, first[0], second[0], first[1], second[1])
    far1, far2 = move(far1, 1), move(far2, -1)
    order = [block(0), block(0), block(3), block(1)]
    own, ahead2, behind1 = call(
        near_kernel,
        RING,
        unit + order * 2,
        [both, one, one],
        [shaped((RING, 2, 48, ff), F32), single, single],
        [],
        cost(12 * size, 28 * size),
        "near",
    )(
        at, u0, u1, first[0], second[0], first[0], second[0],
        first[1], second[1], first[1], second[1],
    )
    up2, down1 = move(ahead2, 1), move(behind1, -1)
    ahead1, behind2 = call(
        relay_kernel,
        RING,
        unit + [block(1), block(3)] * 2 + [one, one],
        [one, one],
        [single] * 2,
        [],
        cost(8 * size, 16 * size),
        "relay",
    )(at, u0, u1, first[0], second[0], first[1], second[1], far1, far2)
    up1, down2 = move(ahead1, 1), move(behind2, -1)
    place = lambda s, a: a[16 + s]
    return call(
        close_kernel,
        RING,
        [pl.BlockSpec((1, 2, 48, ff), lambda s, a: (place(s, a), 0, 0, 0))]
        + [pl.BlockSpec((1, 48, ff), lambda s, a: (place(s, a), 0, 0))] * 4,
        [pl.BlockSpec((2, 48, ff), lambda s, *_: (0, 0, 0))] * 4,
        [shaped((2, 48, ff), k) for k in (F32, BF, BF, BF)],
        [],
        cost(4 * size, 20 * size),
        "close",
    )(at, own, up1, down1, up2, down2)


def local(
    latents,
    targets,
    tok_count,
    caption_states,
    cap_len,
    owner,
    ctx_w,
    mod_w,
    in_w,
    out_w,
    noise_in,
    noise_out,
):
    rows = latents.shape[0]
    token_span = rows // DRAWS
    me_x = lax.axis_index("mp")
    me_dp = lax.axis_index("dp")
    me_y, me_z, me_c = me_dp // 8, (me_dp // 2) % 4, me_dp % 2
    way = 1 - 2 * me_c

    ahead = [(me_x + k * way) % RING for k in range(RING)]
    swapped = [me_x, me_x ^ 1, 3 - me_x, (3 - me_x) ^ 1]
    me_one = jnp.where(me_c == 0, me_y, me_z)
    me_two = jnp.where(me_c == 0, me_z, me_y)
    stride = jnp.where(me_c == 0, 4, 1)
    at = jnp.stack(
        [b * PART for b in swapped]
        + [me_c * 48, jnp.where(me_c == 0, 1, 4), me_c * 0, me_c * 0]
        + ahead
        + [((me_one + k) % RING) * stride for k in range(RING)]
        + [(me_two + k) % RING for k in (2, 1, 3, 0)]
    ).astype(jnp.int32)
    outs = [lax.dynamic_slice_in_dim(out_w, b * PART, PART, 0) for b in ahead]

    positions = jnp.arange(caption_states.shape[1])
    keep_mask = (positions[None, :] < cap_len[:, None]).astype(BF)
    summed = jnp.einsum("ec,ecf->ef", keep_mask, caption_states, preferred_element_type=F32)
    pooled = (summed / cap_len[:, None].astype(F32)).astype(BF).astype(F32)
    everywhere = jnp.broadcast_to(pooled.reshape(1, 8, -1), (32, 8, pooled.shape[1] // 8))
    received = lax.all_to_all(everywhere, "dp", 0, 0, tiled=True)

    behind, next_ahead = by_x(latents, 1), by_x(latents, -1)
    half = rows // 2
    received, behind, at, outs = lax.optimization_barrier((received, behind, at, outs))
    far = by_x(behind, 1)
    wanted = (owner == me_dp)[:, None, None]
    mine = jnp.sum(jnp.where(wanted, received, 0.0), 0).reshape(1, -1).astype(BF)

    context = dot(mine, ctx_w)
    swapped_context, next_ahead = lax.optimization_barrier((swap_x(context, 0), next_ahead))
    context = context + swapped_context
    swapped_context, far = lax.optimization_barrier((swap_x(context, 1), far))
    context = context + swapped_context
    conditioning = context * lax.rsqrt(jnp.mean(context * context, 1, keepdims=True) + 1e-06)
    chosen = jax.nn.silu(conditioning).astype(BF)
    modulation = jnp.einsum("ed,dkf->ekf", chosen, mod_w, preferred_element_type=F32)[0]
    gate = modulation[2:3]
    own_mods = modulation
    pair_mods = swap_x(own_mods, 0)
    far_mods = swap_x(jnp.concatenate([own_mods, pair_mods], 0), 1)
    mods = (own_mods, pair_mods, far_mods)

    count = tok_count[0]
    factor = 2.0 / (D * DRAWS * count.astype(F32))

    def slope_of(pre):
        square = pre * pre
        bent = jnp.tanh(pre * (C1 + (C1 * C2) * square))
        half = 0.5 * (1.0 + bent)
        return half + (0.5 * pre) * (1.0 - bent * bent) * (C1 + (3.0 * C1 * C2) * square)

    def project(hidden, j):
        return lax.dot_general(
            hidden, outs[j], (((1,), (1,)), ((), ())), preferred_element_type=F32
        )

    def leave(k, own, up, down):
        at_rows = slice(k * half, (k + 1) * half)
        output = latents[at_rows].astype(F32) + gate * (
            own + up.astype(F32) + down.astype(F32)
        )
        live = (jnp.arange(k * half, (k + 1) * half) % token_span < count).astype(F32)[:, None]
        delta = (output - targets[at_rows].astype(F32)) * live * factor
        return (gate * delta).astype(BF)

    latent_blocks = (latents, next_ahead, far, behind)
    modded0, hidden0, pre0 = forward(0, at, latent_blocks, mods, in_w)
    far0, down0 = project(hidden0, 2).astype(BF), project(hidden0, 3).astype(BF)
    far0 = by_x(far0, 1)
    at_next, down0 = lax.optimization_barrier((at, down0))
    down0 = by_x(down0, -1)
    up0 = lax.optimization_barrier(project(hidden0, 1))
    modded1, hidden1, pre1 = forward(1, at_next, latent_blocks, mods, in_w)
    hidden1, far0, down0 = lax.optimization_barrier((hidden1, far0, down0))
    up0 = by_x((up0 + far0.astype(F32)).astype(BF), 1)
    far1, up1 = project(hidden1, 2).astype(BF), project(hidden1, 1).astype(BF)
    far1, up1, hidden1, hidden0, at_late, pre0, pre1 = lax.optimization_barrier(
        (far1, up1, hidden1, hidden0, at, pre0, pre1)
    )
    own0 = lax.optimization_barrier(project(hidden0, 0))
    far1, up1 = by_x(far1, -1), by_x(up1, 1)
    down1, own1 = lax.optimization_barrier((project(hidden1, 3), project(hidden1, 0)))
    back0 = leave(0, own0, up0, down0)
    behind0, ahead0 = by_x(back0, 1), by_x(back0, -1)
    down1 = by_x((down1 + far1.astype(F32)).astype(BF), -1)
    slope0, slope1 = slope_of(pre0).astype(BF), slope_of(pre1).astype(BF)
    mod_keep, mod_send = turn(at_late, modded0, modded1)
    down1, slope0, slope1, mod_keep, mod_send, behind0, ahead0 = lax.optimization_barrier(
        (down1, slope0, slope1, mod_keep, mod_send, behind0, ahead0)
    )
    back1 = leave(1, own1, up1, down1)
    far0 = by_x(behind0, 1)
    behind1, ahead1 = by_x(back1, 1), by_x(back1, -1)
    far1 = by_x(ahead1, -1)

    rights = (hidden0, hidden1)
    *second, square_a = rows_grad(at, (0,), (back0,), (back1,), rights, ())
    early0 = backward_early(at, (back0, ahead0, behind0), (outs[0], outs[1], outs[3]))
    early1 = backward_early(at, (back1, ahead1, behind1), (outs[0], outs[1], outs[3]))
    grad0 = backward_late(at, far0, outs[2], early0, slope0)
    *second, square_b = rows_grad(
        at, (1, 3), (ahead0, behind0), (ahead1, behind1), rights, tuple(second)
    )
    grad1 = backward_late(at, far1, outs[2], early1, slope1)
    *second, square_c = rows_grad(at, (2,), (far0,), (far1,), rights, tuple(second))
    keep2, send2 = second
    got2 = by_core(send2)
    keep1, send1, square = weight_grad(
        at, mod_keep, mod_send, (grad0, grad1), (square_a, square_b, square_c)
    )
    got1 = by_core(send1)
    square = square + swap_x(square, 0)
    square = square + swap_x(square, 1)
    root = math.sqrt(2.0 * D * FF)
    unit = root / (jnp.sqrt(square) + 0.01)

    own, ahead, far, behind = ring_stage(
        at, unit, by_core(unit), (keep1, got1), (keep2, got2), lambda v, w: by_turns(v, w, True)
    )
    value = own + (
        by_turns(far, 2, False).astype(F32)
        + by_turns(ahead, 1, False).astype(F32)
        + by_turns(behind, -1, False).astype(F32)
    )
    return (value[0] + noise_in) / 32.0, (value[1] + noise_out) / 32.0


def solution(mesh):
    placed = (
        P("dp", "mp"),
        P("dp", "mp"),
        P("dp"),
        P("dp", None, "mp"),
        P("dp"),
        P(),
        P("mp", None),
        P(None, None, "mp"),
        P(None, "mp"),
        P(None, "mp"),
        P("dp", "mp"),
        P("dp", "mp"),
    )
    return jax.shard_map(
        local, mesh=mesh, in_specs=placed, out_specs=(P("dp", "mp"), P("dp", "mp")), check_vma=False
    )
```

```python
import math

import jax
import jax.numpy as jnp
from jax import lax
from jax.experimental import pallas as pl
from jax.experimental.pallas import tpu as pltpu
from jax.sharding import PartitionSpec as P

D = 1536
FF = 6144
DRAWS = 4
BF = jnp.bfloat16
F32 = jnp.float32
RING = 4
PART = D // RING
WIDE = 512
VMEM_LIMIT = 32 * 1024 * 1024
C1 = math.sqrt(2.0 / math.pi)
C2 = 0.044715


def dot(left, right):
    return jnp.dot(left, right, preferred_element_type=F32)


def sign(core, way):
    return way if core == 0 else -way


def by_x(value, way):
    pairs = []
    for dp in range(32):
        for x in range(RING):
            pairs.append((dp * RING + x, dp * RING + (x + sign(dp % 2, way)) % RING))
    return lax.ppermute(value, ("dp", "mp"), pairs)


def by_dp(value, target):
    pairs = []
    for y in range(RING):
        for z in range(RING):
            for c in range(2):
                ty, tz, tc = target(y, z, c)
                pairs.append(((y * RING + z) * 2 + c, ((ty % RING) * RING + tz % RING) * 2 + tc))
    return lax.ppermute(value, "dp", pairs)


def by_turns(value, way, first):
    return by_dp(
        value,
        lambda y, z, c: (y + way, z, c) if (c == 0) == first else (y, z + way, c),
    )


def by_core(value):
    return by_dp(value, lambda y, z, c: (y, z, 1 - c))


def swap_x(value, kind):
    other = [x ^ 1 for x in range(RING)] if kind == 0 else [3 - x for x in range(RING)]
    return lax.ppermute(value, "mp", list(enumerate(other)))


def params():
    return pltpu.CompilerParams(vmem_limit_bytes=VMEM_LIMIT)


def shaped(shape, dtype=BF):
    return jax.ShapeDtypeStruct(shape, dtype)


def cost(flops, size, special=0):
    return pl.CostEstimate(flops=flops, bytes_accessed=size, transcendentals=special)


def in_hbm(value):
    return pltpu.with_memory_space_constraint(value, pltpu.HBM)


def whole(shape):
    return pl.BlockSpec(shape, lambda s, *_: (0, 0))


def columns(rows, width):
    return pl.BlockSpec((rows, width), lambda s, *_: (0, s))


def call(kernel, grid, in_specs, out_specs, out_shape, scratch, estimate, name, aliases={}):
    return pl.pallas_call(
        kernel,
        grid_spec=pltpu.PrefetchScalarGridSpec(
            num_scalar_prefetch=1,
            grid=(grid,),
            in_specs=in_specs,
            out_specs=out_specs,
            scratch_shapes=scratch,
        ),
        out_shape=out_shape,
        input_output_aliases=aliases,
        compiler_params=params(),
        cost_estimate=estimate,
        name=name,
    )


def forward_kernel(at, x0, x1, x2, x3, m0, m1, m2, in_w, modded_o, hidden, pre, mods, modded):
    step = pl.program_id(0)

    @pl.when(step == 0)
    def _():
        for place, ref, row in ((0, m0, 0), (1, m1, 0), (2, m2, 0), (3, m2, 3)):
            mods[:, pl.ds(pl.multiple_of(at[place], 128), PART)] = ref[row : row + 2]
        total = 0.0
        squares = 0.0
        for ref in (x0, x1, x2, x3):
            value = ref[...].astype(F32)
            total = total + jnp.sum(value, 1, keepdims=True)
            squares = squares + jnp.sum(value * value, 1, keepdims=True)
        center = total / D
        scale = lax.rsqrt(squares / D - center * center + 1e-06)
        for k, ref in enumerate((x0, x1, x2, x3)):
            cols = pl.ds(pl.multiple_of(at[8 + k] * PART, 128), PART)
            normed = (ref[...].astype(F32) - center) * scale
            modded[:, cols] = (normed * (1.0 + mods[1:2, cols]) + mods[0:1, cols]).astype(BF)

    modded_o[...] = modded[:, pl.ds(pl.multiple_of(step * WIDE, 128), WIDE)]
    value = dot(modded[...], in_w[...])
    pre[...] = value
    bent = jnp.tanh(value * (C1 + (C1 * C2) * (value * value)))
    hidden[...] = ((0.5 * value) * (1.0 + bent)).astype(BF)


def forward(first, rows, at, blocks, mods, in_w):
    ff = in_w.shape[1]
    piece = pl.BlockSpec((rows, PART), lambda s, *_: (first // rows, 0))
    return call(
        forward_kernel,
        ff // WIDE,
        [piece] * 4
        + [whole((3, PART)), whole((3, PART)), whole((6, PART)), columns(D, WIDE)],
        [columns(rows, WIDE)] * 3,
        [shaped((rows, D)), shaped((rows, ff)), shaped((rows, ff), F32)],
        [pltpu.VMEM((2, D), F32), pltpu.VMEM((rows, D), BF)],
        cost(2 * rows * D * ff, 12 * 10**6, rows * ff),
        "forward",
    )(at, *[in_hbm(b) for b in blocks], *mods, in_hbm(in_w))


def split_rows(at, turned, keep, send):
    mine = at[4]
    for z in range(RING):
        keep[z * 48 : (z + 1) * 48] = turned[pl.ds(pl.multiple_of(z * 96 + mine, 16), 48)]
        send[z * 48 : (z + 1) * 48] = turned[pl.ds(pl.multiple_of(z * 96 + 48 - mine, 16), 48)]


def turn_kernel(at, top, low, keep, send, turned):
    turned[:, : top.shape[0]] = top[...].T
    turned[:, top.shape[0] :] = low[...].T
    split_rows(at, turned, keep, send)


def turn(at, top, low):
    rows = top.shape[0] + low.shape[0]
    out = pl.BlockSpec((PART // 2, rows), lambda s, *_: (s, 0))
    return call(
        turn_kernel,
        RING,
        [columns(top.shape[0], PART), columns(low.shape[0], PART)],
        [out, out],
        [shaped((D // 2, rows))] * 2,
        [pltpu.VMEM((PART, rows), BF)],
        cost(rows * D, 4 * rows * D),
        "turn",
    )(at, top, low)


def backward_kernel(at, b0, b1, b2, b3, out_w, slope, grad, back):
    @pl.when(pl.program_id(0) == 0)
    def _():
        for k, ref in enumerate((b0, b1, b2, b3)):
            back[:, pl.ds(pl.multiple_of(at[8 + k] * PART, 128), PART)] = ref[...]

    grad[...] = (dot(back[...], out_w[...]) * slope[...].astype(F32)).astype(BF)


def backward(at, blocks, out_w, slope):
    rows, ff = slope.shape
    return call(
        backward_kernel,
        ff // WIDE,
        [whole((rows, PART))] * 4 + [columns(D, WIDE), columns(rows, WIDE)],
        columns(rows, WIDE),
        shaped((rows, ff)),
        [pltpu.VMEM((rows, D), BF)],
        cost(2 * rows * D * ff, 14 * 10**6),
        "backward",
    )(at, *blocks, out_w, slope)


def rows_kernel(count, at, *refs):
    tops, lows = refs[:count], refs[count : 2 * count]
    right0, right1 = refs[2 * count : 2 * count + 2]
    keep, send, square, turned = refs[-4:]
    rows = right0.shape[0]
    for k in range(count):

        @pl.when(pl.program_id(0) == k)
        def _():
            turned[:, :rows] = tops[k][...].T
            turned[:, rows:] = lows[k][...].T

    mine = at[4]
    for n in range(right0.shape[1] // 512):
        cols = slice(n * 512, (n + 1) * 512)
        value = dot(turned[:, :rows], right0[:, cols]) + dot(turned[:, rows:], right1[:, cols])
        piece = jnp.sum(value * value, 0, keepdims=True)

        @pl.when(pl.program_id(0) == 0)
        def _():
            square[:, cols] = piece

        @pl.when(pl.program_id(0) > 0)
        def _():
            square[:, cols] += piece

        for z in range(RING):
            low = value[z * 96 : z * 96 + 48].astype(BF)
            high = value[z * 96 + 48 : (z + 1) * 96].astype(BF)
            at_rows = slice(z * 48, (z + 1) * 48)
            keep[at_rows, cols] = jnp.where(mine == 0, low, high)
            send[at_rows, cols] = jnp.where(mine == 0, high, low)


def rows_grad(at, places, tops, lows, rights, before):
    ff = rights[0].shape[1]
    rows = rights[0].shape[0] + rights[1].shape[0]
    count = len(tops)
    first = places[0]
    step = places[1] - first if count > 1 else 0
    out = pl.BlockSpec((PART // 2, ff), lambda s, a: (a[8 + first + s * step], 0))
    return call(
        lambda *refs: rows_kernel(count, *refs),
        count,
        [whole(block.shape) for block in (*tops, *lows, *rights)]
        + [pl.BlockSpec(memory_space=pl.ANY)] * len(before),
        [out, out, whole((1, ff))],
        [shaped((D // 2, ff))] * 2 + [shaped((1, ff), F32)],
        [pltpu.VMEM((PART, rows), BF)],
        cost(2 * rows * PART * ff * count, 5 * 10**6 * count),
        "rows_grad",
        {2 * count + 3 + n: n for n in range(len(before))},
    )(at, *tops, *lows, *rights, *before)


def weight_kernel(at, keep_l, send_l, right0, right1, q0, q1, q2, keep, send, square, sums):
    rows = right0.shape[0]
    keep_v = dot(keep_l[:, :rows], right0[...]) + dot(keep_l[:, rows:], right1[...])
    send_v = dot(send_l[:, :rows], right0[...]) + dot(send_l[:, rows:], right1[...])
    keep[...] = keep_v.astype(BF)
    send[...] = send_v.astype(BF)
    piece = jnp.sum(keep_v * keep_v, 0, keepdims=True) + jnp.sum(send_v * send_v, 0, keepdims=True)
    step = pl.program_id(0)

    @pl.when(step == 0)
    def _():
        sums[...] = piece

    @pl.when(step > 0)
    def _():
        sums[...] += piece

    @pl.when(step == pl.num_programs(0) - 1)
    def _():
        rest = q0[...] + q1[...] + q2[...]
        total = jnp.sum(sums[...], 1, keepdims=True) + jnp.sum(rest, 1, keepdims=True)
        square[...] = jnp.broadcast_to(total, square.shape)


def weight_grad(at, keep_l, send_l, rights, squares):
    ff = rights[0].shape[1]
    rows = rights[0].shape[0] + rights[1].shape[0]
    width = 512
    return call(
        weight_kernel,
        ff // width,
        [whole((D // 2, rows))] * 2
        + [columns(right.shape[0], width) for right in rights]
        + [whole((1, ff))] * 3,
        [columns(D // 2, width)] * 2 + [whole((1, 128))],
        [shaped((D // 2, ff))] * 2 + [shaped((1, 128), F32)],
        [pltpu.VMEM((1, width), F32)],
        cost(2 * rows * D * ff, 11 * 10**6),
        "weight_grad",
    )(at, keep_l, send_l, *rights, *squares)


def scaled(kept, got, u0, u1):
    return kept[...].astype(F32) * u0[0:1, 0:1] + got[...].astype(F32) * u1[0:1, 0:1]


def far_kernel(at, u0, u1, k1, k2, g1, g2, far1, far2):
    far1[0] = scaled(k1, g1, u0, u1).astype(BF)
    far2[0] = scaled(k2, g2, u0, u1).astype(BF)


def near_kernel(at, u0, u1, k1, k2, k3, k4, g1, g2, g3, g4, own, ahead2, behind1):
    own[0, 0] = scaled(k1, g1, u0, u1)
    own[0, 1] = scaled(k2, g2, u0, u1)
    behind1[0] = scaled(k3, g3, u0, u1).astype(BF)
    ahead2[0] = scaled(k4, g4, u0, u1).astype(BF)


def relay_kernel(at, u0, u1, k1, k2, g1, g2, up, down, ahead1, behind2):
    ahead1[0] = (scaled(k1, g1, u0, u1) + up[0].astype(F32)).astype(BF)
    behind2[0] = (scaled(k2, g2, u0, u1) + down[0].astype(F32)).astype(BF)


def close_kernel(at, own, up1, down1, up2, down2, out):
    out[0, 0] = (own[0, 0] + up1[0].astype(F32) + down1[0].astype(F32)).astype(BF)
    out[0, 1] = (own[0, 1] + up2[0].astype(F32) + down2[0].astype(F32)).astype(BF)


def ring_stage(at, u0, u1, first, second, move):
    ff = first[0].shape[1]
    block = lambda k: pl.BlockSpec((48, ff), lambda s, a: (a[12 + k] + s * a[5], 0))
    one = pl.BlockSpec((1, 48, ff), lambda s, *_: (s, 0, 0))
    both = pl.BlockSpec((1, 2, 48, ff), lambda s, *_: (s, 0, 0, 0))
    single = shaped((RING, 48, ff))
    unit = [whole((1, 128))] * 2
    size = RING * 48 * ff
    far1, far2 = call(
        far_kernel,
        RING,
        unit + [block(2)] * 4,
        [one, one],
        [single] * 2,
        [],
        cost(6 * size, 12 * size),
        "far",
    )(at, u0, u1, first[0], second[0], first[1], second[1])
    far1, far2 = move(far1, 1), move(far2, -1)
    order = [block(0), block(0), block(3), block(1)]
    own, ahead2, behind1 = call(
        near_kernel,
        RING,
        unit + order * 2,
        [both, one, one],
        [shaped((RING, 2, 48, ff), F32), single, single],
        [],
        cost(12 * size, 28 * size),
        "near",
    )(
        at, u0, u1, first[0], second[0], first[0], second[0],
        first[1], second[1], first[1], second[1],
    )
    up2, down1 = move(ahead2, 1), move(behind1, -1)
    ahead1, behind2 = call(
        relay_kernel,
        RING,
        unit + [block(1), block(3)] * 2 + [one, one],
        [one, one],
        [single] * 2,
        [],
        cost(8 * size, 16 * size),
        "relay",
    )(at, u0, u1, first[0], second[0], first[1], second[1], far1, far2)
    up1, down2 = move(ahead1, 1), move(behind2, -1)
    return call(
        close_kernel,
        RING,
        [both] + [one] * 4,
        both,
        shaped((RING, 2, 48, ff)),
        [],
        cost(4 * size, 20 * size),
        "close",
    )(at, own, up1, down1, up2, down2)


def local(
    latents,
    targets,
    tok_count,
    caption_states,
    cap_len,
    owner,
    ctx_w,
    mod_w,
    in_w,
    out_w,
    noise_in,
    noise_out,
):
    rows = latents.shape[0]
    token_span = rows // DRAWS
    me_x = lax.axis_index("mp")
    me_dp = lax.axis_index("dp")
    me_y, me_z, me_c = me_dp // 8, (me_dp // 2) % 4, me_dp % 2
    way = 1 - 2 * me_c

    ahead = [(me_x + k * way) % RING for k in range(RING)]
    swapped = [me_x, me_x ^ 1, 3 - me_x, (3 - me_x) ^ 1]
    me_one = jnp.where(me_c == 0, me_y, me_z)
    stride = jnp.where(me_c == 0, 4, 1)
    at = jnp.stack(
        [b * PART for b in swapped]
        + [me_c * 48, jnp.where(me_c == 0, 1, 4), me_c * 0, me_c * 0]
        + ahead
        + [((me_one + k) % RING) * stride for k in range(RING)]
    ).astype(jnp.int32)
    outs = [lax.dynamic_slice_in_dim(out_w, b * PART, PART, 0) for b in ahead]

    positions = jnp.arange(caption_states.shape[1])
    keep_mask = (positions[None, :] < cap_len[:, None]).astype(BF)
    summed = jnp.einsum("ec,ecf->ef", keep_mask, caption_states, preferred_element_type=F32)
    pooled = (summed / cap_len[:, None].astype(F32)).astype(BF).astype(F32)
    everywhere = jnp.broadcast_to(pooled.reshape(1, 8, -1), (32, 8, pooled.shape[1] // 8))
    received = lax.all_to_all(everywhere, "dp", 0, 0, tiled=True)

    behind, next_ahead = by_x(latents, 1), by_x(latents, -1)
    cut = rows * 3 // 4
    received, behind, next_ahead, at, outs = lax.optimization_barrier(
        (received, behind, next_ahead, at, outs)
    )
    far = by_x(behind, 1)
    wanted = (owner == me_dp)[:, None, None]
    mine = jnp.sum(jnp.where(wanted, received, 0.0), 0).reshape(1, -1).astype(BF)

    context = dot(mine, ctx_w)
    context = context + swap_x(context, 0)
    swapped_context, far = lax.optimization_barrier((swap_x(context, 1), far))
    context = context + swapped_context
    conditioning = context * lax.rsqrt(jnp.mean(context * context, 1, keepdims=True) + 1e-06)
    chosen = jax.nn.silu(conditioning).astype(BF)
    modulation = jnp.einsum("ed,dkf->ekf", chosen, mod_w, preferred_element_type=F32)[0]
    gate = modulation[2:3]
    own_mods = modulation
    pair_mods = swap_x(own_mods, 0)
    far_mods = swap_x(jnp.concatenate([own_mods, pair_mods], 0), 1)
    mods = (own_mods, pair_mods, far_mods)

    count = tok_count[0]
    factor = 2.0 / (D * DRAWS * count.astype(F32))

    def slope_of(pre):
        square = pre * pre
        bent = jnp.tanh(pre * (C1 + (C1 * C2) * square))
        half = 0.5 * (1.0 + bent)
        return half + (0.5 * pre) * (1.0 - bent * bent) * (C1 + (3.0 * C1 * C2) * square)

    def project(hidden, j):
        return lax.dot_general(
            hidden, outs[j], (((1,), (1,)), ((), ())), preferred_element_type=F32
        )

    def leave(first, last, own, up, down):
        at_rows = slice(first, last)
        output = latents[at_rows].astype(F32) + gate * (
            own + up.astype(F32) + down.astype(F32)
        )
        live = (jnp.arange(first, last) % token_span < count).astype(F32)[:, None]
        delta = (output - targets[at_rows].astype(F32)) * live * factor
        return (gate * delta).astype(BF)

    latent_blocks = (latents, next_ahead, far, behind)
    modded0, hidden0, pre0 = forward(0, cut, at, latent_blocks, mods, in_w)
    far0, down0 = project(hidden0, 2).astype(BF), project(hidden0, 3).astype(BF)
    far0 = by_x(far0, 1)
    at_next, down0 = lax.optimization_barrier((at, down0))
    down0 = by_x(down0, -1)
    up0, own0 = lax.optimization_barrier((project(hidden0, 1), project(hidden0, 0)))
    modded1, hidden1, pre1 = forward(
        cut, rows - cut, at_next, latent_blocks, mods, in_w
    )
    hidden1, far0, down0 = lax.optimization_barrier((hidden1, far0, down0))
    up0 = (up0 + far0.astype(F32)).astype(BF)
    up0, hidden1 = lax.optimization_barrier((up0, hidden1))
    up0 = by_x(up0, 1)
    far1, up1 = project(hidden1, 2).astype(BF), project(hidden1, 1).astype(BF)
    far1, up1, hidden1, at_late, pre0, pre1 = lax.optimization_barrier(
        (far1, up1, hidden1, at, pre0, pre1)
    )
    far1, up1 = by_x(far1, -1), by_x(up1, 1)
    back0 = leave(0, cut, own0, up0, down0)
    hidden1_late, back0 = lax.optimization_barrier((hidden1, back0))
    down1, own1 = project(hidden1_late, 3), project(hidden1_late, 0)
    behind0, ahead0 = by_x(back0, 1), by_x(back0, -1)
    down1 = by_x((down1 + far1.astype(F32)).astype(BF), -1)
    slope0, slope1 = slope_of(pre0).astype(BF), slope_of(pre1).astype(BF)
    mod_keep, mod_send = turn(at_late, modded0, modded1)
    down1, slope0, slope1, mod_keep, mod_send, behind0, ahead0 = lax.optimization_barrier(
        (down1, slope0, slope1, mod_keep, mod_send, behind0, ahead0)
    )
    back1 = leave(cut, rows, own1, up1, down1)
    far0 = by_x(behind0, 1)
    behind1, ahead1 = by_x(back1, 1), by_x(back1, -1)
    far1 = by_x(ahead1, -1)

    rights = (hidden0, hidden1)
    *second, square_a = rows_grad(at, (0,), (back0,), (back1,), rights, ())
    grad0 = backward(at, (back0, ahead0, far0, behind0), out_w, slope0)
    at_last, grad0 = lax.optimization_barrier((at, grad0))
    *second, square_b = rows_grad(
        at_last, (1, 3), (ahead0, behind0), (ahead1, behind1), rights, tuple(second)
    )
    grad1 = backward(at_last, (back1, ahead1, far1, behind1), out_w, slope1)
    *second, square_c = rows_grad(at, (2,), (far0,), (far1,), rights, tuple(second))
    keep2, send2 = second
    got2 = by_core(send2)
    keep1, send1, square = weight_grad(
        at, mod_keep, mod_send, (grad0, grad1), (square_a, square_b, square_c)
    )
    got1 = by_core(send1)
    square = square + swap_x(square, 0)
    square = square + swap_x(square, 1)
    root = math.sqrt(2.0 * D * FF)
    unit = root / (jnp.sqrt(square) + 0.01)

    value = ring_stage(
        at, unit, by_core(unit), (keep1, got1), (keep2, got2), lambda v, w: by_turns(v, w, True)
    )
    groups = [[(y * RING + z) * 2 for z in range(RING)] for y in range(RING)]
    groups += [[(y * RING + z) * 2 + 1 for y in range(RING)] for z in range(RING)]
    got = lax.all_to_all(value, "dp", 0, 0, axis_index_groups=groups, tiled=True)
    value = jnp.sum(got.astype(F32), 0)
    return (value[0] + noise_in) / 32.0, (value[1] + noise_out) / 32.0


def solution(mesh):
    placed = (
        P("dp", "mp"),
        P("dp", "mp"),
        P("dp"),
        P("dp", None, "mp"),
        P("dp"),
        P(),
        P("mp", None),
        P(None, None, "mp"),
        P(None, "mp"),
        P(None, "mp"),
        P("dp", "mp"),
        P("dp", "mp"),
    )
    return jax.shard_map(
        local, mesh=mesh, in_specs=placed, out_specs=(P("dp", "mp"), P("dp", "mp")), check_vma=False
    )
```

```python
import math

import jax
import jax.numpy as jnp
from jax import lax
from jax.experimental import pallas as pl
from jax.experimental.pallas import tpu as pltpu
from jax.sharding import PartitionSpec as P

D = 1536
FF = 6144
DRAWS = 4
BF = jnp.bfloat16
F32 = jnp.float32
RING = 4
PART = D // RING
WIDE = 512
VMEM_LIMIT = 32 * 1024 * 1024
C1 = math.sqrt(2.0 / math.pi)
C2 = 0.044715


def dot(left, right):
    return jnp.dot(left, right, preferred_element_type=F32)


def sign(core, way):
    return way if core == 0 else -way


def by_x(value, way):
    pairs = []
    for dp in range(32):
        for x in range(RING):
            pairs.append((dp * RING + x, dp * RING + (x + sign(dp % 2, way)) % RING))
    return lax.ppermute(value, ("dp", "mp"), pairs)


def by_dp(value, target):
    pairs = []
    for y in range(RING):
        for z in range(RING):
            for c in range(2):
                ty, tz, tc = target(y, z, c)
                pairs.append(((y * RING + z) * 2 + c, ((ty % RING) * RING + tz % RING) * 2 + tc))
    return lax.ppermute(value, "dp", pairs)


def by_turns(value, way, first):
    return by_dp(
        value,
        lambda y, z, c: (y + way, z, c) if (c == 0) == first else (y, z + way, c),
    )


def by_core(value):
    return by_dp(value, lambda y, z, c: (y, z, 1 - c))


def swap_x(value, kind):
    other = [x ^ 1 for x in range(RING)] if kind == 0 else [3 - x for x in range(RING)]
    return lax.ppermute(value, "mp", list(enumerate(other)))


def params():
    return pltpu.CompilerParams(vmem_limit_bytes=VMEM_LIMIT)


def shaped(shape, dtype=BF):
    return jax.ShapeDtypeStruct(shape, dtype)


def cost(flops, size, special=0):
    return pl.CostEstimate(flops=flops, bytes_accessed=size, transcendentals=special)


def in_hbm(value):
    return pltpu.with_memory_space_constraint(value, pltpu.HBM)


def whole(shape):
    return pl.BlockSpec(shape, lambda s, *_: (0, 0))


def columns(rows, width):
    return pl.BlockSpec((rows, width), lambda s, *_: (0, s))


def call(kernel, grid, in_specs, out_specs, out_shape, scratch, estimate, name, aliases={}):
    return pl.pallas_call(
        kernel,
        grid_spec=pltpu.PrefetchScalarGridSpec(
            num_scalar_prefetch=1,
            grid=(grid,),
            in_specs=in_specs,
            out_specs=out_specs,
            scratch_shapes=scratch,
        ),
        out_shape=out_shape,
        input_output_aliases=aliases,
        compiler_params=params(),
        cost_estimate=estimate,
        name=name,
    )


def forward_kernel(at, x0, x1, x2, x3, m0, m1, m2, in_w, modded_o, hidden, pre, mods, modded):
    step = pl.program_id(0)

    @pl.when(step == 0)
    def _():
        for place, ref, row in ((0, m0, 0), (1, m1, 0), (2, m2, 0), (3, m2, 3)):
            mods[:, pl.ds(pl.multiple_of(at[place], 128), PART)] = ref[row : row + 2]
        total = 0.0
        squares = 0.0
        for ref in (x0, x1, x2, x3):
            value = ref[...].astype(F32)
            total = total + jnp.sum(value, 1, keepdims=True)
            squares = squares + jnp.sum(value * value, 1, keepdims=True)
        center = total / D
        scale = lax.rsqrt(squares / D - center * center + 1e-06)
        for k, ref in enumerate((x0, x1, x2, x3)):
            cols = pl.ds(pl.multiple_of(at[8 + k] * PART, 128), PART)
            normed = (ref[...].astype(F32) - center) * scale
            modded[:, cols] = (normed * (1.0 + mods[1:2, cols]) + mods[0:1, cols]).astype(BF)

    modded_o[...] = modded[:, pl.ds(pl.multiple_of(step * WIDE, 128), WIDE)]
    value = dot(modded[...], in_w[...])
    pre[...] = value
    bent = jnp.tanh(value * (C1 + (C1 * C2) * (value * value)))
    hidden[...] = ((0.5 * value) * (1.0 + bent)).astype(BF)


def forward(chunk, at, blocks, mods, in_w):
    rows, ff = blocks[0].shape[0] // 2, in_w.shape[1]
    piece = pl.BlockSpec((rows, PART), lambda s, *_: (chunk, 0))
    return call(
        forward_kernel,
        ff // WIDE,
        [piece] * 4
        + [whole((3, PART)), whole((3, PART)), whole((6, PART)), columns(D, WIDE)],
        [columns(rows, WIDE)] * 3,
        [shaped((rows, D)), shaped((rows, ff)), shaped((rows, ff), F32)],
        [pltpu.VMEM((2, D), F32), pltpu.VMEM((rows, D), BF)],
        cost(2 * rows * D * ff, 12 * 10**6, rows * ff),
        "forward",
    )(at, *[in_hbm(b) for b in blocks], *mods, in_hbm(in_w))


def split_rows(at, turned, keep, send):
    mine = at[4]
    for z in range(RING):
        keep[z * 48 : (z + 1) * 48] = turned[pl.ds(pl.multiple_of(z * 96 + mine, 16), 48)]
        send[z * 48 : (z + 1) * 48] = turned[pl.ds(pl.multiple_of(z * 96 + 48 - mine, 16), 48)]


def turn_kernel(at, top, low, keep, send, turned):
    turned[:, : top.shape[0]] = top[...].T
    turned[:, top.shape[0] :] = low[...].T
    split_rows(at, turned, keep, send)


def turn(at, top, low):
    rows = top.shape[0]
    out = pl.BlockSpec((PART // 2, 2 * rows), lambda s, *_: (s, 0))
    return call(
        turn_kernel,
        RING,
        [columns(rows, PART)] * 2,
        [out, out],
        [shaped((D // 2, 2 * rows))] * 2,
        [pltpu.VMEM((PART, 2 * rows), BF)],
        cost(2 * rows * D, 8 * rows * D),
        "turn",
    )(at, top, low)


def backward_kernel(at, b0, b1, b2, b3, out_w, slope, grad, back):
    @pl.when(pl.program_id(0) == 0)
    def _():
        for k, ref in enumerate((b0, b1, b2, b3)):
            back[:, pl.ds(pl.multiple_of(at[8 + k] * PART, 128), PART)] = ref[...]

    grad[...] = (dot(back[...], out_w[...]) * slope[...].astype(F32)).astype(BF)


def backward(at, blocks, out_w, slope):
    rows, ff = slope.shape
    return call(
        backward_kernel,
        ff // WIDE,
        [whole((rows, PART))] * 4 + [columns(D, WIDE), columns(rows, WIDE)],
        columns(rows, WIDE),
        shaped((rows, ff)),
        [pltpu.VMEM((rows, D), BF)],
        cost(2 * rows * D * ff, 14 * 10**6),
        "backward",
    )(at, *blocks, out_w, slope)


def turn_blocks(groups, turned):
    for k in range(len(groups[0])):

        @pl.when(pl.program_id(0) == k)
        def _():
            start = 0
            for group in groups:
                rows = group[k].shape[0]
                turned[:, start : start + rows] = group[k][...].T
                start += rows


def cut_refs(refs, count, groups):
    return [refs[g * count : (g + 1) * count] for g in range(groups)], refs[groups * count :]


def product(turned, rights, cols):
    start = 0
    value = 0.0
    for right in rights:
        rows = right.shape[0]
        value = value + dot(turned[:, start : start + rows], right[:, cols])
        start += rows
    return value


def partial_kernel(count, at, *refs):
    groups, (right, out, turned) = cut_refs(refs, count, 1)
    turn_blocks(groups, turned)
    for n in range(right.shape[1] // 512):
        cols = slice(n * 512, (n + 1) * 512)
        out[:, cols] = product(turned, [right], cols)


def rows_partial(at, blocks, right):
    rows, ff = right.shape
    count = len(blocks)
    return call(
        lambda *refs: partial_kernel(count, *refs),
        count,
        [whole((rows, PART))] * count + [whole((rows, ff))],
        pl.BlockSpec((PART, ff), lambda s, *_: (s, 0)),
        shaped((count * PART, ff), F32),
        [pltpu.VMEM((PART, rows), BF)],
        cost(2 * rows * PART * ff * count, 4 * 10**6 * count),
        "rows_partial",
    )(at, *blocks, right)


def rows_kernel(count, parts, partials, at, *refs):
    groups, rest = cut_refs(refs, count, parts)
    rights, rest = rest[:parts], rest[parts:]
    keep, send, square, turned = refs[-4:]
    turn_blocks(groups, turned)
    mine = at[4]
    for n in range(rights[0].shape[1] // 512):
        cols = slice(n * 512, (n + 1) * 512)
        value = product(turned, rights, cols)
        if partials:
            value = value + rest[0][:, cols]
        piece = jnp.sum(value * value, 0, keepdims=True)

        @pl.when(pl.program_id(0) == 0)
        def _():
            square[:, cols] = piece

        @pl.when(pl.program_id(0) > 0)
        def _():
            square[:, cols] += piece

        for z in range(RING):
            low = value[z * 96 : z * 96 + 48].astype(BF)
            high = value[z * 96 + 48 : (z + 1) * 96].astype(BF)
            at_rows = slice(z * 48, (z + 1) * 48)
            keep[at_rows, cols] = jnp.where(mine == 0, low, high)
            send[at_rows, cols] = jnp.where(mine == 0, high, low)


def rows_grad(at, places, groups, rights, partials, before):
    ff = rights[0].shape[1]
    rows = sum(right.shape[0] for right in rights)
    count, parts = len(places), len(groups)
    first = places[0]
    step = places[1] - first if count > 1 else 0
    out = pl.BlockSpec((PART // 2, ff), lambda s, a: (a[8 + first + s * step], 0))
    blocks = [block for group in groups for block in group]
    operands = [*blocks, *rights, *partials, *before]
    return call(
        lambda *refs: rows_kernel(count, parts, len(partials), *refs),
        count,
        [whole(value.shape) for value in (*blocks, *rights)]
        + [pl.BlockSpec((PART, ff), lambda s, *_: (s, 0))] * len(partials)
        + [pl.BlockSpec(memory_space=pl.ANY)] * len(before),
        [out, out, whole((1, ff))],
        [shaped((D // 2, ff))] * 2 + [shaped((1, ff), F32)],
        [pltpu.VMEM((PART, rows), BF)],
        cost(2 * rows * PART * ff * count, 5 * 10**6 * count),
        "rows_grad",
        {len(operands) - len(before) + 1 + n: n for n in range(len(before))},
    )(at, *operands)


def weight_kernel(at, keep_l, send_l, right0, right1, q0, q1, q2, keep, send, square, sums):
    rows = right0.shape[0]
    keep_v = dot(keep_l[:, :rows], right0[...]) + dot(keep_l[:, rows:], right1[...])
    send_v = dot(send_l[:, :rows], right0[...]) + dot(send_l[:, rows:], right1[...])
    keep[...] = keep_v.astype(BF)
    send[...] = send_v.astype(BF)
    piece = jnp.sum(keep_v * keep_v, 0, keepdims=True) + jnp.sum(send_v * send_v, 0, keepdims=True)
    step = pl.program_id(0)

    @pl.when(step == 0)
    def _():
        sums[...] = piece

    @pl.when(step > 0)
    def _():
        sums[...] += piece

    @pl.when(step == pl.num_programs(0) - 1)
    def _():
        rest = q0[...] + q1[...] + q2[...]
        total = jnp.sum(sums[...], 1, keepdims=True) + jnp.sum(rest, 1, keepdims=True)
        square[...] = jnp.broadcast_to(total, square.shape)


def weight_grad(at, keep_l, send_l, rights, squares):
    rows, ff = rights[0].shape
    width = 512
    return call(
        weight_kernel,
        ff // width,
        [whole((D // 2, 2 * rows))] * 2 + [columns(rows, width)] * 2 + [whole((1, ff))] * 3,
        [columns(D // 2, width)] * 2 + [whole((1, 128))],
        [shaped((D // 2, ff))] * 2 + [shaped((1, 128), F32)],
        [pltpu.VMEM((1, width), F32)],
        cost(4 * rows * D * ff, 11 * 10**6),
        "weight_grad",
    )(at, keep_l, send_l, *rights, *squares)


def scaled(kept, got, u0, u1):
    return kept[...].astype(F32) * u0[0:1, 0:1] + got[...].astype(F32) * u1[0:1, 0:1]


def far_kernel(at, u0, u1, k1, k2, g1, g2, far1, far2):
    far1[0] = scaled(k1, g1, u0, u1).astype(BF)
    far2[0] = scaled(k2, g2, u0, u1).astype(BF)


def near_kernel(at, u0, u1, k1, k2, k3, k4, g1, g2, g3, g4, own, ahead2, behind1):
    own[0, 0] = scaled(k1, g1, u0, u1)
    own[0, 1] = scaled(k2, g2, u0, u1)
    behind1[0] = scaled(k3, g3, u0, u1).astype(BF)
    ahead2[0] = scaled(k4, g4, u0, u1).astype(BF)


def relay_kernel(at, u0, u1, k1, k2, g1, g2, up, down, ahead1, behind2):
    ahead1[0] = (scaled(k1, g1, u0, u1) + up[0].astype(F32)).astype(BF)
    behind2[0] = (scaled(k2, g2, u0, u1) + down[0].astype(F32)).astype(BF)


def close_kernel(at, own, up1, down1, up2, down2, out):
    out[0, 0] = (own[0, 0] + up1[0].astype(F32) + down1[0].astype(F32)).astype(BF)
    out[0, 1] = (own[0, 1] + up2[0].astype(F32) + down2[0].astype(F32)).astype(BF)


def ring_stage(at, u0, u1, first, second, move):
    ff = first[0].shape[1]
    block = lambda k: pl.BlockSpec((48, ff), lambda s, a: (a[12 + k] + s * a[5], 0))
    one = pl.BlockSpec((1, 48, ff), lambda s, *_: (s, 0, 0))
    both = pl.BlockSpec((1, 2, 48, ff), lambda s, *_: (s, 0, 0, 0))
    single = shaped((RING, 48, ff))
    unit = [whole((1, 128))] * 2
    size = RING * 48 * ff
    far1, far2 = call(
        far_kernel,
        RING,
        unit + [block(2)] * 4,
        [one, one],
        [single] * 2,
        [],
        cost(6 * size, 12 * size),
        "far",
    )(at, u0, u1, first[0], second[0], first[1], second[1])
    far1, far2 = move(far1, 1), move(far2, -1)
    order = [block(0), block(0), block(3), block(1)]
    own, ahead2, behind1 = call(
        near_kernel,
        RING,
        unit + order * 2,
        [both, one, one],
        [shaped((RING, 2, 48, ff), F32), single, single],
        [],
        cost(12 * size, 28 * size),
        "near",
    )(
        at, u0, u1, first[0], second[0], first[0], second[0],
        first[1], second[1], first[1], second[1],
    )
    up2, down1 = move(ahead2, 1), move(behind1, -1)
    ahead1, behind2 = call(
        relay_kernel,
        RING,
        unit + [block(1), block(3)] * 2 + [one, one],
        [one, one],
        [single] * 2,
        [],
        cost(8 * size, 16 * size),
        "relay",
    )(at, u0, u1, first[0], second[0], first[1], second[1], far1, far2)
    up1, down2 = move(ahead1, 1), move(behind2, -1)
    return call(
        close_kernel,
        RING,
        [both] + [one] * 4,
        both,
        shaped((RING, 2, 48, ff)),
        [],
        cost(4 * size, 20 * size),
        "close",
    )(at, own, up1, down1, up2, down2)


def local(
    latents,
    targets,
    tok_count,
    caption_states,
    cap_len,
    owner,
    ctx_w,
    mod_w,
    in_w,
    out_w,
    noise_in,
    noise_out,
):
    rows = latents.shape[0]
    token_span = rows // DRAWS
    me_x = lax.axis_index("mp")
    me_dp = lax.axis_index("dp")
    me_y, me_z, me_c = me_dp // 8, (me_dp // 2) % 4, me_dp % 2
    way = 1 - 2 * me_c

    ahead = [(me_x + k * way) % RING for k in range(RING)]
    swapped = [me_x, me_x ^ 1, 3 - me_x, (3 - me_x) ^ 1]
    me_one = jnp.where(me_c == 0, me_y, me_z)
    stride = jnp.where(me_c == 0, 4, 1)
    at = jnp.stack(
        [b * PART for b in swapped]
        + [me_c * 48, jnp.where(me_c == 0, 1, 4), me_c * 0, me_c * 0]
        + ahead
        + [((me_one + k) % RING) * stride for k in range(RING)]
    ).astype(jnp.int32)
    outs = [lax.dynamic_slice_in_dim(out_w, b * PART, PART, 0) for b in ahead]

    positions = jnp.arange(caption_states.shape[1])
    keep_mask = (positions[None, :] < cap_len[:, None]).astype(BF)
    summed = jnp.einsum("ec,ecf->ef", keep_mask, caption_states, preferred_element_type=F32)
    pooled = (summed / cap_len[:, None].astype(F32)).astype(BF).astype(F32)
    everywhere = jnp.broadcast_to(pooled.reshape(1, 8, -1), (32, 8, pooled.shape[1] // 8))
    received = lax.all_to_all(everywhere, "dp", 0, 0, tiled=True)

    behind, next_ahead = by_x(latents, 1), by_x(latents, -1)
    half = rows // 2
    received, behind, next_ahead, at, outs = lax.optimization_barrier(
        (received, behind, next_ahead, at, outs)
    )
    far = by_x(behind, 1)
    wanted = (owner == me_dp)[:, None, None]
    mine = jnp.sum(jnp.where(wanted, received, 0.0), 0).reshape(1, -1).astype(BF)

    context = dot(mine, ctx_w)
    context = context + swap_x(context, 0)
    swapped_context, far = lax.optimization_barrier((swap_x(context, 1), far))
    context = context + swapped_context
    conditioning = context * lax.rsqrt(jnp.mean(context * context, 1, keepdims=True) + 1e-06)
    chosen = jax.nn.silu(conditioning).astype(BF)
    modulation = jnp.einsum("ed,dkf->ekf", chosen, mod_w, preferred_element_type=F32)[0]
    gate = modulation[2:3]
    own_mods = modulation
    pair_mods = swap_x(own_mods, 0)
    far_mods = swap_x(jnp.concatenate([own_mods, pair_mods], 0), 1)
    mods = (own_mods, pair_mods, far_mods)

    count = tok_count[0]
    factor = 2.0 / (D * DRAWS * count.astype(F32))

    def slope_of(pre):
        square = pre * pre
        bent = jnp.tanh(pre * (C1 + (C1 * C2) * square))
        half = 0.5 * (1.0 + bent)
        return half + (0.5 * pre) * (1.0 - bent * bent) * (C1 + (3.0 * C1 * C2) * square)

    def project(hidden, j):
        return lax.dot_general(
            hidden, outs[j], (((1,), (1,)), ((), ())), preferred_element_type=F32
        )

    def leave(k, own, up, down):
        at_rows = slice(k * half, (k + 1) * half)
        output = latents[at_rows].astype(F32) + gate * (
            own + up.astype(F32) + down.astype(F32)
        )
        live = (jnp.arange(k * half, (k + 1) * half) % token_span < count).astype(F32)[:, None]
        delta = (output - targets[at_rows].astype(F32)) * live * factor
        return (gate * delta).astype(BF)

    latent_blocks = (latents, next_ahead, far, behind)
    modded0, hidden0, pre0 = forward(0, at, latent_blocks, mods, in_w)
    far0, down0 = project(hidden0, 2).astype(BF), project(hidden0, 3).astype(BF)
    far0 = by_x(far0, 1)
    at_next, down0 = lax.optimization_barrier((at, down0))
    down0 = by_x(down0, -1)
    up0 = lax.optimization_barrier(project(hidden0, 1))
    modded1, hidden1, pre1 = forward(1, at_next, latent_blocks, mods, in_w)
    hidden1, far0, down0 = lax.optimization_barrier((hidden1, far0, down0))
    up0 = (up0 + far0.astype(F32)).astype(BF)
    up0, hidden1 = lax.optimization_barrier((up0, hidden1))
    up0 = by_x(up0, 1)
    far1, up1 = project(hidden1, 2).astype(BF), project(hidden1, 1).astype(BF)
    far1, up1, hidden0_late, at_late, pre0, pre1 = lax.optimization_barrier(
        (far1, up1, hidden0, at, pre0, pre1)
    )
    own0 = lax.optimization_barrier(project(hidden0_late, 0))
    far1, up1 = by_x(far1, -1), by_x(up1, 1)
    back0 = leave(0, own0, up0, down0)
    hidden1_late, back0 = lax.optimization_barrier((hidden1, back0))
    down1, own1 = lax.optimization_barrier(
        (project(hidden1_late, 3), project(hidden1_late, 0))
    )
    behind0, ahead0 = by_x(back0, 1), by_x(back0, -1)
    down1 = by_x((down1 + far1.astype(F32)).astype(BF), -1)
    slope0, slope1 = slope_of(pre0).astype(BF), slope_of(pre1).astype(BF)
    mod_keep, mod_send = turn(at_late, modded0, modded1)
    down1, slope0, slope1, mod_keep, mod_send, behind0, ahead0 = lax.optimization_barrier(
        (down1, slope0, slope1, mod_keep, mod_send, behind0, ahead0)
    )
    back1 = leave(1, own1, up1, down1)
    far0 = by_x(behind0, 1)
    behind1, ahead1 = by_x(back1, 1), by_x(back1, -1)
    far1 = by_x(ahead1, -1)

    rights = (hidden0, hidden1)
    *second, square_a = rows_grad(at, (0,), ((back0,), (back1,)), rights, (), ())
    partial = rows_partial(at, (ahead0, behind0), hidden0)
    grad0 = backward(at, (back0, ahead0, far0, behind0), out_w, slope0)
    *second, square_b = rows_grad(
        at, (1, 3), ((ahead1, behind1),), (hidden1,), (partial,), tuple(second)
    )
    grad1 = backward(at, (back1, ahead1, far1, behind1), out_w, slope1)
    *second, square_c = rows_grad(at, (2,), ((far0,), (far1,)), rights, (), tuple(second))
    keep2, send2 = second
    got2 = by_core(send2)
    keep1, send1, square = weight_grad(
        at, mod_keep, mod_send, (grad0, grad1), (square_a, square_b, square_c)
    )
    got1 = by_core(send1)
    square = square + swap_x(square, 0)
    square = square + swap_x(square, 1)
    root = math.sqrt(2.0 * D * FF)
    unit = root / (jnp.sqrt(square) + 0.01)

    value = ring_stage(
        at, unit, by_core(unit), (keep1, got1), (keep2, got2), lambda v, w: by_turns(v, w, True)
    )
    groups = [[(y * RING + z) * 2 for z in range(RING)] for y in range(RING)]
    groups += [[(y * RING + z) * 2 + 1 for y in range(RING)] for z in range(RING)]
    got = lax.all_to_all(value, "dp", 0, 0, axis_index_groups=groups, tiled=True)
    value = jnp.sum(got.astype(F32), 0)
    return (value[0] + noise_in) / 32.0, (value[1] + noise_out) / 32.0


def solution(mesh):
    placed = (
        P("dp", "mp"),
        P("dp", "mp"),
        P("dp"),
        P("dp", None, "mp"),
        P("dp"),
        P(),
        P("mp", None),
        P(None, None, "mp"),
        P(None, "mp"),
        P(None, "mp"),
        P("dp", "mp"),
        P("dp", "mp"),
    )
    return jax.shard_map(
        local, mesh=mesh, in_specs=placed, out_specs=(P("dp", "mp"), P("dp", "mp")), check_vma=False
    )
```

```python
import math

import jax
import jax.numpy as jnp
from jax import lax
from jax.experimental import pallas as pl
from jax.experimental.pallas import tpu as pltpu
from jax.sharding import PartitionSpec as P

D = 1536
FF = 6144
DRAWS = 4
BF = jnp.bfloat16
F32 = jnp.float32
RING = 4
PART = D // RING
WIDE = 512
VMEM_LIMIT = 32 * 1024 * 1024
C1 = math.sqrt(2.0 / math.pi)
C2 = 0.044715


def dot(left, right):
    return jnp.dot(left, right, preferred_element_type=F32)


def sign(core, way):
    return way if core == 0 else -way


def by_x(value, way):
    pairs = []
    for dp in range(32):
        for x in range(RING):
            pairs.append((dp * RING + x, dp * RING + (x + sign(dp % 2, way)) % RING))
    return lax.ppermute(value, ("dp", "mp"), pairs)


def by_dp(value, target):
    pairs = []
    for y in range(RING):
        for z in range(RING):
            for c in range(2):
                ty, tz, tc = target(y, z, c)
                pairs.append(((y * RING + z) * 2 + c, ((ty % RING) * RING + tz % RING) * 2 + tc))
    return lax.ppermute(value, "dp", pairs)


def by_turns(value, way, first):
    return by_dp(
        value,
        lambda y, z, c: (y + way, z, c) if (c == 0) == first else (y, z + way, c),
    )


def by_core(value):
    return by_dp(value, lambda y, z, c: (y, z, 1 - c))


def swap_x(value, kind):
    other = [x ^ 1 for x in range(RING)] if kind == 0 else [x ^ 2 for x in range(RING)]
    return lax.ppermute(value, "mp", list(enumerate(other)))


def params():
    return pltpu.CompilerParams(vmem_limit_bytes=VMEM_LIMIT)


def shaped(shape, dtype=BF):
    return jax.ShapeDtypeStruct(shape, dtype)


def cost(flops, size, special=0):
    return pl.CostEstimate(flops=flops, bytes_accessed=size, transcendentals=special)


def in_hbm(value):
    return pltpu.with_memory_space_constraint(value, pltpu.HBM)


def whole(shape):
    return pl.BlockSpec(shape, lambda s, *_: (0, 0))


def columns(rows, width):
    return pl.BlockSpec((rows, width), lambda s, *_: (0, s))


def call(kernel, grid, in_specs, out_specs, out_shape, scratch, estimate, name, aliases={}):
    return pl.pallas_call(
        kernel,
        grid_spec=pltpu.PrefetchScalarGridSpec(
            num_scalar_prefetch=1,
            grid=(grid,),
            in_specs=in_specs,
            out_specs=out_specs,
            scratch_shapes=scratch,
        ),
        out_shape=out_shape,
        input_output_aliases=aliases,
        compiler_params=params(),
        cost_estimate=estimate,
        name=name,
    )


def forward_kernel(at, x0, x1, x2, x3, m0, m1, m2, in_w, modded_o, hidden, pre, mods, modded):
    step = pl.program_id(0)

    @pl.when(step == 0)
    def _():
        for place, ref, row in ((0, m0, 0), (1, m1, 0), (2, m2, 0), (3, m2, 3)):
            mods[:, pl.ds(pl.multiple_of(at[place], 128), PART)] = ref[row : row + 2]
        total = 0.0
        squares = 0.0
        for ref in (x0, x1, x2, x3):
            value = ref[...].astype(F32)
            total = total + jnp.sum(value, 1, keepdims=True)
            squares = squares + jnp.sum(value * value, 1, keepdims=True)
        center = total / D
        scale = lax.rsqrt(squares / D - center * center + 1e-06)
        for k, ref in enumerate((x0, x1, x2, x3)):
            cols = pl.ds(pl.multiple_of(at[8 + k] * PART, 128), PART)
            normed = (ref[...].astype(F32) - center) * scale
            modded[:, cols] = (normed * (1.0 + mods[1:2, cols]) + mods[0:1, cols]).astype(BF)

    modded_o[...] = modded[:, pl.ds(pl.multiple_of(step * WIDE, 128), WIDE)]
    value = dot(modded[...], in_w[...])
    pre[...] = value
    bent = jnp.tanh(value * (C1 + (C1 * C2) * (value * value)))
    hidden[...] = ((0.5 * value) * (1.0 + bent)).astype(BF)


def forward(chunk, at, blocks, mods, in_w):
    rows, ff = blocks[0].shape[0] // 2, in_w.shape[1]
    piece = pl.BlockSpec((rows, PART), lambda s, *_: (chunk, 0))
    return call(
        forward_kernel,
        ff // WIDE,
        [piece] * 4
        + [whole((3, PART)), whole((3, PART)), whole((6, PART)), columns(D, WIDE)],
        [columns(rows, WIDE)] * 3,
        [shaped((rows, D)), shaped((rows, ff)), shaped((rows, ff), F32)],
        [pltpu.VMEM((2, D), F32), pltpu.VMEM((rows, D), BF)],
        cost(2 * rows * D * ff, 12 * 10**6, rows * ff),
        "forward",
    )(at, *[in_hbm(b) for b in blocks], *mods, in_hbm(in_w))


def split_rows(at, turned, keep, send):
    mine = at[4]
    for z in range(RING):
        keep[z * 48 : (z + 1) * 48] = turned[pl.ds(pl.multiple_of(z * 96 + mine, 16), 48)]
        send[z * 48 : (z + 1) * 48] = turned[pl.ds(pl.multiple_of(z * 96 + 48 - mine, 16), 48)]


def turn_kernel(at, top, low, keep, send, turned):
    turned[:, : top.shape[0]] = top[...].T
    turned[:, top.shape[0] :] = low[...].T
    split_rows(at, turned, keep, send)


def turn(at, top, low):
    rows = top.shape[0]
    out = pl.BlockSpec((PART // 2, 2 * rows), lambda s, *_: (s, 0))
    return call(
        turn_kernel,
        RING,
        [columns(rows, PART)] * 2,
        [out, out],
        [shaped((D // 2, 2 * rows))] * 2,
        [pltpu.VMEM((PART, 2 * rows), BF)],
        cost(2 * rows * D, 8 * rows * D),
        "turn",
    )(at, top, low)


def backward_kernel(at, b0, b1, b2, b3, out_w, slope, grad, back):
    @pl.when(pl.program_id(0) == 0)
    def _():
        for k, ref in enumerate((b0, b1, b2, b3)):
            back[:, pl.ds(pl.multiple_of(at[8 + k] * PART, 128), PART)] = ref[...]

    grad[...] = (dot(back[...], out_w[...]) * slope[...].astype(F32)).astype(BF)


def backward(at, blocks, out_w, slope):
    rows, ff = slope.shape
    return call(
        backward_kernel,
        ff // WIDE,
        [whole((rows, PART))] * 4 + [columns(D, WIDE), columns(rows, WIDE)],
        columns(rows, WIDE),
        shaped((rows, ff)),
        [pltpu.VMEM((rows, D), BF)],
        cost(2 * rows * D * ff, 14 * 10**6),
        "backward",
    )(at, *blocks, out_w, slope)


def turn_blocks(groups, turned):
    for k in range(len(groups[0])):

        @pl.when(pl.program_id(0) == k)
        def _():
            start = 0
            for group in groups:
                rows = group[k].shape[0]
                turned[:, start : start + rows] = group[k][...].T
                start += rows


def cut_refs(refs, count, groups):
    return [refs[g * count : (g + 1) * count] for g in range(groups)], refs[groups * count :]


def product(turned, rights, cols):
    start = 0
    value = 0.0
    for right in rights:
        rows = right.shape[0]
        value = value + dot(turned[:, start : start + rows], right[:, cols])
        start += rows
    return value


def partial_kernel(count, at, *refs):
    groups, (right, out, turned) = cut_refs(refs, count, 1)
    turn_blocks(groups, turned)
    for n in range(right.shape[1] // 512):
        cols = slice(n * 512, (n + 1) * 512)
        out[:, cols] = product(turned, [right], cols)


def rows_partial(at, blocks, right):
    rows, ff = right.shape
    count = len(blocks)
    return call(
        lambda *refs: partial_kernel(count, *refs),
        count,
        [whole((rows, PART))] * count + [whole((rows, ff))],
        pl.BlockSpec((PART, ff), lambda s, *_: (s, 0)),
        shaped((count * PART, ff), F32),
        [pltpu.VMEM((PART, rows), BF)],
        cost(2 * rows * PART * ff * count, 4 * 10**6 * count),
        "rows_partial",
    )(at, *blocks, right)


def rows_kernel(count, parts, partials, at, *refs):
    groups, rest = cut_refs(refs, count, parts)
    rights, rest = rest[:parts], rest[parts:]
    keep, send, square, turned = refs[-4:]
    turn_blocks(groups, turned)
    mine = at[4]
    for n in range(rights[0].shape[1] // 512):
        cols = slice(n * 512, (n + 1) * 512)
        value = product(turned, rights, cols)
        if partials:
            value = value + rest[0][:, cols]
        piece = jnp.sum(value * value, 0, keepdims=True)

        @pl.when(pl.program_id(0) == 0)
        def _():
            square[:, cols] = piece

        @pl.when(pl.program_id(0) > 0)
        def _():
            square[:, cols] += piece

        for z in range(RING):
            low = value[z * 96 : z * 96 + 48].astype(BF)
            high = value[z * 96 + 48 : (z + 1) * 96].astype(BF)
            at_rows = slice(z * 48, (z + 1) * 48)
            keep[at_rows, cols] = jnp.where(mine == 0, low, high)
            send[at_rows, cols] = jnp.where(mine == 0, high, low)


def rows_grad(at, places, groups, rights, partials, before):
    ff = rights[0].shape[1]
    rows = sum(right.shape[0] for right in rights)
    count, parts = len(places), len(groups)
    first = places[0]
    step = places[1] - first if count > 1 else 0
    out = pl.BlockSpec((PART // 2, ff), lambda s, a: (a[8 + first + s * step], 0))
    blocks = [block for group in groups for block in group]
    operands = [*blocks, *rights, *partials, *before]
    return call(
        lambda *refs: rows_kernel(count, parts, len(partials), *refs),
        count,
        [whole(value.shape) for value in (*blocks, *rights)]
        + [pl.BlockSpec((PART, ff), lambda s, *_: (s, 0))] * len(partials)
        + [pl.BlockSpec(memory_space=pl.ANY)] * len(before),
        [out, out, whole((1, ff))],
        [shaped((D // 2, ff))] * 2 + [shaped((1, ff), F32)],
        [pltpu.VMEM((PART, rows), BF)],
        cost(2 * rows * PART * ff * count, 5 * 10**6 * count),
        "rows_grad",
        {len(operands) - len(before) + 1 + n: n for n in range(len(before))},
    )(at, *operands)


def weight_kernel(at, keep_l, send_l, right0, right1, q0, q1, q2, keep, send, square, sums):
    rows = right0.shape[0]
    keep_v = dot(keep_l[:, :rows], right0[...]) + dot(keep_l[:, rows:], right1[...])
    send_v = dot(send_l[:, :rows], right0[...]) + dot(send_l[:, rows:], right1[...])
    keep[...] = keep_v.astype(BF)
    send[...] = send_v.astype(BF)
    piece = jnp.sum(keep_v * keep_v, 0, keepdims=True) + jnp.sum(send_v * send_v, 0, keepdims=True)
    step = pl.program_id(0)

    @pl.when(step == 0)
    def _():
        sums[...] = piece

    @pl.when(step > 0)
    def _():
        sums[...] += piece

    @pl.when(step == pl.num_programs(0) - 1)
    def _():
        rest = q0[...] + q1[...] + q2[...]
        total = jnp.sum(sums[...], 1, keepdims=True) + jnp.sum(rest, 1, keepdims=True)
        square[...] = jnp.broadcast_to(total, square.shape)


def weight_grad(at, keep_l, send_l, rights, squares):
    rows, ff = rights[0].shape
    width = 512
    return call(
        weight_kernel,
        ff // width,
        [whole((D // 2, 2 * rows))] * 2 + [columns(rows, width)] * 2 + [whole((1, ff))] * 3,
        [columns(D // 2, width)] * 2 + [whole((1, 128))],
        [shaped((D // 2, ff))] * 2 + [shaped((1, 128), F32)],
        [pltpu.VMEM((1, width), F32)],
        cost(4 * rows * D * ff, 11 * 10**6),
        "weight_grad",
    )(at, keep_l, send_l, *rights, *squares)


def scaled(kept, got, u0, u1):
    return kept[...].astype(F32) * u0[0:1, 0:1] + got[...].astype(F32) * u1[0:1, 0:1]


def spread_kernel(at, u0, u1, k1, k2, k3, k4, g1, g2, g3, g4, far1, far2, behind1, ahead2):
    far1[0] = scaled(k1, g1, u0, u1).astype(BF)
    far2[0] = scaled(k2, g2, u0, u1).astype(BF)
    behind1[0] = scaled(k3, g3, u0, u1).astype(BF)
    ahead2[0] = scaled(k4, g4, u0, u1).astype(BF)


def own_kernel(at, u0, u1, k1, k2, g1, g2, own):
    own[0, 0] = scaled(k1, g1, u0, u1)
    own[0, 1] = scaled(k2, g2, u0, u1)


def relay_kernel(at, u0, u1, k1, k2, g1, g2, up, down, ahead1, behind2):
    ahead1[0] = (scaled(k1, g1, u0, u1) + up[0].astype(F32)).astype(BF)
    behind2[0] = (scaled(k2, g2, u0, u1) + down[0].astype(F32)).astype(BF)


def close_kernel(at, own, up1, down1, up2, down2, out):
    out[0, 0] = (own[0, 0] + up1[0].astype(F32) + down1[0].astype(F32)).astype(BF)
    out[0, 1] = (own[0, 1] + up2[0].astype(F32) + down2[0].astype(F32)).astype(BF)


def ring_stage(at, u0, u1, first, second, move):
    ff = first[0].shape[1]
    block = lambda k: pl.BlockSpec((48, ff), lambda s, a: (a[12 + k] + s * a[5], 0))
    one = pl.BlockSpec((1, 48, ff), lambda s, *_: (s, 0, 0))
    both = pl.BlockSpec((1, 2, 48, ff), lambda s, *_: (s, 0, 0, 0))
    single = shaped((RING, 48, ff))
    unit = [whole((1, 128))] * 2
    size = RING * 48 * ff
    order = [block(2), block(2), block(3), block(1)]
    far1, far2, behind1, ahead2 = call(
        spread_kernel,
        RING,
        unit + order * 2,
        [one] * 4,
        [single] * 4,
        [],
        cost(12 * size, 24 * size),
        "spread",
    )(
        at, u0, u1, first[0], second[0], first[0], second[0],
        first[1], second[1], first[1], second[1],
    )
    far1, far2 = move(far1, 1), move(far2, -1)
    up2, down1 = move(ahead2, 1), move(behind1, -1)
    own = call(
        own_kernel,
        RING,
        unit + [block(0)] * 4,
        both,
        shaped((RING, 2, 48, ff), F32),
        [],
        cost(6 * size, 16 * size),
        "own",
    )(at, u0, u1, first[0], second[0], first[1], second[1])
    own, far1, far2 = lax.optimization_barrier((own, far1, far2))
    ahead1, behind2 = call(
        relay_kernel,
        RING,
        unit + [block(1), block(3)] * 2 + [one, one],
        [one, one],
        [single] * 2,
        [],
        cost(8 * size, 16 * size),
        "relay",
    )(at, u0, u1, first[0], second[0], first[1], second[1], far1, far2)
    up1, down2 = move(ahead1, 1), move(behind2, -1)
    return call(
        close_kernel,
        RING,
        [both] + [one] * 4,
        both,
        shaped((RING, 2, 48, ff)),
        [],
        cost(4 * size, 20 * size),
        "close",
    )(at, own, up1, down1, up2, down2)


def local(
    latents,
    targets,
    tok_count,
    caption_states,
    cap_len,
    owner,
    ctx_w,
    mod_w,
    in_w,
    out_w,
    noise_in,
    noise_out,
):
    rows = latents.shape[0]
    token_span = rows // DRAWS
    me_x = lax.axis_index("mp")
    me_dp = lax.axis_index("dp")
    me_y, me_z, me_c = me_dp // 8, (me_dp // 2) % 4, me_dp % 2
    way = 1 - 2 * me_c

    ahead = [(me_x + k * way) % RING for k in range(RING)]
    swapped = [me_x, me_x ^ 1, me_x ^ 2, me_x ^ 3]
    me_one = jnp.where(me_c == 0, me_y, me_z)
    stride = jnp.where(me_c == 0, 4, 1)
    at = jnp.stack(
        [b * PART for b in swapped]
        + [me_c * 48, jnp.where(me_c == 0, 1, 4), me_c * 0, me_c * 0]
        + ahead
        + [((me_one + k) % RING) * stride for k in range(RING)]
    ).astype(jnp.int32)
    outs = [lax.dynamic_slice_in_dim(out_w, b * PART, PART, 0) for b in ahead]

    positions = jnp.arange(caption_states.shape[1])
    keep_mask = (positions[None, :] < cap_len[:, None]).astype(BF)
    summed = jnp.einsum("ec,ecf->ef", keep_mask, caption_states, preferred_element_type=F32)
    pooled = (summed / cap_len[:, None].astype(F32)).astype(BF).astype(F32)
    everywhere = jnp.broadcast_to(pooled.reshape(1, 8, -1), (32, 8, pooled.shape[1] // 8))
    received = lax.all_to_all(everywhere, "dp", 0, 0, tiled=True)

    behind, next_ahead = by_x(latents, 1), by_x(latents, -1)
    half = rows // 2
    received, behind, next_ahead, at, outs = lax.optimization_barrier(
        (received, behind, next_ahead, at, outs)
    )
    far = by_x(behind, 1)
    wanted = (owner == me_dp)[:, None, None]
    mine = jnp.sum(jnp.where(wanted, received, 0.0), 0).reshape(1, -1).astype(BF)

    context = dot(mine, ctx_w)
    context = context + swap_x(context, 0)
    swapped_context, far = lax.optimization_barrier((swap_x(context, 1), far))
    context = context + swapped_context
    conditioning = context * lax.rsqrt(jnp.mean(context * context, 1, keepdims=True) + 1e-06)
    chosen = jax.nn.silu(conditioning).astype(BF)
    modulation = jnp.einsum("ed,dkf->ekf", chosen, mod_w, preferred_element_type=F32)[0]
    gate = modulation[2:3]
    own_mods = modulation
    pair_mods = swap_x(own_mods, 0)
    far_mods = swap_x(jnp.concatenate([own_mods, pair_mods], 0), 1)
    mods = (own_mods, pair_mods, far_mods)

    count = tok_count[0]
    factor = 2.0 / (D * DRAWS * count.astype(F32))

    def slope_of(pre):
        square = pre * pre
        bent = jnp.tanh(pre * (C1 + (C1 * C2) * square))
        half = 0.5 * (1.0 + bent)
        return half + (0.5 * pre) * (1.0 - bent * bent) * (C1 + (3.0 * C1 * C2) * square)

    def project(hidden, j):
        return lax.dot_general(
            hidden, outs[j], (((1,), (1,)), ((), ())), preferred_element_type=F32
        )

    def leave(k, own, up, down):
        at_rows = slice(k * half, (k + 1) * half)
        output = latents[at_rows].astype(F32) + gate * (
            own + up.astype(F32) + down.astype(F32)
        )
        live = (jnp.arange(k * half, (k + 1) * half) % token_span < count).astype(F32)[:, None]
        delta = (output - targets[at_rows].astype(F32)) * live * factor
        return (gate * delta).astype(BF)

    latent_blocks = (latents, next_ahead, far, behind)
    modded0, hidden0, pre0 = forward(0, at, latent_blocks, mods, in_w)
    far0, down0 = project(hidden0, 2).astype(BF), project(hidden0, 3).astype(BF)
    far0 = by_x(far0, 1)
    at_next, down0 = lax.optimization_barrier((at, down0))
    down0 = by_x(down0, -1)
    up0 = lax.optimization_barrier(project(hidden0, 1))
    modded1, hidden1, pre1 = forward(1, at_next, latent_blocks, mods, in_w)
    hidden1, far0, down0 = lax.optimization_barrier((hidden1, far0, down0))
    up0 = (up0 + far0.astype(F32)).astype(BF)
    up0, hidden1 = lax.optimization_barrier((up0, hidden1))
    up0 = by_x(up0, 1)
    far1, up1 = project(hidden1, 2).astype(BF), project(hidden1, 1).astype(BF)
    far1, up1, hidden0_late, at_late, pre0, pre1 = lax.optimization_barrier(
        (far1, up1, hidden0, at, pre0, pre1)
    )
    own0 = lax.optimization_barrier(project(hidden0_late, 0))
    far1, up1 = by_x(far1, -1), by_x(up1, 1)
    back0 = leave(0, own0, up0, down0)
    hidden1_late, back0 = lax.optimization_barrier((hidden1, back0))
    down1, own1 = lax.optimization_barrier(
        (project(hidden1_late, 3), project(hidden1_late, 0))
    )
    behind0, ahead0 = by_x(back0, 1), by_x(back0, -1)
    down1 = by_x((down1 + far1.astype(F32)).astype(BF), -1)
    slope0, slope1 = slope_of(pre0).astype(BF), slope_of(pre1).astype(BF)
    mod_keep, mod_send = turn(at_late, modded0, modded1)
    down1, slope0, slope1, mod_keep, mod_send, behind0, ahead0 = lax.optimization_barrier(
        (down1, slope0, slope1, mod_keep, mod_send, behind0, ahead0)
    )
    back1 = leave(1, own1, up1, down1)
    far0 = by_x(behind0, 1)
    behind1, ahead1 = by_x(back1, 1), by_x(back1, -1)
    rights = (hidden0, hidden1)
    *second, square_a = rows_grad(at, (0,), ((back0,), (back1,)), rights, (), ())
    partial = rows_partial(at, (ahead0, behind0), hidden0)
    ahead1, partial, square_a = lax.optimization_barrier((ahead1, partial, square_a))
    far1 = by_x(ahead1, -1)
    grad0 = backward(at, (back0, ahead0, far0, behind0), out_w, slope0)
    *second, square_b = rows_grad(
        at, (1, 3), ((ahead1, behind1),), (hidden1,), (partial,), tuple(second)
    )
    grad1 = backward(at, (back1, ahead1, far1, behind1), out_w, slope1)
    *second, square_c = rows_grad(at, (2,), ((far0,), (far1,)), rights, (), tuple(second))
    keep2, send2 = second
    got2 = by_core(send2)
    keep1, send1, square = weight_grad(
        at, mod_keep, mod_send, (grad0, grad1), (square_a, square_b, square_c)
    )
    got1 = by_core(send1)
    square = square + swap_x(square, 0)
    square = square + swap_x(square, 1)
    root = math.sqrt(2.0 * D * FF)
    unit = root / (jnp.sqrt(square) + 0.01)

    value = ring_stage(
        at, unit, by_core(unit), (keep1, got1), (keep2, got2), lambda v, w: by_turns(v, w, True)
    )
    groups = [[(y * RING + z) * 2 for z in range(RING)] for y in range(RING)]
    groups += [[(y * RING + z) * 2 + 1 for y in range(RING)] for z in range(RING)]
    got = lax.all_to_all(value, "dp", 0, 0, axis_index_groups=groups, tiled=True)
    value = jnp.sum(got.astype(F32), 0)
    return (value[0] + noise_in) / 32.0, (value[1] + noise_out) / 32.0


def solution(mesh):
    placed = (
        P("dp", "mp"),
        P("dp", "mp"),
        P("dp"),
        P("dp", None, "mp"),
        P("dp"),
        P(),
        P("mp", None),
        P(None, None, "mp"),
        P(None, "mp"),
        P(None, "mp"),
        P("dp", "mp"),
        P("dp", "mp"),
    )
    return jax.shard_map(
        local, mesh=mesh, in_specs=placed, out_specs=(P("dp", "mp"), P("dp", "mp")), check_vma=False
    )
```

```python
import math

import jax
import jax.numpy as jnp
from jax import lax
from jax.experimental import pallas as pl
from jax.experimental.pallas import tpu as pltpu
from jax.sharding import PartitionSpec as P

D = 1536
FF = 6144
DRAWS = 4
BF = jnp.bfloat16
F32 = jnp.float32
RING = 4
PART = D // RING
WIDE = 512
VMEM_LIMIT = 32 * 1024 * 1024
C1 = math.sqrt(2.0 / math.pi)
C2 = 0.044715


def dot(left, right):
    return jnp.dot(left, right, preferred_element_type=F32)


def sign(core, way):
    return way if core == 0 else -way


def by_x(value, way):
    pairs = []
    for dp in range(32):
        for x in range(RING):
            pairs.append((dp * RING + x, dp * RING + (x + sign(dp % 2, way)) % RING))
    return lax.ppermute(value, ("dp", "mp"), pairs)


def by_dp(value, target):
    pairs = []
    for y in range(RING):
        for z in range(RING):
            for c in range(2):
                ty, tz, tc = target(y, z, c)
                pairs.append(((y * RING + z) * 2 + c, ((ty % RING) * RING + tz % RING) * 2 + tc))
    return lax.ppermute(value, "dp", pairs)


def by_turns(value, way, first):
    return by_dp(
        value,
        lambda y, z, c: (y + way, z, c) if (c == 0) == first else (y, z + way, c),
    )


def by_core(value):
    return by_dp(value, lambda y, z, c: (y, z, 1 - c))


def swap_x(value, kind):
    other = [x ^ 1 for x in range(RING)] if kind == 0 else [3 - x for x in range(RING)]
    return lax.ppermute(value, "mp", list(enumerate(other)))


def params():
    return pltpu.CompilerParams(vmem_limit_bytes=VMEM_LIMIT)


def shaped(shape, dtype=BF):
    return jax.ShapeDtypeStruct(shape, dtype)


def cost(flops, size, special=0):
    return pl.CostEstimate(flops=flops, bytes_accessed=size, transcendentals=special)


def in_hbm(value):
    return pltpu.with_memory_space_constraint(value, pltpu.HBM)


def whole(shape):
    return pl.BlockSpec(shape, lambda s, *_: (0, 0))


def columns(rows, width):
    return pl.BlockSpec((rows, width), lambda s, *_: (0, s))


def call(kernel, grid, in_specs, out_specs, out_shape, scratch, estimate, name, aliases={}):
    return pl.pallas_call(
        kernel,
        grid_spec=pltpu.PrefetchScalarGridSpec(
            num_scalar_prefetch=1,
            grid=(grid,),
            in_specs=in_specs,
            out_specs=out_specs,
            scratch_shapes=scratch,
        ),
        out_shape=out_shape,
        input_output_aliases=aliases,
        compiler_params=params(),
        cost_estimate=estimate,
        name=name,
    )


def forward_kernel(at, x0, x1, x2, x3, m0, m1, m2, in_w, modded_o, hidden, pre, mods, modded):
    step = pl.program_id(0)

    @pl.when(step == 0)
    def _():
        for place, ref, row in ((0, m0, 0), (1, m1, 0), (2, m2, 0), (3, m2, 3)):
            mods[:, pl.ds(pl.multiple_of(at[place], 128), PART)] = ref[row : row + 2]
        total = 0.0
        squares = 0.0
        for ref in (x0, x1, x2, x3):
            value = ref[...].astype(F32)
            total = total + jnp.sum(value, 1, keepdims=True)
            squares = squares + jnp.sum(value * value, 1, keepdims=True)
        center = total / D
        scale = lax.rsqrt(squares / D - center * center + 1e-06)
        for k, ref in enumerate((x0, x1, x2, x3)):
            cols = pl.ds(pl.multiple_of(at[8 + k] * PART, 128), PART)
            normed = (ref[...].astype(F32) - center) * scale
            modded[:, cols] = (normed * (1.0 + mods[1:2, cols]) + mods[0:1, cols]).astype(BF)

    modded_o[...] = modded[:, pl.ds(pl.multiple_of(step * WIDE, 128), WIDE)]
    value = dot(modded[...], in_w[...])
    pre[...] = value
    bent = jnp.tanh(value * (C1 + (C1 * C2) * (value * value)))
    hidden[...] = ((0.5 * value) * (1.0 + bent)).astype(BF)


def forward(chunk, at, blocks, mods, in_w):
    rows, ff = blocks[0].shape[0] // 2, in_w.shape[1]
    piece = pl.BlockSpec((rows, PART), lambda s, *_: (chunk, 0))
    return call(
        forward_kernel,
        ff // WIDE,
        [piece] * 4
        + [whole((3, PART)), whole((3, PART)), whole((6, PART)), columns(D, WIDE)],
        [columns(rows, WIDE)] * 3,
        [shaped((rows, D)), shaped((rows, ff)), shaped((rows, ff), F32)],
        [pltpu.VMEM((2, D), F32), pltpu.VMEM((rows, D), BF)],
        cost(2 * rows * D * ff, 12 * 10**6, rows * ff),
        "forward",
    )(at, *[in_hbm(b) for b in blocks], *mods, in_hbm(in_w))


def split_rows(at, turned, keep, send):
    mine = at[4]
    for z in range(RING):
        keep[z * 48 : (z + 1) * 48] = turned[pl.ds(pl.multiple_of(z * 96 + mine, 16), 48)]
        send[z * 48 : (z + 1) * 48] = turned[pl.ds(pl.multiple_of(z * 96 + 48 - mine, 16), 48)]


def turn_kernel(at, top, low, keep, send, turned):
    turned[:, : top.shape[0]] = top[...].T
    turned[:, top.shape[0] :] = low[...].T
    split_rows(at, turned, keep, send)


def turn(at, top, low):
    rows = top.shape[0]
    out = pl.BlockSpec((PART // 2, 2 * rows), lambda s, *_: (s, 0))
    return call(
        turn_kernel,
        RING,
        [columns(rows, PART)] * 2,
        [out, out],
        [shaped((D // 2, 2 * rows))] * 2,
        [pltpu.VMEM((PART, 2 * rows), BF)],
        cost(2 * rows * D, 8 * rows * D),
        "turn",
    )(at, top, low)


def backward_kernel(at, b0, b1, b2, b3, out_w, slope, grad, back):
    @pl.when(pl.program_id(0) == 0)
    def _():
        for k, ref in enumerate((b0, b1, b2, b3)):
            back[:, pl.ds(pl.multiple_of(at[8 + k] * PART, 128), PART)] = ref[...]

    grad[...] = (dot(back[...], out_w[...]) * slope[...].astype(F32)).astype(BF)


def backward(at, blocks, out_w, slope):
    rows, ff = slope.shape
    return call(
        backward_kernel,
        ff // WIDE,
        [whole((rows, PART))] * 4 + [columns(D, WIDE), columns(rows, WIDE)],
        columns(rows, WIDE),
        shaped((rows, ff)),
        [pltpu.VMEM((rows, D), BF)],
        cost(2 * rows * D * ff, 14 * 10**6),
        "backward",
    )(at, *blocks, out_w, slope)


def turn_blocks(groups, turned):
    for k in range(len(groups[0])):

        @pl.when(pl.program_id(0) == k)
        def _():
            start = 0
            for group in groups:
                rows = group[k].shape[0]
                turned[:, start : start + rows] = group[k][...].T
                start += rows


def cut_refs(refs, count, groups):
    return [refs[g * count : (g + 1) * count] for g in range(groups)], refs[groups * count :]


def product(turned, rights, cols):
    start = 0
    value = 0.0
    for right in rights:
        rows = right.shape[0]
        value = value + dot(turned[:, start : start + rows], right[:, cols])
        start += rows
    return value


def partial_kernel(count, at, *refs):
    groups, (right, out, turned) = cut_refs(refs, count, 1)
    turn_blocks(groups, turned)
    for n in range(right.shape[1] // 512):
        cols = slice(n * 512, (n + 1) * 512)
        out[:, cols] = product(turned, [right], cols)


def rows_partial(at, blocks, right):
    rows, ff = right.shape
    count = len(blocks)
    return call(
        lambda *refs: partial_kernel(count, *refs),
        count,
        [whole((rows, PART))] * count + [whole((rows, ff))],
        pl.BlockSpec((PART, ff), lambda s, *_: (s, 0)),
        shaped((count * PART, ff), F32),
        [pltpu.VMEM((PART, rows), BF)],
        cost(2 * rows * PART * ff * count, 4 * 10**6 * count),
        "rows_partial",
    )(at, *blocks, right)


def rows_kernel(count, parts, partials, at, *refs):
    groups, rest = cut_refs(refs, count, parts)
    rights, rest = rest[:parts], rest[parts:]
    keep, send, square, turned = refs[-4:]
    turn_blocks(groups, turned)
    mine = at[4]
    for n in range(rights[0].shape[1] // 512):
        cols = slice(n * 512, (n + 1) * 512)
        value = product(turned, rights, cols)
        if partials:
            value = value + rest[0][:, cols]
        piece = jnp.sum(value * value, 0, keepdims=True)

        @pl.when(pl.program_id(0) == 0)
        def _():
            square[:, cols] = piece

        @pl.when(pl.program_id(0) > 0)
        def _():
            square[:, cols] += piece

        for z in range(RING):
            low = value[z * 96 : z * 96 + 48].astype(BF)
            high = value[z * 96 + 48 : (z + 1) * 96].astype(BF)
            at_rows = slice(z * 48, (z + 1) * 48)
            keep[at_rows, cols] = jnp.where(mine == 0, low, high)
            send[at_rows, cols] = jnp.where(mine == 0, high, low)


def rows_grad(at, place, groups, rights, partials, before):
    ff = rights[0].shape[1]
    rows = sum(right.shape[0] for right in rights)
    count, parts = 1, len(groups)
    out = pl.BlockSpec((PART // 2, ff), lambda s, a: (a[8 + place], 0))
    offset = place // 2
    blocks = [block for group in groups for block in group]
    operands = [*blocks, *rights, *partials, *before]
    return call(
        lambda *refs: rows_kernel(count, parts, len(partials), *refs),
        count,
        [whole(value.shape) for value in (*blocks, *rights)]
        + [pl.BlockSpec((PART, ff), lambda s, *_: (offset, 0))] * len(partials)
        + [pl.BlockSpec(memory_space=pl.ANY)] * len(before),
        [out, out, whole((1, ff))],
        [shaped((D // 2, ff))] * 2 + [shaped((1, ff), F32)],
        [pltpu.VMEM((PART, rows), BF)],
        cost(2 * rows * PART * ff * count, 5 * 10**6 * count),
        "rows_grad",
        {len(operands) - len(before) + 1 + n: n for n in range(len(before))},
    )(at, *operands)


def weight_kernel(at, keep_l, send_l, right0, right1, q0, q1, q2, q3, keep, send, square, sums):
    rows = right0.shape[0]
    keep_v = dot(keep_l[:, :rows], right0[...]) + dot(keep_l[:, rows:], right1[...])
    send_v = dot(send_l[:, :rows], right0[...]) + dot(send_l[:, rows:], right1[...])
    keep[...] = keep_v.astype(BF)
    send[...] = send_v.astype(BF)
    piece = jnp.sum(keep_v * keep_v, 0, keepdims=True) + jnp.sum(send_v * send_v, 0, keepdims=True)
    step = pl.program_id(0)

    @pl.when(step == 0)
    def _():
        sums[...] = piece

    @pl.when(step > 0)
    def _():
        sums[...] += piece

    @pl.when(step == pl.num_programs(0) - 1)
    def _():
        rest = q0[...] + q1[...] + q2[...] + q3[...]
        total = jnp.sum(sums[...], 1, keepdims=True) + jnp.sum(rest, 1, keepdims=True)
        square[...] = jnp.broadcast_to(total, square.shape)


def weight_grad(at, keep_l, send_l, rights, squares):
    rows, ff = rights[0].shape
    width = 512
    return call(
        weight_kernel,
        ff // width,
        [whole((D // 2, 2 * rows))] * 2 + [columns(rows, width)] * 2 + [whole((1, ff))] * 4,
        [columns(D // 2, width)] * 2 + [whole((1, 128))],
        [shaped((D // 2, ff))] * 2 + [shaped((1, 128), F32)],
        [pltpu.VMEM((1, width), F32)],
        cost(4 * rows * D * ff, 11 * 10**6),
        "weight_grad",
    )(at, keep_l, send_l, *rights, *squares)


def scaled(kept, got, u0, u1):
    return kept[...].astype(F32) * u0[0:1, 0:1] + got[...].astype(F32) * u1[0:1, 0:1]


def spread_kernel(at, u0, u1, k1, k2, k3, k4, g1, g2, g3, g4, far1, far2, behind1, ahead2):
    far1[0] = scaled(k1, g1, u0, u1).astype(BF)
    far2[0] = scaled(k2, g2, u0, u1).astype(BF)
    behind1[0] = scaled(k3, g3, u0, u1).astype(BF)
    ahead2[0] = scaled(k4, g4, u0, u1).astype(BF)


def own_kernel(at, u0, u1, k1, k2, g1, g2, own):
    own[0, 0] = scaled(k1, g1, u0, u1)
    own[0, 1] = scaled(k2, g2, u0, u1)


def relay_kernel(at, u0, u1, k1, k2, g1, g2, up, down, ahead1, behind2):
    ahead1[0] = (scaled(k1, g1, u0, u1) + up[0].astype(F32)).astype(BF)
    behind2[0] = (scaled(k2, g2, u0, u1) + down[0].astype(F32)).astype(BF)


def close_kernel(at, own, up1, down1, up2, down2, out):
    out[0, 0] = (own[0, 0] + up1[0].astype(F32) + down1[0].astype(F32)).astype(BF)
    out[0, 1] = (own[0, 1] + up2[0].astype(F32) + down2[0].astype(F32)).astype(BF)


def ring_stage(at, u0, u1, first, second, move):
    ff = first[0].shape[1]
    block = lambda k: pl.BlockSpec((48, ff), lambda s, a: (a[12 + k] + s * a[5], 0))
    one = pl.BlockSpec((1, 48, ff), lambda s, *_: (s, 0, 0))
    both = pl.BlockSpec((1, 2, 48, ff), lambda s, *_: (s, 0, 0, 0))
    single = shaped((RING, 48, ff))
    unit = [whole((1, 128))] * 2
    size = RING * 48 * ff
    order = [block(2), block(2), block(3), block(1)]
    far1, far2, behind1, ahead2 = call(
        spread_kernel,
        RING,
        unit + order * 2,
        [one] * 4,
        [single] * 4,
        [],
        cost(12 * size, 24 * size),
        "spread",
    )(
        at, u0, u1, first[0], second[0], first[0], second[0],
        first[1], second[1], first[1], second[1],
    )
    far1, far2 = move(far1, 1), move(far2, -1)
    up2, down1 = move(ahead2, 1), move(behind1, -1)
    own = call(
        own_kernel,
        RING,
        unit + [block(0)] * 4,
        both,
        shaped((RING, 2, 48, ff), F32),
        [],
        cost(6 * size, 16 * size),
        "own",
    )(at, u0, u1, first[0], second[0], first[1], second[1])
    own, far1, far2 = lax.optimization_barrier((own, far1, far2))
    ahead1, behind2 = call(
        relay_kernel,
        RING,
        unit + [block(1), block(3)] * 2 + [one, one],
        [one, one],
        [single] * 2,
        [],
        cost(8 * size, 16 * size),
        "relay",
    )(at, u0, u1, first[0], second[0], first[1], second[1], far1, far2)
    up1, down2 = move(ahead1, 1), move(behind2, -1)
    return call(
        close_kernel,
        RING,
        [both] + [one] * 4,
        both,
        shaped((RING, 2, 48, ff)),
        [],
        cost(4 * size, 20 * size),
        "close",
    )(at, own, up1, down1, up2, down2)


def local(
    latents,
    targets,
    tok_count,
    caption_states,
    cap_len,
    owner,
    ctx_w,
    mod_w,
    in_w,
    out_w,
    noise_in,
    noise_out,
):
    rows = latents.shape[0]
    token_span = rows // DRAWS
    me_x = lax.axis_index("mp")
    me_dp = lax.axis_index("dp")
    me_y, me_z, me_c = me_dp // 8, (me_dp // 2) % 4, me_dp % 2
    way = 1 - 2 * me_c

    ahead = [(me_x + k * way) % RING for k in range(RING)]
    swapped = [me_x, me_x ^ 1, 3 - me_x, (3 - me_x) ^ 1]
    me_one = jnp.where(me_c == 0, me_y, me_z)
    stride = jnp.where(me_c == 0, 4, 1)
    at = jnp.stack(
        [b * PART for b in swapped]
        + [me_c * 48, jnp.where(me_c == 0, 1, 4), me_c * 0, me_c * 0]
        + ahead
        + [((me_one + k) % RING) * stride for k in range(RING)]
    ).astype(jnp.int32)
    outs = [lax.dynamic_slice_in_dim(out_w, b * PART, PART, 0) for b in ahead]

    positions = jnp.arange(caption_states.shape[1])
    keep_mask = (positions[None, :] < cap_len[:, None]).astype(BF)
    summed = jnp.einsum("ec,ecf->ef", keep_mask, caption_states, preferred_element_type=F32)
    pooled = (summed / cap_len[:, None].astype(F32)).astype(BF).astype(F32)
    everywhere = jnp.broadcast_to(pooled.reshape(1, 8, -1), (32, 8, pooled.shape[1] // 8))
    received = lax.all_to_all(everywhere, "dp", 0, 0, tiled=True)

    behind, next_ahead = by_x(latents, 1), by_x(latents, -1)
    half = rows // 2
    received, behind, next_ahead, at, outs = lax.optimization_barrier(
        (received, behind, next_ahead, at, outs)
    )
    far = by_x(behind, 1)
    wanted = (owner == me_dp)[:, None, None]
    mine = jnp.sum(jnp.where(wanted, received, 0.0), 0).reshape(1, -1).astype(BF)

    context = dot(mine, ctx_w)
    context = context + swap_x(context, 0)
    swapped_context, far = lax.optimization_barrier((swap_x(context, 1), far))
    context = context + swapped_context
    conditioning = context * lax.rsqrt(jnp.mean(context * context, 1, keepdims=True) + 1e-06)
    chosen = jax.nn.silu(conditioning).astype(BF)
    modulation = jnp.einsum("ed,dkf->ekf", chosen, mod_w, preferred_element_type=F32)[0]
    gate = modulation[2:3]
    own_mods = modulation
    pair_mods = swap_x(own_mods, 0)
    far_mods = swap_x(jnp.concatenate([own_mods, pair_mods], 0), 1)
    mods = (own_mods, pair_mods, far_mods)

    count = tok_count[0]
    factor = 2.0 / (D * DRAWS * count.astype(F32))

    def slope_of(pre):
        square = pre * pre
        bent = jnp.tanh(pre * (C1 + (C1 * C2) * square))
        half = 0.5 * (1.0 + bent)
        return half + (0.5 * pre) * (1.0 - bent * bent) * (C1 + (3.0 * C1 * C2) * square)

    def project(hidden, j):
        return lax.dot_general(
            hidden, outs[j], (((1,), (1,)), ((), ())), preferred_element_type=F32
        )

    def leave(k, own, up, down):
        at_rows = slice(k * half, (k + 1) * half)
        output = latents[at_rows].astype(F32) + gate * (
            own + up.astype(F32) + down.astype(F32)
        )
        live = (jnp.arange(k * half, (k + 1) * half) % token_span < count).astype(F32)[:, None]
        delta = (output - targets[at_rows].astype(F32)) * live * factor
        return (gate * delta).astype(BF)

    latent_blocks = (latents, next_ahead, far, behind)
    modded0, hidden0, pre0 = forward(0, at, latent_blocks, mods, in_w)
    far0, down0 = project(hidden0, 2).astype(BF), project(hidden0, 3).astype(BF)
    far0 = by_x(far0, 1)
    at_next, down0 = lax.optimization_barrier((at, down0))
    down0 = by_x(down0, -1)
    up0 = lax.optimization_barrier(project(hidden0, 1))
    modded1, hidden1, pre1 = forward(1, at_next, latent_blocks, mods, in_w)
    hidden1, far0, down0 = lax.optimization_barrier((hidden1, far0, down0))
    up0 = (up0 + far0.astype(F32)).astype(BF)
    up0, hidden1 = lax.optimization_barrier((up0, hidden1))
    up0 = by_x(up0, 1)
    far1, up1 = project(hidden1, 2).astype(BF), project(hidden1, 1).astype(BF)
    far1, up1, hidden0_late, at_late, pre0, pre1 = lax.optimization_barrier(
        (far1, up1, hidden0, at, pre0, pre1)
    )
    own0 = lax.optimization_barrier(project(hidden0_late, 0))
    far1, up1 = by_x(far1, -1), by_x(up1, 1)
    back0 = leave(0, own0, up0, down0)
    hidden1_late, back0 = lax.optimization_barrier((hidden1, back0))
    down1, own1 = lax.optimization_barrier(
        (project(hidden1_late, 3), project(hidden1_late, 0))
    )
    behind0, ahead0 = by_x(back0, 1), by_x(back0, -1)
    down1 = by_x((down1 + far1.astype(F32)).astype(BF), -1)
    slope0, slope1 = slope_of(pre0).astype(BF), slope_of(pre1).astype(BF)
    mod_keep, mod_send = turn(at_late, modded0, modded1)
    down1, slope0, slope1, mod_keep, mod_send, behind0, ahead0 = lax.optimization_barrier(
        (down1, slope0, slope1, mod_keep, mod_send, behind0, ahead0)
    )
    back1 = leave(1, own1, up1, down1)
    far0 = by_x(behind0, 1)
    ahead1 = by_x(back1, -1)
    back1_late, far0 = lax.optimization_barrier((back1, far0))
    behind1 = by_x(back1_late, 1)
    rights = (hidden0, hidden1)
    *second, square_a = rows_grad(at, 0, ((back0,), (back1,)), rights, (), ())
    partial = rows_partial(at, (ahead0, behind0), hidden0)
    ahead1, partial, square_a = lax.optimization_barrier((ahead1, partial, square_a))
    far1 = by_x(ahead1, -1)
    grad0 = backward(at, (back0, ahead0, far0, behind0), out_w, slope0)
    *second, square_b = rows_grad(at, 1, ((ahead1,),), (hidden1,), (partial,), tuple(second))
    *second, square_d = rows_grad(at, 3, ((behind1,),), (hidden1,), (partial,), tuple(second))
    grad1 = backward(at, (back1, ahead1, far1, behind1), out_w, slope1)
    *second, square_c = rows_grad(at, 2, ((far0,), (far1,)), rights, (), tuple(second))
    keep2, send2 = second
    got2 = by_core(send2)
    keep1, send1, square = weight_grad(
        at, mod_keep, mod_send, (grad0, grad1), (square_a, square_b, square_c, square_d)
    )
    got1 = by_core(send1)
    square = square + swap_x(square, 0)
    square = square + swap_x(square, 1)
    root = math.sqrt(2.0 * D * FF)
    unit = root / (jnp.sqrt(square) + 0.01)

    value = ring_stage(
        at, unit, by_core(unit), (keep1, got1), (keep2, got2), lambda v, w: by_turns(v, w, True)
    )
    groups = [[(y * RING + z) * 2 for z in range(RING)] for y in range(RING)]
    groups += [[(y * RING + z) * 2 + 1 for y in range(RING)] for z in range(RING)]
    got = lax.all_to_all(value, "dp", 0, 0, axis_index_groups=groups, tiled=True)
    value = jnp.sum(got.astype(F32), 0)
    return (value[0] + noise_in) / 32.0, (value[1] + noise_out) / 32.0


def solution(mesh):
    placed = (
        P("dp", "mp"),
        P("dp", "mp"),
        P("dp"),
        P("dp", None, "mp"),
        P("dp"),
        P(),
        P("mp", None),
        P(None, None, "mp"),
        P(None, "mp"),
        P(None, "mp"),
        P("dp", "mp"),
        P("dp", "mp"),
    )
    return jax.shard_map(
        local, mesh=mesh, in_specs=placed, out_specs=(P("dp", "mp"), P("dp", "mp")), check_vma=False
    )
```

```python
import math

import jax
import jax.numpy as jnp
from jax import lax
from jax.experimental import pallas as pl
from jax.experimental.pallas import tpu as pltpu
from jax.sharding import PartitionSpec as P

D = 1536
FF = 6144
DRAWS = 4
BF = jnp.bfloat16
F32 = jnp.float32
RING = 4
PART = D // RING
WIDE = 512
VMEM_LIMIT = 32 * 1024 * 1024
C1 = math.sqrt(2.0 / math.pi)
C2 = 0.044715


def dot(left, right):
    return jnp.dot(left, right, preferred_element_type=F32)


def sign(core, way):
    return way if core == 0 else -way


def by_x(value, way):
    pairs = []
    for dp in range(32):
        for x in range(RING):
            pairs.append((dp * RING + x, dp * RING + (x + sign(dp % 2, way)) % RING))
    return lax.ppermute(value, ("dp", "mp"), pairs)


def by_dp(value, target):
    pairs = []
    for y in range(RING):
        for z in range(RING):
            for c in range(2):
                ty, tz, tc = target(y, z, c)
                pairs.append(((y * RING + z) * 2 + c, ((ty % RING) * RING + tz % RING) * 2 + tc))
    return lax.ppermute(value, "dp", pairs)


def by_turns(value, way, first):
    return by_dp(
        value,
        lambda y, z, c: (y + way, z, c) if (c == 0) == first else (y, z + way, c),
    )


def by_core(value):
    return by_dp(value, lambda y, z, c: (y, z, 1 - c))


def swap_x(value, kind):
    other = [x ^ 1 for x in range(RING)] if kind == 0 else [3 - x for x in range(RING)]
    return lax.ppermute(value, "mp", list(enumerate(other)))


def params():
    return pltpu.CompilerParams(vmem_limit_bytes=VMEM_LIMIT)


def shaped(shape, dtype=BF):
    return jax.ShapeDtypeStruct(shape, dtype)


def cost(flops, size, special=0):
    return pl.CostEstimate(flops=flops, bytes_accessed=size, transcendentals=special)


def in_hbm(value):
    return pltpu.with_memory_space_constraint(value, pltpu.HBM)


def whole(shape):
    return pl.BlockSpec(shape, lambda s, *_: (0, 0))


def columns(rows, width):
    return pl.BlockSpec((rows, width), lambda s, *_: (0, s))


def call(kernel, grid, in_specs, out_specs, out_shape, scratch, estimate, name, aliases={}):
    return pl.pallas_call(
        kernel,
        grid_spec=pltpu.PrefetchScalarGridSpec(
            num_scalar_prefetch=1,
            grid=(grid,),
            in_specs=in_specs,
            out_specs=out_specs,
            scratch_shapes=scratch,
        ),
        out_shape=out_shape,
        input_output_aliases=aliases,
        compiler_params=params(),
        cost_estimate=estimate,
        name=name,
    )


def statistics_kernel(at, x0, x1, x2, x3, center_o, scale_o):
    total = 0.0
    squares = 0.0
    for ref in (x0, x1, x2, x3):
        value = ref[...].astype(F32)
        total = total + jnp.sum(value, 1, keepdims=True)
        squares = squares + jnp.sum(value * value, 1, keepdims=True)
    center = total / D
    scale = lax.rsqrt(squares / D - center * center + 1e-06)
    center_o[...] = jnp.broadcast_to(center, center_o.shape)
    scale_o[...] = jnp.broadcast_to(scale, scale_o.shape)


def statistics(chunk, at, blocks):
    rows = blocks[0].shape[0] // 2
    steps = 2
    out = pl.BlockSpec((rows // steps, 128), lambda s, *_: (s, 0))
    return call(
        statistics_kernel,
        steps,
        [pl.BlockSpec((rows // steps, PART), lambda s, *_: (chunk * steps + s, 0))] * 4,
        [out] * 2,
        [shaped((rows, 128), F32)] * 2,
        [],
        cost(4 * rows * D, 3 * rows * D),
        "statistics",
    )(at, *[in_hbm(b) for b in blocks])


def forward_kernel(
    at, x0, x1, x2, x3, center, scale, m0, m1, m2, in_w, modded_o, hidden, pre, mods, modded
):
    step = pl.program_id(0)

    @pl.when(step == 0)
    def _():
        for place, ref, row in ((0, m0, 0), (1, m1, 0), (2, m2, 0), (3, m2, 3)):
            mods[:, pl.ds(pl.multiple_of(at[place], 128), PART)] = ref[row : row + 2]
        for k, ref in enumerate((x0, x1, x2, x3)):
            cols = pl.ds(pl.multiple_of(at[8 + k] * PART, 128), PART)
            normed = (ref[...].astype(F32) - center[:, 0:1]) * scale[:, 0:1]
            modded[:, cols] = (normed * (1.0 + mods[1:2, cols]) + mods[0:1, cols]).astype(BF)

    modded_o[...] = modded[:, pl.ds(pl.multiple_of(step * WIDE, 128), WIDE)]
    value = dot(modded[...], in_w[...])
    pre[...] = value
    bent = jnp.tanh(value * (C1 + (C1 * C2) * (value * value)))
    hidden[...] = ((0.5 * value) * (1.0 + bent)).astype(BF)


def forward(chunk, at, blocks, stats, mods, in_w):
    rows, ff = blocks[0].shape[0] // 2, in_w.shape[1]
    piece = pl.BlockSpec((rows, PART), lambda s, *_: (chunk, 0))
    return call(
        forward_kernel,
        ff // WIDE,
        [piece] * 4
        + [whole((rows, 128))] * 2
        + [whole((3, PART)), whole((3, PART)), whole((6, PART)), columns(D, WIDE)],
        [columns(rows, WIDE)] * 3,
        [shaped((rows, D)), shaped((rows, ff)), shaped((rows, ff), F32)],
        [pltpu.VMEM((2, D), F32), pltpu.VMEM((rows, D), BF)],
        cost(2 * rows * D * ff, 12 * 10**6, rows * ff),
        "forward",
    )(at, *[in_hbm(b) for b in blocks], *stats, *mods, in_hbm(in_w))


def split_rows(at, turned, keep, send):
    mine = at[4]
    for z in range(RING):
        keep[z * 48 : (z + 1) * 48] = turned[pl.ds(pl.multiple_of(z * 96 + mine, 16), 48)]
        send[z * 48 : (z + 1) * 48] = turned[pl.ds(pl.multiple_of(z * 96 + 48 - mine, 16), 48)]


def turn_kernel(at, top, low, keep, send, turned):
    turned[:, : top.shape[0]] = top[...].T
    turned[:, top.shape[0] :] = low[...].T
    split_rows(at, turned, keep, send)


def turn(at, top, low):
    rows = top.shape[0]
    out = pl.BlockSpec((PART // 2, 2 * rows), lambda s, *_: (s, 0))
    return call(
        turn_kernel,
        RING,
        [columns(rows, PART)] * 2,
        [out, out],
        [shaped((D // 2, 2 * rows))] * 2,
        [pltpu.VMEM((PART, 2 * rows), BF)],
        cost(2 * rows * D, 8 * rows * D),
        "turn",
    )(at, top, low)


def backward_kernel(at, b0, b1, b2, b3, out_w, slope, grad, back):
    @pl.when(pl.program_id(0) == 0)
    def _():
        for k, ref in enumerate((b0, b1, b2, b3)):
            back[:, pl.ds(pl.multiple_of(at[8 + k] * PART, 128), PART)] = ref[...]

    grad[...] = (dot(back[...], out_w[...]) * slope[...].astype(F32)).astype(BF)


def backward(at, blocks, out_w, slope):
    rows, ff = slope.shape
    return call(
        backward_kernel,
        ff // WIDE,
        [whole((rows, PART))] * 4 + [columns(D, WIDE), columns(rows, WIDE)],
        columns(rows, WIDE),
        shaped((rows, ff)),
        [pltpu.VMEM((rows, D), BF)],
        cost(2 * rows * D * ff, 14 * 10**6),
        "backward",
    )(at, *blocks, out_w, slope)


def turn_blocks(groups, turned):
    for k in range(len(groups[0])):

        @pl.when(pl.program_id(0) == k)
        def _():
            start = 0
            for group in groups:
                rows = group[k].shape[0]
                turned[:, start : start + rows] = group[k][...].T
                start += rows


def cut_refs(refs, count, groups):
    return [refs[g * count : (g + 1) * count] for g in range(groups)], refs[groups * count :]


def product(turned, rights, cols):
    start = 0
    value = 0.0
    for right in rights:
        rows = right.shape[0]
        value = value + dot(turned[:, start : start + rows], right[:, cols])
        start += rows
    return value


def partial_kernel(count, at, *refs):
    groups, (right, out, turned) = cut_refs(refs, count, 1)
    turn_blocks(groups, turned)
    for n in range(right.shape[1] // 512):
        cols = slice(n * 512, (n + 1) * 512)
        out[:, cols] = product(turned, [right], cols)


def rows_partial(at, blocks, right):
    rows, ff = right.shape
    count = len(blocks)
    return call(
        lambda *refs: partial_kernel(count, *refs),
        count,
        [whole((rows, PART))] * count + [whole((rows, ff))],
        pl.BlockSpec((PART, ff), lambda s, *_: (s, 0)),
        shaped((count * PART, ff), F32),
        [pltpu.VMEM((PART, rows), BF)],
        cost(2 * rows * PART * ff * count, 4 * 10**6 * count),
        "rows_partial",
    )(at, *blocks, right)


def rows_kernel(count, parts, partials, at, *refs):
    groups, rest = cut_refs(refs, count, parts)
    rights, rest = rest[:parts], rest[parts:]
    keep, send, square, turned = refs[-4:]
    turn_blocks(groups, turned)
    mine = at[4]
    for n in range(rights[0].shape[1] // 512):
        cols = slice(n * 512, (n + 1) * 512)
        value = product(turned, rights, cols)
        if partials:
            value = value + rest[0][:, cols]
        piece = jnp.sum(value * value, 0, keepdims=True)

        @pl.when(pl.program_id(0) == 0)
        def _():
            square[:, cols] = piece

        @pl.when(pl.program_id(0) > 0)
        def _():
            square[:, cols] += piece

        for z in range(RING):
            low = value[z * 96 : z * 96 + 48].astype(BF)
            high = value[z * 96 + 48 : (z + 1) * 96].astype(BF)
            at_rows = slice(z * 48, (z + 1) * 48)
            keep[at_rows, cols] = jnp.where(mine == 0, low, high)
            send[at_rows, cols] = jnp.where(mine == 0, high, low)


def rows_grad(at, place, groups, rights, partials, before):
    ff = rights[0].shape[1]
    rows = sum(right.shape[0] for right in rights)
    count, parts = 1, len(groups)
    out = pl.BlockSpec((PART // 2, ff), lambda s, a: (a[8 + place], 0))
    offset = place // 2
    blocks = [block for group in groups for block in group]
    operands = [*blocks, *rights, *partials, *before]
    return call(
        lambda *refs: rows_kernel(count, parts, len(partials), *refs),
        count,
        [whole(value.shape) for value in (*blocks, *rights)]
        + [pl.BlockSpec((PART, ff), lambda s, *_: (offset, 0))] * len(partials)
        + [pl.BlockSpec(memory_space=pl.ANY)] * len(before),
        [out, out, whole((1, ff))],
        [shaped((D // 2, ff))] * 2 + [shaped((1, ff), F32)],
        [pltpu.VMEM((PART, rows), BF)],
        cost(2 * rows * PART * ff * count, 5 * 10**6 * count),
        "rows_grad",
        {len(operands) - len(before) + 1 + n: n for n in range(len(before))},
    )(at, *operands)


def weight_kernel(at, keep_l, send_l, right0, right1, q0, q1, q2, q3, keep, send, square, sums):
    rows = right0.shape[0]
    keep_v = dot(keep_l[:, :rows], right0[...]) + dot(keep_l[:, rows:], right1[...])
    send_v = dot(send_l[:, :rows], right0[...]) + dot(send_l[:, rows:], right1[...])
    keep[...] = keep_v.astype(BF)
    send[...] = send_v.astype(BF)
    piece = jnp.sum(keep_v * keep_v, 0, keepdims=True) + jnp.sum(send_v * send_v, 0, keepdims=True)
    step = pl.program_id(0)

    @pl.when(step == 0)
    def _():
        sums[...] = piece

    @pl.when(step > 0)
    def _():
        sums[...] += piece

    @pl.when(step == pl.num_programs(0) - 1)
    def _():
        rest = q0[...] + q1[...] + q2[...] + q3[...]
        total = jnp.sum(sums[...], 1, keepdims=True) + jnp.sum(rest, 1, keepdims=True)
        square[...] = jnp.broadcast_to(total, square.shape)


def weight_grad(at, keep_l, send_l, rights, squares):
    rows, ff = rights[0].shape
    width = 512
    return call(
        weight_kernel,
        ff // width,
        [whole((D // 2, 2 * rows))] * 2 + [columns(rows, width)] * 2 + [whole((1, ff))] * 4,
        [columns(D // 2, width)] * 2 + [whole((1, 128))],
        [shaped((D // 2, ff))] * 2 + [shaped((1, 128), F32)],
        [pltpu.VMEM((1, width), F32)],
        cost(4 * rows * D * ff, 11 * 10**6),
        "weight_grad",
    )(at, keep_l, send_l, *rights, *squares)


def scaled(kept, got, u0, u1):
    return kept[...].astype(F32) * u0[0:1, 0:1] + got[...].astype(F32) * u1[0:1, 0:1]


def spread_kernel(at, u0, u1, k1, k2, k3, k4, g1, g2, g3, g4, far1, far2, behind1, ahead2):
    far1[0] = scaled(k1, g1, u0, u1).astype(BF)
    far2[0] = scaled(k2, g2, u0, u1).astype(BF)
    behind1[0] = scaled(k3, g3, u0, u1).astype(BF)
    ahead2[0] = scaled(k4, g4, u0, u1).astype(BF)


def own_kernel(at, u0, u1, k1, k2, g1, g2, own):
    own[0, 0] = scaled(k1, g1, u0, u1)
    own[0, 1] = scaled(k2, g2, u0, u1)


def relay_kernel(at, u0, u1, k1, k2, g1, g2, up, down, ahead1, behind2):
    ahead1[0] = (scaled(k1, g1, u0, u1) + up[0].astype(F32)).astype(BF)
    behind2[0] = (scaled(k2, g2, u0, u1) + down[0].astype(F32)).astype(BF)


def close_kernel(at, own, up1, down1, up2, down2, out):
    out[0, 0] = (own[0, 0] + up1[0].astype(F32) + down1[0].astype(F32)).astype(BF)
    out[0, 1] = (own[0, 1] + up2[0].astype(F32) + down2[0].astype(F32)).astype(BF)


def ring_stage(at, u0, u1, first, second, move):
    ff = first[0].shape[1]
    block = lambda k: pl.BlockSpec((48, ff), lambda s, a: (a[12 + k] + s * a[5], 0))
    one = pl.BlockSpec((1, 48, ff), lambda s, *_: (s, 0, 0))
    both = pl.BlockSpec((1, 2, 48, ff), lambda s, *_: (s, 0, 0, 0))
    single = shaped((RING, 48, ff))
    unit = [whole((1, 128))] * 2
    size = RING * 48 * ff
    order = [block(2), block(2), block(3), block(1)]
    far1, far2, behind1, ahead2 = call(
        spread_kernel,
        RING,
        unit + order * 2,
        [one] * 4,
        [single] * 4,
        [],
        cost(12 * size, 24 * size),
        "spread",
    )(
        at, u0, u1, first[0], second[0], first[0], second[0],
        first[1], second[1], first[1], second[1],
    )
    far1, far2 = move(far1, 1), move(far2, -1)
    up2, down1 = move(ahead2, 1), move(behind1, -1)
    own = call(
        own_kernel,
        RING,
        unit + [block(0)] * 4,
        both,
        shaped((RING, 2, 48, ff), F32),
        [],
        cost(6 * size, 16 * size),
        "own",
    )(at, u0, u1, first[0], second[0], first[1], second[1])
    own, far1, far2 = lax.optimization_barrier((own, far1, far2))
    ahead1, behind2 = call(
        relay_kernel,
        RING,
        unit + [block(1), block(3)] * 2 + [one, one],
        [one, one],
        [single] * 2,
        [],
        cost(8 * size, 16 * size),
        "relay",
    )(at, u0, u1, first[0], second[0], first[1], second[1], far1, far2)
    up1, down2 = move(ahead1, 1), move(behind2, -1)
    return call(
        close_kernel,
        RING,
        [both] + [one] * 4,
        both,
        shaped((RING, 2, 48, ff)),
        [],
        cost(4 * size, 20 * size),
        "close",
    )(at, own, up1, down1, up2, down2)


def local(
    latents,
    targets,
    tok_count,
    caption_states,
    cap_len,
    owner,
    ctx_w,
    mod_w,
    in_w,
    out_w,
    noise_in,
    noise_out,
):
    rows = latents.shape[0]
    token_span = rows // DRAWS
    me_x = lax.axis_index("mp")
    me_dp = lax.axis_index("dp")
    me_y, me_z, me_c = me_dp // 8, (me_dp // 2) % 4, me_dp % 2
    way = 1 - 2 * me_c

    ahead = [(me_x + k * way) % RING for k in range(RING)]
    swapped = [me_x, me_x ^ 1, 3 - me_x, (3 - me_x) ^ 1]
    me_one = jnp.where(me_c == 0, me_y, me_z)
    stride = jnp.where(me_c == 0, 4, 1)
    at = jnp.stack(
        [b * PART for b in swapped]
        + [me_c * 48, jnp.where(me_c == 0, 1, 4), me_c * 0, me_c * 0]
        + ahead
        + [((me_one + k) % RING) * stride for k in range(RING)]
    ).astype(jnp.int32)
    outs = [lax.dynamic_slice_in_dim(out_w, b * PART, PART, 0) for b in ahead]

    positions = jnp.arange(caption_states.shape[1])
    keep_mask = (positions[None, :] < cap_len[:, None]).astype(BF)
    summed = jnp.einsum("ec,ecf->ef", keep_mask, caption_states, preferred_element_type=F32)
    pooled = (summed / cap_len[:, None].astype(F32)).astype(BF).astype(F32)
    everywhere = jnp.broadcast_to(pooled.reshape(1, 8, -1), (32, 8, pooled.shape[1] // 8))
    received = lax.all_to_all(everywhere, "dp", 0, 0, tiled=True)

    behind, next_ahead = by_x(latents, 1), by_x(latents, -1)
    half = rows // 2
    received, behind, next_ahead, at, outs = lax.optimization_barrier(
        (received, behind, next_ahead, at, outs)
    )
    far = by_x(behind, 1)
    wanted = (owner == me_dp)[:, None, None]
    mine = jnp.sum(jnp.where(wanted, received, 0.0), 0).reshape(1, -1).astype(BF)

    context = dot(mine, ctx_w)
    context = context + swap_x(context, 0)
    swapped_context, far = lax.optimization_barrier((swap_x(context, 1), far))
    context = context + swapped_context
    conditioning = context * lax.rsqrt(jnp.mean(context * context, 1, keepdims=True) + 1e-06)
    chosen = jax.nn.silu(conditioning).astype(BF)
    modulation = jnp.einsum("ed,dkf->ekf", chosen, mod_w, preferred_element_type=F32)[0]
    gate = modulation[2:3]
    own_mods = modulation
    latent_blocks = (latents, next_ahead, far, behind)
    pair_mods, *stats0 = lax.optimization_barrier(
        (swap_x(own_mods, 0), *statistics(0, at, latent_blocks))
    )
    far_mods = swap_x(jnp.concatenate([own_mods, pair_mods], 0), 1)
    far_mods, *stats1 = lax.optimization_barrier(
        (far_mods, *statistics(1, at, latent_blocks))
    )
    mods = (own_mods, pair_mods, far_mods)

    count = tok_count[0]
    factor = 2.0 / (D * DRAWS * count.astype(F32))

    def slope_of(pre):
        square = pre * pre
        bent = jnp.tanh(pre * (C1 + (C1 * C2) * square))
        half = 0.5 * (1.0 + bent)
        return half + (0.5 * pre) * (1.0 - bent * bent) * (C1 + (3.0 * C1 * C2) * square)

    def project(hidden, j):
        return lax.dot_general(
            hidden, outs[j], (((1,), (1,)), ((), ())), preferred_element_type=F32
        )

    def leave(k, own, up, down):
        at_rows = slice(k * half, (k + 1) * half)
        output = latents[at_rows].astype(F32) + gate * (
            own + up.astype(F32) + down.astype(F32)
        )
        live = (jnp.arange(k * half, (k + 1) * half) % token_span < count).astype(F32)[:, None]
        delta = (output - targets[at_rows].astype(F32)) * live * factor
        return (gate * delta).astype(BF)

    modded0, hidden0, pre0 = forward(0, at, latent_blocks, stats0, mods, in_w)
    far0, down0 = project(hidden0, 2).astype(BF), project(hidden0, 3).astype(BF)
    far0 = by_x(far0, 1)
    at_next, down0 = lax.optimization_barrier((at, down0))
    down0 = by_x(down0, -1)
    up0 = lax.optimization_barrier(project(hidden0, 1))
    modded1, hidden1, pre1 = forward(1, at_next, latent_blocks, stats1, mods, in_w)
    hidden1, far0, down0 = lax.optimization_barrier((hidden1, far0, down0))
    up0 = (up0 + far0.astype(F32)).astype(BF)
    up0, hidden1 = lax.optimization_barrier((up0, hidden1))
    up0 = by_x(up0, 1)
    far1, up1 = project(hidden1, 2).astype(BF), project(hidden1, 1).astype(BF)
    far1, up1, hidden0_late, at_late, pre0, pre1 = lax.optimization_barrier(
        (far1, up1, hidden0, at, pre0, pre1)
    )
    own0 = lax.optimization_barrier(project(hidden0_late, 0))
    far1, up1 = by_x(far1, -1), by_x(up1, 1)
    back0 = leave(0, own0, up0, down0)
    hidden1_late, back0 = lax.optimization_barrier((hidden1, back0))
    down1, own1 = lax.optimization_barrier(
        (project(hidden1_late, 3), project(hidden1_late, 0))
    )
    behind0, ahead0 = by_x(back0, 1), by_x(back0, -1)
    down1 = by_x((down1 + far1.astype(F32)).astype(BF), -1)
    slope0, slope1 = slope_of(pre0).astype(BF), slope_of(pre1).astype(BF)
    mod_keep, mod_send = turn(at_late, modded0, modded1)
    down1, slope0, slope1, mod_keep, mod_send, behind0, ahead0 = lax.optimization_barrier(
        (down1, slope0, slope1, mod_keep, mod_send, behind0, ahead0)
    )
    back1 = leave(1, own1, up1, down1)
    far0 = by_x(behind0, 1)
    ahead1 = by_x(back1, -1)
    back1_late, far0 = lax.optimization_barrier((back1, far0))
    behind1 = by_x(back1_late, 1)
    rights = (hidden0, hidden1)
    *second, square_a = rows_grad(at, 0, ((back0,), (back1,)), rights, (), ())
    partial = rows_partial(at, (ahead0, behind0), hidden0)
    ahead1, partial, square_a = lax.optimization_barrier((ahead1, partial, square_a))
    far1 = by_x(ahead1, -1)
    grad0 = backward(at, (back0, ahead0, far0, behind0), out_w, slope0)
    *second, square_b = rows_grad(at, 1, ((ahead1,),), (hidden1,), (partial,), tuple(second))
    *second, square_d = rows_grad(at, 3, ((behind1,),), (hidden1,), (partial,), tuple(second))
    grad1 = backward(at, (back1, ahead1, far1, behind1), out_w, slope1)
    *second, square_c = rows_grad(at, 2, ((far0,), (far1,)), rights, (), tuple(second))
    keep2, send2 = second
    got2 = by_core(send2)
    keep1, send1, square = weight_grad(
        at, mod_keep, mod_send, (grad0, grad1), (square_a, square_b, square_c, square_d)
    )
    got1 = by_core(send1)
    square = square + swap_x(square, 0)
    square = square + swap_x(square, 1)
    root = math.sqrt(2.0 * D * FF)
    unit = root / (jnp.sqrt(square) + 0.01)

    value = ring_stage(
        at, unit, by_core(unit), (keep1, got1), (keep2, got2), lambda v, w: by_turns(v, w, True)
    )
    groups = [[(y * RING + z) * 2 for z in range(RING)] for y in range(RING)]
    groups += [[(y * RING + z) * 2 + 1 for y in range(RING)] for z in range(RING)]
    got = lax.all_to_all(value, "dp", 0, 0, axis_index_groups=groups, tiled=True)
    value = jnp.sum(got.astype(F32), 0)
    return (value[0] + noise_in) / 32.0, (value[1] + noise_out) / 32.0


def solution(mesh):
    placed = (
        P("dp", "mp"),
        P("dp", "mp"),
        P("dp"),
        P("dp", None, "mp"),
        P("dp"),
        P(),
        P("mp", None),
        P(None, None, "mp"),
        P(None, "mp"),
        P(None, "mp"),
        P("dp", "mp"),
        P("dp", "mp"),
    )
    return jax.shard_map(
        local, mesh=mesh, in_specs=placed, out_specs=(P("dp", "mp"), P("dp", "mp")), check_vma=False
    )
```

```python
import math

import jax
import jax.numpy as jnp
from jax import lax
from jax.experimental import pallas as pl
from jax.experimental.pallas import tpu as pltpu
from jax.sharding import PartitionSpec as P

D = 1536
FF = 6144
DRAWS = 4
BF = jnp.bfloat16
F32 = jnp.float32
RING = 4
PART = D // RING
WIDE = 512
VMEM_LIMIT = 32 * 1024 * 1024
C1 = math.sqrt(2.0 / math.pi)
C2 = 0.044715


def dot(left, right):
    return jnp.dot(left, right, preferred_element_type=F32)


def sign(core, way):
    return way if core == 0 else -way


def by_x(value, way):
    pairs = []
    for dp in range(32):
        for x in range(RING):
            pairs.append((dp * RING + x, dp * RING + (x + sign(dp % 2, way)) % RING))
    return lax.ppermute(value, ("dp", "mp"), pairs)


def by_dp(value, target):
    pairs = []
    for y in range(RING):
        for z in range(RING):
            for c in range(2):
                ty, tz, tc = target(y, z, c)
                pairs.append(((y * RING + z) * 2 + c, ((ty % RING) * RING + tz % RING) * 2 + tc))
    return lax.ppermute(value, "dp", pairs)


def by_turns(value, way, first):
    return by_dp(
        value,
        lambda y, z, c: (y + way, z, c) if (c == 0) == first else (y, z + way, c),
    )


def by_core(value):
    return by_dp(value, lambda y, z, c: (y, z, 1 - c))


def swap_x(value, kind):
    other = [x ^ 1 for x in range(RING)] if kind == 0 else [3 - x for x in range(RING)]
    return lax.ppermute(value, "mp", list(enumerate(other)))


def params():
    return pltpu.CompilerParams(vmem_limit_bytes=VMEM_LIMIT)


def shaped(shape, dtype=BF):
    return jax.ShapeDtypeStruct(shape, dtype)


def cost(flops, size, special=0):
    return pl.CostEstimate(flops=flops, bytes_accessed=size, transcendentals=special)


def in_hbm(value):
    return pltpu.with_memory_space_constraint(value, pltpu.HBM)


def whole(shape):
    return pl.BlockSpec(shape, lambda s, *_: (0, 0))


def columns(rows, width):
    return pl.BlockSpec((rows, width), lambda s, *_: (0, s))


def call(kernel, grid, in_specs, out_specs, out_shape, scratch, estimate, name, aliases={}):
    return pl.pallas_call(
        kernel,
        grid_spec=pltpu.PrefetchScalarGridSpec(
            num_scalar_prefetch=1,
            grid=(grid,),
            in_specs=in_specs,
            out_specs=out_specs,
            scratch_shapes=scratch,
        ),
        out_shape=out_shape,
        input_output_aliases=aliases,
        compiler_params=params(),
        cost_estimate=estimate,
        name=name,
    )


def forward_kernel(at, x0, x1, x2, x3, m0, m1, m2, in_w, modded_o, hidden, pre, mods, modded):
    step = pl.program_id(0)

    @pl.when(step == 0)
    def _():
        for place, ref, row in ((0, m0, 0), (1, m1, 0), (2, m2, 0), (3, m2, 3)):
            mods[:, pl.ds(pl.multiple_of(at[place], 128), PART)] = ref[row : row + 2]
        total = 0.0
        squares = 0.0
        for ref in (x0, x1, x2, x3):
            value = ref[...].astype(F32)
            total = total + jnp.sum(value, 1, keepdims=True)
            squares = squares + jnp.sum(value * value, 1, keepdims=True)
        center = total / D
        scale = lax.rsqrt(squares / D - center * center + 1e-06)
        for k, ref in enumerate((x0, x1, x2, x3)):
            cols = pl.ds(pl.multiple_of(at[8 + k] * PART, 128), PART)
            normed = (ref[...].astype(F32) - center) * scale
            modded[:, cols] = (normed * (1.0 + mods[1:2, cols]) + mods[0:1, cols]).astype(BF)

    modded_o[...] = modded[:, pl.ds(pl.multiple_of(step * WIDE, 128), WIDE)]
    value = dot(modded[...], in_w[...])
    pre[...] = value
    bent = jnp.tanh(value * (C1 + (C1 * C2) * (value * value)))
    hidden[...] = ((0.5 * value) * (1.0 + bent)).astype(BF)


def forward(chunk, at, blocks, mods, in_w):
    rows, ff = blocks[0].shape[0] // 2, in_w.shape[1]
    piece = pl.BlockSpec((rows, PART), lambda s, *_: (chunk, 0))
    return call(
        forward_kernel,
        ff // WIDE,
        [piece] * 4
        + [whole((3, PART)), whole((3, PART)), whole((6, PART)), columns(D, WIDE)],
        [columns(rows, WIDE)] * 3,
        [shaped((rows, D)), shaped((rows, ff)), shaped((rows, ff), F32)],
        [pltpu.VMEM((2, D), F32), pltpu.VMEM((rows, D), BF)],
        cost(2 * rows * D * ff, 12 * 10**6, rows * ff),
        "forward",
    )(at, *[in_hbm(b) for b in blocks], *mods, in_hbm(in_w))


def split_rows(at, turned, keep, send):
    mine = at[4]
    for z in range(RING):
        keep[z * 48 : (z + 1) * 48] = turned[pl.ds(pl.multiple_of(z * 96 + mine, 16), 48)]
        send[z * 48 : (z + 1) * 48] = turned[pl.ds(pl.multiple_of(z * 96 + 48 - mine, 16), 48)]


def turn_kernel(at, top, low, keep, send, turned):
    turned[:, : top.shape[0]] = top[...].T
    turned[:, top.shape[0] :] = low[...].T
    split_rows(at, turned, keep, send)


def turn(at, top, low):
    rows = top.shape[0]
    out = pl.BlockSpec((PART // 2, 2 * rows), lambda s, *_: (s, 0))
    return call(
        turn_kernel,
        RING,
        [columns(rows, PART)] * 2,
        [out, out],
        [shaped((D // 2, 2 * rows))] * 2,
        [pltpu.VMEM((PART, 2 * rows), BF)],
        cost(2 * rows * D, 8 * rows * D),
        "turn",
    )(at, top, low)


def backward_kernel(at, b0, b1, b2, b3, out_w, slope, grad, back):
    @pl.when(pl.program_id(0) == 0)
    def _():
        for k, ref in enumerate((b0, b1, b2, b3)):
            back[:, pl.ds(pl.multiple_of(at[8 + k] * PART, 128), PART)] = ref[...]

    grad[...] = (dot(back[...], out_w[...]) * slope[...].astype(F32)).astype(BF)


def backward(at, blocks, out_w, slope):
    rows, ff = slope.shape
    return call(
        backward_kernel,
        ff // WIDE,
        [whole((rows, PART))] * 4 + [columns(D, WIDE), columns(rows, WIDE)],
        columns(rows, WIDE),
        shaped((rows, ff)),
        [pltpu.VMEM((rows, D), BF)],
        cost(2 * rows * D * ff, 14 * 10**6),
        "backward",
    )(at, *blocks, out_w, slope)


def turn_blocks(groups, turned):
    for k in range(len(groups[0])):

        @pl.when(pl.program_id(0) == k)
        def _():
            start = 0
            for group in groups:
                rows = group[k].shape[0]
                turned[:, start : start + rows] = group[k][...].T
                start += rows


def cut_refs(refs, count, groups):
    return [refs[g * count : (g + 1) * count] for g in range(groups)], refs[groups * count :]


def product(turned, rights, cols):
    start = 0
    value = 0.0
    for right in rights:
        rows = right.shape[0]
        value = value + dot(turned[:, start : start + rows], right[:, cols])
        start += rows
    return value


def partial_kernel(count, at, *refs):
    groups, (right, out, turned) = cut_refs(refs, count, 1)
    turn_blocks(groups, turned)
    for n in range(right.shape[1] // 512):
        cols = slice(n * 512, (n + 1) * 512)
        out[:, cols] = product(turned, [right], cols)


def rows_partial(at, blocks, right):
    rows, ff = right.shape
    count = len(blocks)
    return call(
        lambda *refs: partial_kernel(count, *refs),
        count,
        [whole((rows, PART))] * count + [whole((rows, ff))],
        pl.BlockSpec((PART, ff), lambda s, *_: (s, 0)),
        shaped((count * PART, ff), F32),
        [pltpu.VMEM((PART, rows), BF)],
        cost(2 * rows * PART * ff * count, 4 * 10**6 * count),
        "rows_partial",
    )(at, *blocks, right)


def rows_kernel(count, parts, partials, at, *refs):
    groups, rest = cut_refs(refs, count, parts)
    rights, rest = rest[:parts], rest[parts:]
    keep, send, square, turned = refs[-4:]
    turn_blocks(groups, turned)
    mine = at[4]
    for n in range(rights[0].shape[1] // 512):
        cols = slice(n * 512, (n + 1) * 512)
        value = product(turned, rights, cols)
        if partials:
            value = value + rest[0][:, cols]
        piece = jnp.sum(value * value, 0, keepdims=True)

        @pl.when(pl.program_id(0) == 0)
        def _():
            square[:, cols] = piece

        @pl.when(pl.program_id(0) > 0)
        def _():
            square[:, cols] += piece

        for z in range(RING):
            low = value[z * 96 : z * 96 + 48].astype(BF)
            high = value[z * 96 + 48 : (z + 1) * 96].astype(BF)
            at_rows = slice(z * 48, (z + 1) * 48)
            keep[at_rows, cols] = jnp.where(mine == 0, low, high)
            send[at_rows, cols] = jnp.where(mine == 0, high, low)


def rows_grad(at, place, groups, rights, partials, before):
    ff = rights[0].shape[1]
    rows = sum(right.shape[0] for right in rights)
    count, parts = 1, len(groups)
    out = pl.BlockSpec((PART // 2, ff), lambda s, a: (a[8 + place], 0))
    offset = place // 2
    blocks = [block for group in groups for block in group]
    operands = [*blocks, *rights, *partials, *before]
    return call(
        lambda *refs: rows_kernel(count, parts, len(partials), *refs),
        count,
        [whole(value.shape) for value in (*blocks, *rights)]
        + [pl.BlockSpec((PART, ff), lambda s, *_: (offset, 0))] * len(partials)
        + [pl.BlockSpec(memory_space=pl.ANY)] * len(before),
        [out, out, whole((1, ff))],
        [shaped((D // 2, ff))] * 2 + [shaped((1, ff), F32)],
        [pltpu.VMEM((PART, rows), BF)],
        cost(2 * rows * PART * ff * count, 5 * 10**6 * count),
        "rows_grad",
        {len(operands) - len(before) + 1 + n: n for n in range(len(before))},
    )(at, *operands)


def weight_kernel(at, keep_l, send_l, right0, right1, q0, q1, q2, q3, keep, send, square, sums):
    rows = right0.shape[0]
    keep_v = dot(keep_l[:, :rows], right0[...]) + dot(keep_l[:, rows:], right1[...])
    send_v = dot(send_l[:, :rows], right0[...]) + dot(send_l[:, rows:], right1[...])
    keep[...] = keep_v.astype(BF)
    send[...] = send_v.astype(BF)
    piece = jnp.sum(keep_v * keep_v, 0, keepdims=True) + jnp.sum(send_v * send_v, 0, keepdims=True)
    step = pl.program_id(0)

    @pl.when(step == 0)
    def _():
        sums[...] = piece

    @pl.when(step > 0)
    def _():
        sums[...] += piece

    @pl.when(step == pl.num_programs(0) - 1)
    def _():
        rest = q0[...] + q1[...] + q2[...] + q3[...]
        total = jnp.sum(sums[...], 1, keepdims=True) + jnp.sum(rest, 1, keepdims=True)
        square[...] = jnp.broadcast_to(total, square.shape)


def weight_grad(at, keep_l, send_l, rights, squares):
    rows, ff = rights[0].shape
    width = 512
    return call(
        weight_kernel,
        ff // width,
        [whole((D // 2, 2 * rows))] * 2 + [columns(rows, width)] * 2 + [whole((1, ff))] * 4,
        [columns(D // 2, width)] * 2 + [whole((1, 128))],
        [shaped((D // 2, ff))] * 2 + [shaped((1, 128), F32)],
        [pltpu.VMEM((1, width), F32)],
        cost(4 * rows * D * ff, 11 * 10**6),
        "weight_grad",
    )(at, keep_l, send_l, *rights, *squares)


def scaled(kept, got, u0, u1):
    return kept[...].astype(F32) * u0[0:1, 0:1] + got[...].astype(F32) * u1[0:1, 0:1]


def spread_kernel(at, u0, u1, k1, k2, k3, k4, g1, g2, g3, g4, far1, far2, behind1, ahead2):
    far1[0] = scaled(k1, g1, u0, u1).astype(BF)
    far2[0] = scaled(k2, g2, u0, u1).astype(BF)
    behind1[0] = scaled(k3, g3, u0, u1).astype(BF)
    ahead2[0] = scaled(k4, g4, u0, u1).astype(BF)


def own_kernel(at, u0, u1, k1, k2, g1, g2, own):
    own[0, 0] = scaled(k1, g1, u0, u1)
    own[0, 1] = scaled(k2, g2, u0, u1)


def relay_kernel(at, u0, u1, k1, k2, g1, g2, up, down, ahead1, behind2):
    ahead1[0] = (scaled(k1, g1, u0, u1) + up[0].astype(F32)).astype(BF)
    behind2[0] = (scaled(k2, g2, u0, u1) + down[0].astype(F32)).astype(BF)


def close_kernel(at, own, up1, down1, up2, down2, own_o, ahead, far, behind):
    first = own[0, 0] + up1[0].astype(F32) + down1[0].astype(F32)
    second = own[0, 1] + up2[0].astype(F32) + down2[0].astype(F32)
    step = pl.program_id(0)
    for k, out in enumerate((far, ahead, behind, own_o)):

        @pl.when(step == k)
        def _():
            out[0] = first.astype(out.dtype)
            out[1] = second.astype(out.dtype)


def ring_stage(at, u0, u1, first, second, move):
    ff = first[0].shape[1]
    block = lambda k: pl.BlockSpec((48, ff), lambda s, a: (a[12 + k] + s * a[5], 0))
    one = pl.BlockSpec((1, 48, ff), lambda s, *_: (s, 0, 0))
    both = pl.BlockSpec((1, 2, 48, ff), lambda s, *_: (s, 0, 0, 0))
    single = shaped((RING, 48, ff))
    unit = [whole((1, 128))] * 2
    size = RING * 48 * ff
    order = [block(2), block(2), block(3), block(1)]
    far1, far2, behind1, ahead2 = call(
        spread_kernel,
        RING,
        unit + order * 2,
        [one] * 4,
        [single] * 4,
        [],
        cost(12 * size, 24 * size),
        "spread",
    )(
        at, u0, u1, first[0], second[0], first[0], second[0],
        first[1], second[1], first[1], second[1],
    )
    far1, far2 = move(far1, 1), move(far2, -1)
    up2, down1 = move(ahead2, 1), move(behind1, -1)
    own = call(
        own_kernel,
        RING,
        unit + [block(0)] * 4,
        both,
        shaped((RING, 2, 48, ff), F32),
        [],
        cost(6 * size, 16 * size),
        "own",
    )(at, u0, u1, first[0], second[0], first[1], second[1])
    own, far1, far2 = lax.optimization_barrier((own, far1, far2))
    ahead1, behind2 = call(
        relay_kernel,
        RING,
        unit + [block(1), block(3)] * 2 + [one, one],
        [one, one],
        [single] * 2,
        [],
        cost(8 * size, 16 * size),
        "relay",
    )(at, u0, u1, first[0], second[0], first[1], second[1], far1, far2)
    up1, down2 = move(ahead1, 1), move(behind2, -1)
    place = lambda s, a: a[16 + s]
    return call(
        close_kernel,
        RING,
        [pl.BlockSpec((1, 2, 48, ff), lambda s, a: (place(s, a), 0, 0, 0))]
        + [pl.BlockSpec((1, 48, ff), lambda s, a: (place(s, a), 0, 0))] * 4,
        [pl.BlockSpec((2, 48, ff), lambda s, *_: (0, 0, 0))] * 4,
        [shaped((2, 48, ff), k) for k in (F32, BF, BF, BF)],
        [],
        cost(4 * size, 20 * size),
        "close",
    )(at, own, up1, down1, up2, down2)


def local(
    latents,
    targets,
    tok_count,
    caption_states,
    cap_len,
    owner,
    ctx_w,
    mod_w,
    in_w,
    out_w,
    noise_in,
    noise_out,
):
    rows = latents.shape[0]
    token_span = rows // DRAWS
    me_x = lax.axis_index("mp")
    me_dp = lax.axis_index("dp")
    me_y, me_z, me_c = me_dp // 8, (me_dp // 2) % 4, me_dp % 2
    way = 1 - 2 * me_c

    ahead = [(me_x + k * way) % RING for k in range(RING)]
    swapped = [me_x, me_x ^ 1, 3 - me_x, (3 - me_x) ^ 1]
    me_one = jnp.where(me_c == 0, me_y, me_z)
    me_two = jnp.where(me_c == 0, me_z, me_y)
    stride = jnp.where(me_c == 0, 4, 1)
    at = jnp.stack(
        [b * PART for b in swapped]
        + [me_c * 48, jnp.where(me_c == 0, 1, 4), me_c * 0, me_c * 0]
        + ahead
        + [((me_one + k) % RING) * stride for k in range(RING)]
        + [(me_two + k) % RING for k in (2, 1, 3, 0)]
    ).astype(jnp.int32)
    outs = [lax.dynamic_slice_in_dim(out_w, b * PART, PART, 0) for b in ahead]

    positions = jnp.arange(caption_states.shape[1])
    keep_mask = (positions[None, :] < cap_len[:, None]).astype(BF)
    summed = jnp.einsum("ec,ecf->ef", keep_mask, caption_states, preferred_element_type=F32)
    pooled = (summed / cap_len[:, None].astype(F32)).astype(BF).astype(F32)
    everywhere = jnp.broadcast_to(pooled.reshape(1, 8, -1), (32, 8, pooled.shape[1] // 8))
    received = lax.all_to_all(everywhere, "dp", 0, 0, tiled=True)

    behind, next_ahead = by_x(latents, 1), by_x(latents, -1)
    half = rows // 2
    received, behind, next_ahead, at, outs = lax.optimization_barrier(
        (received, behind, next_ahead, at, outs)
    )
    far = by_x(behind, 1)
    wanted = (owner == me_dp)[:, None, None]
    mine = jnp.sum(jnp.where(wanted, received, 0.0), 0).reshape(1, -1).astype(BF)

    context = dot(mine, ctx_w)
    context = context + swap_x(context, 0)
    swapped_context, far = lax.optimization_barrier((swap_x(context, 1), far))
    context = context + swapped_context
    conditioning = context * lax.rsqrt(jnp.mean(context * context, 1, keepdims=True) + 1e-06)
    chosen = jax.nn.silu(conditioning).astype(BF)
    modulation = jnp.einsum("ed,dkf->ekf", chosen, mod_w, preferred_element_type=F32)[0]
    gate = modulation[2:3]
    own_mods = modulation
    pair_mods = swap_x(own_mods, 0)
    far_mods = swap_x(jnp.concatenate([own_mods, pair_mods], 0), 1)
    mods = (own_mods, pair_mods, far_mods)

    count = tok_count[0]
    factor = 2.0 / (D * DRAWS * count.astype(F32))

    def slope_of(pre):
        square = pre * pre
        bent = jnp.tanh(pre * (C1 + (C1 * C2) * square))
        half = 0.5 * (1.0 + bent)
        return half + (0.5 * pre) * (1.0 - bent * bent) * (C1 + (3.0 * C1 * C2) * square)

    def project(hidden, j):
        return lax.dot_general(
            hidden, outs[j], (((1,), (1,)), ((), ())), preferred_element_type=F32
        )

    def leave(k, own, up, down):
        at_rows = slice(k * half, (k + 1) * half)
        output = latents[at_rows].astype(F32) + gate * (
            own + up.astype(F32) + down.astype(F32)
        )
        live = (jnp.arange(k * half, (k + 1) * half) % token_span < count).astype(F32)[:, None]
        delta = (output - targets[at_rows].astype(F32)) * live * factor
        return (gate * delta).astype(BF)

    latent_blocks = (latents, next_ahead, far, behind)
    modded0, hidden0, pre0 = forward(0, at, latent_blocks, mods, in_w)
    far0, down0 = project(hidden0, 2).astype(BF), project(hidden0, 3).astype(BF)
    far0 = by_x(far0, 1)
    at_next, down0 = lax.optimization_barrier((at, down0))
    down0 = by_x(down0, -1)
    up0 = lax.optimization_barrier(project(hidden0, 1))
    modded1, hidden1, pre1 = forward(1, at_next, latent_blocks, mods, in_w)
    hidden1, far0, down0 = lax.optimization_barrier((hidden1, far0, down0))
    up0 = (up0 + far0.astype(F32)).astype(BF)
    up0, hidden1 = lax.optimization_barrier((up0, hidden1))
    up0 = by_x(up0, 1)
    far1, up1 = project(hidden1, 2).astype(BF), project(hidden1, 1).astype(BF)
    far1, up1, hidden0_late, at_late, pre0, pre1 = lax.optimization_barrier(
        (far1, up1, hidden0, at, pre0, pre1)
    )
    own0 = lax.optimization_barrier(project(hidden0_late, 0))
    far1, up1 = by_x(far1, -1), by_x(up1, 1)
    back0 = leave(0, own0, up0, down0)
    hidden1_late, back0 = lax.optimization_barrier((hidden1, back0))
    down1, own1 = lax.optimization_barrier(
        (project(hidden1_late, 3), project(hidden1_late, 0))
    )
    behind0, ahead0 = by_x(back0, 1), by_x(back0, -1)
    down1 = by_x((down1 + far1.astype(F32)).astype(BF), -1)
    slope0, slope1 = slope_of(pre0).astype(BF), slope_of(pre1).astype(BF)
    mod_keep, mod_send = turn(at_late, modded0, modded1)
    down1, slope0, slope1, mod_keep, mod_send, behind0, ahead0 = lax.optimization_barrier(
        (down1, slope0, slope1, mod_keep, mod_send, behind0, ahead0)
    )
    back1 = leave(1, own1, up1, down1)
    far0 = by_x(behind0, 1)
    ahead1 = by_x(back1, -1)
    back1_late, far0 = lax.optimization_barrier((back1, far0))
    behind1 = by_x(back1_late, 1)
    rights = (hidden0, hidden1)
    *second, square_a = rows_grad(at, 0, ((back0,), (back1,)), rights, (), ())
    partial = rows_partial(at, (ahead0, behind0), hidden0)
    ahead1, partial, square_a = lax.optimization_barrier((ahead1, partial, square_a))
    far1 = by_x(ahead1, -1)
    grad0 = backward(at, (back0, ahead0, far0, behind0), out_w, slope0)
    *second, square_b = rows_grad(at, 1, ((ahead1,),), (hidden1,), (partial,), tuple(second))
    *second, square_d = rows_grad(at, 3, ((behind1,),), (hidden1,), (partial,), tuple(second))
    grad1 = backward(at, (back1, ahead1, far1, behind1), out_w, slope1)
    *second, square_c = rows_grad(at, 2, ((far0,), (far1,)), rights, (), tuple(second))
    keep2, send2 = second
    got2 = by_core(send2)
    keep1, send1, square = weight_grad(
        at, mod_keep, mod_send, (grad0, grad1), (square_a, square_b, square_c, square_d)
    )
    got1 = by_core(send1)
    square = square + swap_x(square, 0)
    square = square + swap_x(square, 1)
    root = math.sqrt(2.0 * D * FF)
    unit = root / (jnp.sqrt(square) + 0.01)

    own, ahead, far, behind = ring_stage(
        at, unit, by_core(unit), (keep1, got1), (keep2, got2), lambda v, w: by_turns(v, w, True)
    )
    value = own + (
        by_turns(far, 2, False).astype(F32)
        + by_turns(ahead, 1, False).astype(F32)
        + by_turns(behind, -1, False).astype(F32)
    )
    return (value[0] + noise_in) / 32.0, (value[1] + noise_out) / 32.0


def solution(mesh):
    placed = (
        P("dp", "mp"),
        P("dp", "mp"),
        P("dp"),
        P("dp", None, "mp"),
        P("dp"),
        P(),
        P("mp", None),
        P(None, None, "mp"),
        P(None, "mp"),
        P(None, "mp"),
        P("dp", "mp"),
        P("dp", "mp"),
    )
    return jax.shard_map(
        local, mesh=mesh, in_specs=placed, out_specs=(P("dp", "mp"), P("dp", "mp")), check_vma=False
    )
```

```python
import math

import jax
import jax.numpy as jnp
from jax import lax
from jax.experimental import pallas as pl
from jax.experimental.pallas import tpu as pltpu
from jax.sharding import PartitionSpec as P

D = 1536
FF = 6144
DRAWS = 4
BF = jnp.bfloat16
F32 = jnp.float32
RING = 4
PART = D // RING
WIDE = 512
VMEM_LIMIT = 32 * 1024 * 1024
C1 = math.sqrt(2.0 / math.pi)
C2 = 0.044715


def dot(left, right):
    return jnp.dot(left, right, preferred_element_type=F32)


def sign(core, way):
    return way if core == 0 else -way


def by_x(value, way):
    pairs = []
    for dp in range(32):
        for x in range(RING):
            pairs.append((dp * RING + x, dp * RING + (x + sign(dp % 2, way)) % RING))
    return lax.ppermute(value, ("dp", "mp"), pairs)


def by_dp(value, target):
    pairs = []
    for y in range(RING):
        for z in range(RING):
            for c in range(2):
                ty, tz, tc = target(y, z, c)
                pairs.append(((y * RING + z) * 2 + c, ((ty % RING) * RING + tz % RING) * 2 + tc))
    return lax.ppermute(value, "dp", pairs)


def by_turns(value, way, first):
    return by_dp(
        value,
        lambda y, z, c: (y + way, z, c) if (c == 0) == first else (y, z + way, c),
    )


def by_core(value):
    return by_dp(value, lambda y, z, c: (y, z, 1 - c))


def swap_x(value, kind):
    other = [x ^ 1 for x in range(RING)] if kind == 0 else [3 - x for x in range(RING)]
    return lax.ppermute(value, "mp", list(enumerate(other)))


def params():
    return pltpu.CompilerParams(vmem_limit_bytes=VMEM_LIMIT)


def shaped(shape, dtype=BF):
    return jax.ShapeDtypeStruct(shape, dtype)


def cost(flops, size, special=0):
    return pl.CostEstimate(flops=flops, bytes_accessed=size, transcendentals=special)


def in_hbm(value):
    return pltpu.with_memory_space_constraint(value, pltpu.HBM)


def whole(shape):
    return pl.BlockSpec(shape, lambda s, *_: (0, 0))


def columns(rows, width):
    return pl.BlockSpec((rows, width), lambda s, *_: (0, s))


def call(kernel, grid, in_specs, out_specs, out_shape, scratch, estimate, name, aliases={}):
    return pl.pallas_call(
        kernel,
        grid_spec=pltpu.PrefetchScalarGridSpec(
            num_scalar_prefetch=1,
            grid=(grid,),
            in_specs=in_specs,
            out_specs=out_specs,
            scratch_shapes=scratch,
        ),
        out_shape=out_shape,
        input_output_aliases=aliases,
        compiler_params=params(),
        cost_estimate=estimate,
        name=name,
    )


def forward_kernel(at, x0, x1, x2, x3, m0, m1, m2, in_w, modded_o, hidden, pre, mods, modded):
    step = pl.program_id(0)

    @pl.when(step == 0)
    def _():
        for place, ref, row in ((0, m0, 0), (1, m1, 0), (2, m2, 0), (3, m2, 3)):
            mods[:, pl.ds(pl.multiple_of(at[place], 128), PART)] = ref[row : row + 2]
        total = 0.0
        squares = 0.0
        for ref in (x0, x1, x2, x3):
            value = ref[...].astype(F32)
            total = total + jnp.sum(value, 1, keepdims=True)
            squares = squares + jnp.sum(value * value, 1, keepdims=True)
        center = total / D
        scale = lax.rsqrt(squares / D - center * center + 1e-06)
        for k, ref in enumerate((x0, x1, x2, x3)):
            cols = pl.ds(pl.multiple_of(at[8 + k] * PART, 128), PART)
            normed = (ref[...].astype(F32) - center) * scale
            modded[:, cols] = (normed * (1.0 + mods[1:2, cols]) + mods[0:1, cols]).astype(BF)

    modded_o[...] = modded[:, pl.ds(pl.multiple_of(step * WIDE, 128), WIDE)]
    value = dot(modded[...], in_w[...])
    pre[...] = value
    bent = jnp.tanh(value * (C1 + (C1 * C2) * (value * value)))
    hidden[...] = ((0.5 * value) * (1.0 + bent)).astype(BF)


def forward(chunk, at, blocks, mods, in_w):
    rows, ff = blocks[0].shape[0] // 2, in_w.shape[1]
    piece = pl.BlockSpec((rows, PART), lambda s, *_: (chunk, 0))
    return call(
        forward_kernel,
        ff // WIDE,
        [piece] * 4
        + [whole((3, PART)), whole((3, PART)), whole((6, PART)), columns(D, WIDE)],
        [columns(rows, WIDE)] * 3,
        [shaped((rows, D)), shaped((rows, ff)), shaped((rows, ff), F32)],
        [pltpu.VMEM((2, D), F32), pltpu.VMEM((rows, D), BF)],
        cost(2 * rows * D * ff, 12 * 10**6, rows * ff),
        "forward",
    )(at, *[in_hbm(b) for b in blocks], *mods, in_hbm(in_w))


def split_rows(at, turned, keep, send):
    mine = at[4]
    for z in range(RING):
        keep[z * 48 : (z + 1) * 48] = turned[pl.ds(pl.multiple_of(z * 96 + mine, 16), 48)]
        send[z * 48 : (z + 1) * 48] = turned[pl.ds(pl.multiple_of(z * 96 + 48 - mine, 16), 48)]


def turn_kernel(at, top, low, keep, send, turned):
    turned[:, : top.shape[0]] = top[...].T
    turned[:, top.shape[0] :] = low[...].T
    split_rows(at, turned, keep, send)


def turn(at, top, low):
    rows = top.shape[0]
    out = pl.BlockSpec((PART // 2, 2 * rows), lambda s, *_: (s, 0))
    return call(
        turn_kernel,
        RING,
        [columns(rows, PART)] * 2,
        [out, out],
        [shaped((D // 2, 2 * rows))] * 2,
        [pltpu.VMEM((PART, 2 * rows), BF)],
        cost(2 * rows * D, 8 * rows * D),
        "turn",
    )(at, top, low)


def backward_kernel(at, b0, b1, b2, b3, out_w, slope, grad, back):
    @pl.when(pl.program_id(0) == 0)
    def _():
        for k, ref in enumerate((b0, b1, b2, b3)):
            back[:, pl.ds(pl.multiple_of(at[8 + k] * PART, 128), PART)] = ref[...]

    grad[...] = (dot(back[...], out_w[...]) * slope[...].astype(F32)).astype(BF)


def backward(at, blocks, out_w, slope):
    rows, ff = slope.shape
    return call(
        backward_kernel,
        ff // WIDE,
        [whole((rows, PART))] * 4 + [columns(D, WIDE), columns(rows, WIDE)],
        columns(rows, WIDE),
        shaped((rows, ff)),
        [pltpu.VMEM((rows, D), BF)],
        cost(2 * rows * D * ff, 14 * 10**6),
        "backward",
    )(at, *blocks, out_w, slope)


def turn_blocks(groups, turned):
    for k in range(len(groups[0])):

        @pl.when(pl.program_id(0) == k)
        def _():
            start = 0
            for group in groups:
                rows = group[k].shape[0]
                turned[:, start : start + rows] = group[k][...].T
                start += rows


def cut_refs(refs, count, groups):
    return [refs[g * count : (g + 1) * count] for g in range(groups)], refs[groups * count :]


def product(turned, rights, cols):
    start = 0
    value = 0.0
    for right in rights:
        rows = right.shape[0]
        value = value + dot(turned[:, start : start + rows], right[:, cols])
        start += rows
    return value


def partial_kernel(count, at, *refs):
    groups, (right, out, turned) = cut_refs(refs, count, 1)
    turn_blocks(groups, turned)
    for n in range(right.shape[1] // 512):
        cols = slice(n * 512, (n + 1) * 512)
        out[:, cols] = product(turned, [right], cols)


def rows_partial(at, blocks, right):
    rows, ff = right.shape
    count = len(blocks)
    return call(
        lambda *refs: partial_kernel(count, *refs),
        count,
        [whole((rows, PART))] * count + [whole((rows, ff))],
        pl.BlockSpec((PART, ff), lambda s, *_: (s, 0)),
        shaped((count * PART, ff), F32),
        [pltpu.VMEM((PART, rows), BF)],
        cost(2 * rows * PART * ff * count, 4 * 10**6 * count),
        "rows_partial",
    )(at, *blocks, right)


def rows_kernel(count, parts, partials, at, *refs):
    groups, rest = cut_refs(refs, count, parts)
    rights, rest = rest[:parts], rest[parts:]
    keep, send, square, turned = refs[-4:]
    turn_blocks(groups, turned)
    mine = at[4]
    for n in range(rights[0].shape[1] // 512):
        cols = slice(n * 512, (n + 1) * 512)
        value = product(turned, rights, cols)
        if partials:
            value = value + rest[0][:, cols]
        piece = jnp.sum(value * value, 0, keepdims=True)

        @pl.when(pl.program_id(0) == 0)
        def _():
            square[:, cols] = piece

        @pl.when(pl.program_id(0) > 0)
        def _():
            square[:, cols] += piece

        for z in range(RING):
            low = value[z * 96 : z * 96 + 48].astype(BF)
            high = value[z * 96 + 48 : (z + 1) * 96].astype(BF)
            at_rows = slice(z * 48, (z + 1) * 48)
            keep[at_rows, cols] = jnp.where(mine == 0, low, high)
            send[at_rows, cols] = jnp.where(mine == 0, high, low)


def rows_grad(at, place, groups, rights, partials, before):
    ff = rights[0].shape[1]
    rows = sum(right.shape[0] for right in rights)
    count, parts = 1, len(groups)
    out = pl.BlockSpec((PART // 2, ff), lambda s, a: (a[8 + place], 0))
    offset = place // 2
    blocks = [block for group in groups for block in group]
    operands = [*blocks, *rights, *partials, *before]
    return call(
        lambda *refs: rows_kernel(count, parts, len(partials), *refs),
        count,
        [whole(value.shape) for value in (*blocks, *rights)]
        + [pl.BlockSpec((PART, ff), lambda s, *_: (offset, 0))] * len(partials)
        + [pl.BlockSpec(memory_space=pl.ANY)] * len(before),
        [out, out, whole((1, ff))],
        [shaped((D // 2, ff))] * 2 + [shaped((1, ff), F32)],
        [pltpu.VMEM((PART, rows), BF)],
        cost(2 * rows * PART * ff * count, 5 * 10**6 * count),
        "rows_grad",
        {len(operands) - len(before) + 1 + n: n for n in range(len(before))},
    )(at, *operands)


def weight_kernel(at, keep_l, send_l, right0, right1, q0, q1, q2, q3, keep, send, square, sums):
    rows = right0.shape[0]
    keep_v = dot(keep_l[:, :rows], right0[...]) + dot(keep_l[:, rows:], right1[...])
    send_v = dot(send_l[:, :rows], right0[...]) + dot(send_l[:, rows:], right1[...])
    keep[...] = keep_v.astype(BF)
    send[...] = send_v.astype(BF)
    piece = jnp.sum(keep_v * keep_v, 0, keepdims=True) + jnp.sum(send_v * send_v, 0, keepdims=True)
    step = pl.program_id(0)

    @pl.when(step == 0)
    def _():
        sums[...] = piece

    @pl.when(step > 0)
    def _():
        sums[...] += piece

    @pl.when(step == pl.num_programs(0) - 1)
    def _():
        rest = q0[...] + q1[...] + q2[...] + q3[...]
        total = jnp.sum(sums[...], 1, keepdims=True) + jnp.sum(rest, 1, keepdims=True)
        square[...] = jnp.broadcast_to(total, square.shape)


def weight_grad(at, keep_l, send_l, rights, squares):
    rows, ff = rights[0].shape
    width = 512
    return call(
        weight_kernel,
        ff // width,
        [whole((D // 2, 2 * rows))] * 2 + [columns(rows, width)] * 2 + [whole((1, ff))] * 4,
        [columns(D // 2, width)] * 2 + [whole((1, 128))],
        [shaped((D // 2, ff))] * 2 + [shaped((1, 128), F32)],
        [pltpu.VMEM((1, width), F32)],
        cost(4 * rows * D * ff, 11 * 10**6),
        "weight_grad",
    )(at, keep_l, send_l, *rights, *squares)


def scaled(kept, got, u0, u1):
    return kept[...].astype(F32) * u0[0:1, 0:1] + got[...].astype(F32) * u1[0:1, 0:1]


def spread_kernel(at, u0, u1, k1, k2, k3, k4, g1, g2, g3, g4, far1, far2, behind1, ahead2):
    far1[0] = scaled(k1, g1, u0, u1).astype(BF)
    far2[0] = scaled(k2, g2, u0, u1).astype(BF)
    behind1[0] = scaled(k3, g3, u0, u1).astype(BF)
    ahead2[0] = scaled(k4, g4, u0, u1).astype(BF)


def own_kernel(at, u0, u1, k1, k2, g1, g2, own):
    own[0, 0] = scaled(k1, g1, u0, u1)
    own[0, 1] = scaled(k2, g2, u0, u1)


def relay_kernel(at, u0, u1, k1, k2, g1, g2, up, down, ahead1, behind2):
    ahead1[0] = (scaled(k1, g1, u0, u1) + up[0].astype(F32)).astype(BF)
    behind2[0] = (scaled(k2, g2, u0, u1) + down[0].astype(F32)).astype(BF)


def close_kernel(at, own, up1, down1, up2, down2, own_o, ahead, far, behind):
    first = own[0, 0] + up1[0].astype(F32) + down1[0].astype(F32)
    second = own[0, 1] + up2[0].astype(F32) + down2[0].astype(F32)
    step = pl.program_id(0)
    for k, out in enumerate((far, ahead, behind, own_o)):

        @pl.when(step == k)
        def _():
            out[0] = first.astype(out.dtype)
            out[1] = second.astype(out.dtype)


def ring_stage(at, u0, u1, first, second, move):
    ff = first[0].shape[1]
    block = lambda k: pl.BlockSpec((48, ff), lambda s, a: (a[12 + k] + s * a[5], 0))
    one = pl.BlockSpec((1, 48, ff), lambda s, *_: (s, 0, 0))
    both = pl.BlockSpec((1, 2, 48, ff), lambda s, *_: (s, 0, 0, 0))
    single = shaped((RING, 48, ff))
    unit = [whole((1, 128))] * 2
    size = RING * 48 * ff
    order = [block(2), block(2), block(3), block(1)]
    far1, far2, behind1, ahead2 = call(
        spread_kernel,
        RING,
        unit + order * 2,
        [one] * 4,
        [single] * 4,
        [],
        cost(12 * size, 24 * size),
        "spread",
    )(
        at, u0, u1, first[0], second[0], first[0], second[0],
        first[1], second[1], first[1], second[1],
    )
    far1, far2 = move(far1, 1), move(far2, -1)
    up2, down1 = move(ahead2, 1), move(behind1, -1)
    own = call(
        own_kernel,
        RING,
        unit + [block(0)] * 4,
        both,
        shaped((RING, 2, 48, ff), F32),
        [],
        cost(6 * size, 16 * size),
        "own",
    )(at, u0, u1, first[0], second[0], first[1], second[1])
    own, far1, far2 = lax.optimization_barrier((own, far1, far2))
    ahead1, behind2 = call(
        relay_kernel,
        RING,
        unit + [block(1), block(3)] * 2 + [one, one],
        [one, one],
        [single] * 2,
        [],
        cost(8 * size, 16 * size),
        "relay",
    )(at, u0, u1, first[0], second[0], first[1], second[1], far1, far2)
    up1, down2 = move(ahead1, 1), move(behind2, -1)
    place = lambda s, a: a[16 + s]
    return call(
        close_kernel,
        RING,
        [pl.BlockSpec((1, 2, 48, ff), lambda s, a: (place(s, a), 0, 0, 0))]
        + [pl.BlockSpec((1, 48, ff), lambda s, a: (place(s, a), 0, 0))] * 4,
        [pl.BlockSpec((2, 48, ff), lambda s, *_: (0, 0, 0))] * 4,
        [shaped((2, 48, ff), k) for k in (F32, BF, BF, BF)],
        [],
        cost(4 * size, 20 * size),
        "close",
    )(at, own, up1, down1, up2, down2)


def local(
    latents,
    targets,
    tok_count,
    caption_states,
    cap_len,
    owner,
    ctx_w,
    mod_w,
    in_w,
    out_w,
    noise_in,
    noise_out,
):
    rows = latents.shape[0]
    token_span = rows // DRAWS
    me_x = lax.axis_index("mp")
    me_dp = lax.axis_index("dp")
    me_y, me_z, me_c = me_dp // 8, (me_dp // 2) % 4, me_dp % 2
    way = 1 - 2 * me_c

    ahead = [(me_x + k * way) % RING for k in range(RING)]
    swapped = [me_x, me_x ^ 1, 3 - me_x, (3 - me_x) ^ 1]
    me_one = jnp.where(me_c == 0, me_y, me_z)
    me_two = jnp.where(me_c == 0, me_z, me_y)
    stride = jnp.where(me_c == 0, 4, 1)
    at = jnp.stack(
        [b * PART for b in swapped]
        + [me_c * 48, jnp.where(me_c == 0, 1, 4), me_c * 0, me_c * 0]
        + ahead
        + [((me_one + k) % RING) * stride for k in range(RING)]
        + [(me_two + k) % RING for k in (2, 1, 3, 0)]
    ).astype(jnp.int32)
    outs = [lax.dynamic_slice_in_dim(out_w, b * PART, PART, 0) for b in ahead]

    positions = jnp.arange(caption_states.shape[1])
    keep_mask = (positions[None, :] < cap_len[:, None]).astype(BF)
    summed = jnp.einsum("ec,ecf->ef", keep_mask, caption_states, preferred_element_type=F32)
    pooled = (summed / cap_len[:, None].astype(F32)).astype(BF).astype(F32)
    everywhere = jnp.broadcast_to(pooled.reshape(1, 8, -1), (32, 8, pooled.shape[1] // 8))
    received = lax.all_to_all(everywhere, "dp", 0, 0, tiled=True)

    behind, next_ahead = by_x(latents, 1), by_x(latents, -1)
    half = rows // 2
    received, behind, next_ahead, at, outs = lax.optimization_barrier(
        (received, behind, next_ahead, at, outs)
    )
    far = by_x(behind, 1)
    wanted = (owner == me_dp)[:, None, None]
    mine = jnp.sum(jnp.where(wanted, received, 0.0), 0).reshape(1, -1).astype(BF)

    context = dot(mine, ctx_w)
    context = context + swap_x(context, 0)
    swapped_context, far = lax.optimization_barrier((swap_x(context, 1), far))
    context = context + swapped_context
    conditioning = context * lax.rsqrt(jnp.mean(context * context, 1, keepdims=True) + 1e-06)
    chosen = jax.nn.silu(conditioning).astype(BF)
    modulation = jnp.einsum("ed,dkf->ekf", chosen, mod_w, preferred_element_type=F32)[0]
    gate = modulation[2:3]
    own_mods = modulation
    pair_mods = swap_x(own_mods, 0)
    far_mods = swap_x(jnp.concatenate([own_mods, pair_mods], 0), 1)
    mods = (own_mods, pair_mods, far_mods)

    count = tok_count[0]
    factor = 2.0 / (D * DRAWS * count.astype(F32))

    def slope_of(pre):
        square = pre * pre
        bent = jnp.tanh(pre * (C1 + (C1 * C2) * square))
        half = 0.5 * (1.0 + bent)
        return half + (0.5 * pre) * (1.0 - bent * bent) * (C1 + (3.0 * C1 * C2) * square)

    def project(hidden, j):
        return lax.dot_general(
            hidden, outs[j], (((1,), (1,)), ((), ())), preferred_element_type=F32
        )

    def leave(k, own, up, down):
        at_rows = slice(k * half, (k + 1) * half)
        output = latents[at_rows].astype(F32) + gate * (
            own + up.astype(F32) + down.astype(F32)
        )
        live = (jnp.arange(k * half, (k + 1) * half) % token_span < count).astype(F32)[:, None]
        delta = (output - targets[at_rows].astype(F32)) * live * factor
        return (gate * delta).astype(BF)

    latent_blocks = (latents, next_ahead, far, behind)
    modded0, hidden0, pre0 = forward(0, at, latent_blocks, mods, in_w)
    far0, down0 = project(hidden0, 2).astype(BF), project(hidden0, 3).astype(BF)
    far0 = by_x(far0, 1)
    at_next, down0 = lax.optimization_barrier((at, down0))
    down0 = by_x(down0, -1)
    up0 = lax.optimization_barrier(project(hidden0, 1))
    modded1, hidden1, pre1 = forward(1, at_next, latent_blocks, mods, in_w)
    hidden1, far0, down0 = lax.optimization_barrier((hidden1, far0, down0))
    up0 = (up0 + far0.astype(F32)).astype(BF)
    up0, hidden1 = lax.optimization_barrier((up0, hidden1))
    up0 = by_x(up0, 1)
    far1, up1 = project(hidden1, 2).astype(BF), project(hidden1, 1).astype(BF)
    far1, up1, hidden0_late, at_late, pre0, pre1 = lax.optimization_barrier(
        (far1, up1, hidden0, at, pre0, pre1)
    )
    own0 = lax.optimization_barrier(project(hidden0_late, 0))
    far1, up1 = by_x(far1, -1), by_x(up1, 1)
    back0 = leave(0, own0, up0, down0)
    hidden1_late, back0 = lax.optimization_barrier((hidden1, back0))
    down1, own1 = lax.optimization_barrier(
        (project(hidden1_late, 3), project(hidden1_late, 0))
    )
    behind0, ahead0 = by_x(back0, 1), by_x(back0, -1)
    down1 = by_x((down1 + far1.astype(F32)).astype(BF), -1)
    slope0, slope1 = slope_of(pre0).astype(BF), slope_of(pre1).astype(BF)
    mod_keep, mod_send = turn(at_late, modded0, modded1)
    down1, slope0, slope1, mod_keep, mod_send, behind0, ahead0 = lax.optimization_barrier(
        (down1, slope0, slope1, mod_keep, mod_send, behind0, ahead0)
    )
    back1 = leave(1, own1, up1, down1)
    far0 = by_x(behind0, 1)
    ahead1 = by_x(back1, -1)
    back1_late, far0 = lax.optimization_barrier((back1, far0))
    behind1 = by_x(back1_late, 1)
    rights = (hidden0, hidden1)
    *second, square_a = rows_grad(at, 0, ((back0,), (back1,)), rights, (), ())
    partial = rows_partial(at, (ahead0, behind0), hidden0)
    ahead1, partial, square_a = lax.optimization_barrier((ahead1, partial, square_a))
    far1 = by_x(ahead1, -1)
    grad0 = backward(at, (back0, ahead0, far0, behind0), out_w, slope0)
    *second, square_b = rows_grad(at, 1, ((ahead1,),), (hidden1,), (partial,), tuple(second))
    *second, square_d = rows_grad(at, 3, ((behind1,),), (hidden1,), (partial,), tuple(second))
    grad1 = backward(at, (back1, ahead1, far1, behind1), out_w, slope1)
    *second, square_c = rows_grad(at, 2, ((far0,), (far1,)), rights, (), tuple(second))
    keep2, send2 = second
    got2 = by_core(send2)
    keep1, send1, square = weight_grad(
        at, mod_keep, mod_send, (grad0, grad1), (square_a, square_b, square_c, square_d)
    )
    got1 = by_core(send1)
    square = square + swap_x(square, 0)
    square = square + swap_x(square, 1)
    root = math.sqrt(2.0 * D * FF)
    unit = root / (jnp.sqrt(square) + 0.01)

    own, ahead, far, behind = ring_stage(
        at, unit, by_core(unit), (keep1, got1), (keep2, got2), lambda v, w: by_turns(v, w, True)
    )
    value = own + (
        by_turns(behind, -1, False).astype(F32)
        + by_turns(ahead, 1, False).astype(F32)
        + by_turns(far, 2, False).astype(F32)
    )
    return (value[0] + noise_in) / 32.0, (value[1] + noise_out) / 32.0


def solution(mesh):
    placed = (
        P("dp", "mp"),
        P("dp", "mp"),
        P("dp"),
        P("dp", None, "mp"),
        P("dp"),
        P(),
        P("mp", None),
        P(None, None, "mp"),
        P(None, "mp"),
        P(None, "mp"),
        P("dp", "mp"),
        P("dp", "mp"),
    )
    return jax.shard_map(
        local, mesh=mesh, in_specs=placed, out_specs=(P("dp", "mp"), P("dp", "mp")), check_vma=False
    )
```
